32 devices in a mesh: dp: 16 (over z, y, x), tensor: 2 (over core).
Axes of the slice: x: 2, y: 2, z: 4, core: 2. Of those that a mesh axis runs over, the one named last changes fastest.
Arguments:
- frames: bfloat16 [2, 16, 512, 768], P(None, 'dp', 'tensor'), may hold values from -6 to 6
- cotangent: bfloat16 [2, 16, 512, 768], P(None, 'dp', 'tensor'), may hold values from -6 to 6
- lengths: int32 [2, 16], P(None, 'dp'), may hold values from 102 to 512, as said below
- attn_w: float32 [4, 768, 768], P(None, 'dp', 'tensor')
- attn_m: float32 [4, 768, 768], P(None, 'dp', 'tensor'), may hold values from -6.1035156e-05 to 6.1035156e-05
- attn_v: float32 [4, 768, 768], P(None, 'dp', 'tensor'), may hold values from 7.055068e-13 to 1.12881085e-11
- ffn_w: float32 [2, 768, 3072], P(None, 'dp', 'tensor')
- ffn_m: float32 [2, 768, 3072], P(None, 'dp', 'tensor'), may hold values from -6.1035156e-05 to 6.1035156e-05
- ffn_v: float32 [2, 768, 3072], P(None, 'dp', 'tensor'), may hold values from 7.055068e-13 to 1.12881085e-11
- small_w: float32 [9216], replicated
- small_m: float32 [9216], replicated, may hold values from -0.00018310547 to 0.00018310547
- small_v: float32 [9216], replicated, may hold values from 6.349561e-12 to 1.0159298e-10
Outputs:
- output: bfloat16 [2, 16, 512, 768], P(None, 'dp', 'tensor')
- frames_grad: float32 [2, 16, 512, 768], P(None, 'dp', 'tensor')
- grad_norm: float32 [], replicated
- attn_new: float32 [4, 768, 768], P(None, 'dp', 'tensor')
- attn_m_new: float32 [4, 768, 768], P(None, 'dp', 'tensor')
- attn_v_new: float32 [4, 768, 768], P(None, 'dp', 'tensor')
- ffn_new: float32 [2, 768, 3072], P(None, 'dp', 'tensor')
- ffn_m_new: float32 [2, 768, 3072], P(None, 'dp', 'tensor')
- ffn_v_new: float32 [2, 768, 3072], P(None, 'dp', 'tensor')
- small_new: float32 [9216], replicated
- small_m_new: float32 [9216], replicated
- small_v_new: float32 [9216], replicated
The draws below stay inside these ranges and needn't reach their ends.
Inputs may be any that keep to these rules, and one draw needn't show every extreme that they name: lengths[m, b] is the number of valid frames of utterance b of micro-batch m; some utterance has 512 valid frames.
All inputs are finite; a program needn't handle non-finite values.
Results may differ from the reference program's by a relative error of at most 0.018.
Values may be sent and summed in bfloat16 or wider, within the bound.
No kernel may reach another device: no remote copies, remote signals or barrier semaphores. Data moves between devices by JAX's collectives and lax.ppermute only.
A program may use at most 128 MiB of HBM per device.

```python
import math
import jax
import jax.numpy as jnp
from jax import lax

H = 12
HD = 64
D = 768
FF = 3072
SEQ = 512
UTT = 1
MB = 2
STEP = 10
BATCH = 16
SMALL = 9216
NPARAM = 7087104


def draw_lengths(key, part):
    key = jax.random.fold_in(key, 11)
    first_key, second_key = jax.random.split(key)
    device_count = BATCH // UTT
    device_row = jnp.arange(BATCH, dtype=jnp.int32) // UTT
    lowest = SEQ // 5 + 3 * SEQ // 5 * device_row // (device_count - 1)
    highest = lowest + SEQ // 5 + 1
    drawn = jax.random.randint(first_key, (MB, BATCH), lowest[None, :], highest[None, :])
    chosen = jax.random.randint(second_key, (), 0, MB)
    forced = (jnp.arange(MB)[:, None] == chosen) & (jnp.arange(BATCH)[None, :] == BATCH - 1)
    return jnp.where(forced, SEQ, drawn).astype(jnp.int32)


def draw_attn_w(key, part):
    key = jax.random.fold_in(key, 12)
    noise = jax.random.normal(key, (4, D, D), jnp.float32)
    factors = jnp.array([1.0, 1.0, 1.0, 0.5 * SEQ ** 0.5], jnp.float32) * D ** (-0.5)
    return noise * factors[:, None, None]


def draw_ffn_w(key, part):
    key = jax.random.fold_in(key, 13)
    noise = jax.random.normal(key, (2, D, FF), jnp.float32)
    factors = jnp.array([D ** (-0.5), 1.6 * FF ** (-0.5)], jnp.float32)
    return noise * factors[:, None, None]


def draw_small_w(key, part):
    key = jax.random.fold_in(key, 14)
    noise_key, gain_key = jax.random.split(key)
    noise = jax.random.normal(noise_key, (SMALL,), jnp.float32)
    jitter = jax.random.uniform(gain_key, (2, D), jnp.float32, 0.8, 1.2)
    rising = 1.0 + 2.0 * jnp.arange(D, dtype=jnp.float32) / (D - 1)
    gain_rows = rising[None, :] * jitter
    scaled = 0.3 * noise
    return jnp.concatenate([scaled[:4 * D], gain_rows[0], scaled[5 * D:6 * D], gain_rows[1], scaled[7 * D:]])


def level_of(stream_key, shape, cuts, least, top_value):
    def one(dim, shards_of):
        steps = jax.random.uniform(jax.random.fold_in(jax.random.fold_in(stream_key, 6), dim), (shards_of,), jnp.float32, least / len(cuts), top_value / len(cuts))
        return jnp.repeat(jnp.exp(steps), shape[dim] // shards_of).reshape((-1,) + (1,) * (len(shape) - dim - 1))

    level = one(*cuts[0])
    for cut in cuts[1:]:
        level = level * one(*cut)
    return level


def normal_values(key, shape, scale, limit, pieces=(), held_as=jnp.bfloat16):
    factor_of = level_of(key, shape, pieces, -0.22, 0.18) if pieces else 1.0
    values = jax.random.normal(key, shape, jnp.float32) * scale * factor_of
    return jnp.minimum(jnp.maximum(values, -limit), limit).astype(held_as)


def setup_inputs(seed: int = 0) -> dict:
    splits = jax.random.split(jax.random.key(seed), 13)
    frames = normal_values(splits[0], (MB, BATCH, SEQ, D), 1.0, 6.0, ((1, 16), (2, 2)))
    cotangent = normal_values(splits[1], (MB, BATCH, SEQ, D), 1.0, 6.0, ((1, 16), (2, 2)))
    lengths = draw_lengths(jax.random.fold_in(splits[12], 71), 0)
    attn_w = draw_attn_w(jax.random.fold_in(splits[12], 71), 0)
    attn_m = normal_values(splits[4], (4, D, D), (0.011 / NPARAM ** 0.5), 6.103515625e-05, ((1, 16), (2, 2)), jnp.float32)
    attn_v = jnp.clip(jnp.exp(math.log(1.1288108468787694e-11) - 2.7725887 * jax.random.uniform(splits[5], (4, D, D), jnp.float32) ** level_of(splits[5], (4, D, D), ((1, 16), (2, 2)), -0.2, 0.2)), 7.055067792992309e-13, 1.1288108468787694e-11)
    ffn_w = draw_ffn_w(jax.random.fold_in(splits[12], 71), 0)
    ffn_m = normal_values(splits[7], (2, D, FF), (0.011 / NPARAM ** 0.5), 6.103515625e-05, ((1, 16), (2, 2)), jnp.float32)
    ffn_v = jnp.clip(jnp.exp(math.log(1.1288108468787694e-11) - 2.7725887 * jax.random.uniform(splits[8], (2, D, FF), jnp.float32) ** level_of(splits[8], (2, D, FF), ((1, 16), (2, 2)), -0.2, 0.2)), 7.055067792992309e-13, 1.1288108468787694e-11)
    small_w = draw_small_w(jax.random.fold_in(splits[12], 71), 0)
    small_m = normal_values(splits[10], (SMALL,), (0.033 / NPARAM ** 0.5), 0.00018310547, (), jnp.float32)
    small_v = jnp.clip(jnp.exp(jax.random.uniform(splits[11], (SMALL,), jnp.float32, math.log(6.349561067903187e-12), math.log(1.0159297708645099e-10))), 6.349561067903187e-12, 1.0159297708645099e-10)
    return {"frames": frames, "cotangent": cotangent, "lengths": lengths, "attn_w": attn_w, "attn_m": attn_m, "attn_v": attn_v, "ffn_w": ffn_w, "ffn_m": ffn_m, "ffn_v": ffn_v, "small_w": small_w, "small_m": small_m, "small_v": small_v}


EPS_NORM = 1e-05
MASK_FILL = -1e+30
BETA_ONE = 0.9
BETA_TWO = 0.999
ADAM_EPS = 1e-08
CLIP_NORM = 0.1
RATE = 0.1
SMALL_RATE = 1.5
DECAY = 0.01

@jax.custom_vjp
def low(v):
    return lax.optimization_barrier(v.astype(jnp.bfloat16)).astype(jnp.float32)

@jax.custom_vjp
def low_back(v):
    return v

def low_keep(v):
    return (low(v), None)

def low_pass(kept, grad):
    return (grad,)

def back_keep(v):
    return (v, None)

def back_low(kept, grad):
    return (low(grad),)
low.defvjp(low_keep, low_pass)
low_back.defvjp(back_keep, back_low)

def product(left, right):
    return jnp.dot(left, right, precision=lax.Precision.HIGHEST, preferred_element_type=jnp.float32)

def layer_norm(values, gain, shift):
    centred = values - lax.optimization_barrier(jnp.mean(values, -1, keepdims=True))
    spread = lax.optimization_barrier(jnp.mean(centred * centred, -1, keepdims=True))
    return centred * lax.rsqrt(spread + EPS_NORM) * gain + shift

def adamw(weight, moment_one, moment_two, grad, rate, decay):
    new_one = BETA_ONE * moment_one + (1.0 - BETA_ONE) * grad
    new_two = BETA_TWO * moment_two + (1.0 - BETA_TWO) * grad * grad
    fixed_one = new_one / (1.0 - BETA_ONE ** STEP)
    fixed_two = new_two / (1.0 - BETA_TWO ** STEP)
    update = fixed_one / (jnp.sqrt(fixed_two) + ADAM_EPS) + decay * weight
    return (weight - rate * update, new_one, new_two)

def layer(frame_rows, attn, ffn, small, valid):
    weights = low(attn)
    wide = low(ffn)
    scale = HD ** (-0.5)
    bias_q = small[0:D]
    bias_v = small[D:2 * D]
    bias_o = small[2 * D:3 * D]
    bias_two = small[3 * D:4 * D]
    gain_one = small[4 * D:5 * D]
    shift_one = small[5 * D:6 * D]
    gain_two = small[6 * D:7 * D]
    shift_two = small[7 * D:8 * D]
    bias_one = small[8 * D:]
    query = low(low_back(product(frame_rows, weights[0]) + bias_q)).reshape(SEQ, H, HD)
    keys = low(low_back(product(frame_rows, weights[1]))).reshape(SEQ, H, HD)
    values = low(low_back(product(frame_rows, weights[2]) + bias_v)).reshape(SEQ, H, HD)
    scores = low_back(jnp.einsum('qhd,khd->hqk', query, keys, precision=lax.Precision.HIGHEST) * scale)
    scores = jnp.where(valid[None, None, :], scores, MASK_FILL)
    powers = jnp.exp(scores - lax.optimization_barrier(jnp.max(scores, -1, keepdims=True)))
    probs = low(powers / lax.optimization_barrier(jnp.sum(powers, -1, keepdims=True)))
    mixed = jnp.einsum('hqk,khd->qhd', probs, values, precision=lax.Precision.HIGHEST).reshape(SEQ, D)
    mixed = low(low_back(mixed))
    attended = low_back(product(mixed, weights[3].T)) + bias_o
    hidden = layer_norm(frame_rows + attended, gain_one, shift_one)
    inner = low_back(product(low(hidden), wide[0])) + bias_one
    acted = low(jax.nn.gelu(inner, approximate=False))
    outer = low_back(product(acted, wide[1].T)) + bias_two
    return layer_norm(hidden + outer, gain_two, shift_two)

def reference(frames, cotangent, lengths, attn_w, attn_m, attn_v, ffn_w, ffn_m, ffn_v, small_w, small_m, small_v):

    def one_sequence(carry, item):
        frame_rows, cot_rows, length = item
        valid = jnp.arange(SEQ) < length

        def forward(rows, attn, ffn, small):
            return layer(rows, attn, ffn, small, valid)
        result, backward = jax.vjp(forward, frame_rows.astype(jnp.float32), attn_w, ffn_w, small_w)
        mask = valid.astype(jnp.float32)[:, None]
        rows_grad, attn_grad, ffn_grad, small_grad = backward(cot_rows.astype(jnp.float32) * mask)
        carry = (carry[0] + attn_grad, carry[1] + ffn_grad, carry[2] + small_grad)
        return (carry, (result.astype(jnp.bfloat16), rows_grad))
    start = (jnp.zeros((4, D, D), jnp.float32), jnp.zeros((2, D, FF), jnp.float32), jnp.zeros((SMALL,), jnp.float32))
    inputs = (frames.reshape(MB * BATCH, SEQ, D), cotangent.reshape(MB * BATCH, SEQ, D), lengths.reshape(MB * BATCH))
    totals, stacked = lax.scan(one_sequence, start, inputs)
    attn_grad, ffn_grad, small_grad = totals
    output = stacked[0].reshape(MB, BATCH, SEQ, D)
    frames_grad = stacked[1].reshape(MB, BATCH, SEQ, D)
    count = jnp.sum(lengths).astype(jnp.float32)
    squares = jnp.sum(attn_grad * attn_grad) + jnp.sum(ffn_grad * ffn_grad) + jnp.sum(small_grad * small_grad)
    grad_norm = jnp.sqrt(squares) / count
    factor = jnp.minimum(1.0, CLIP_NORM / grad_norm) / count
    attn_rates = RATE * jnp.array([1.0, 1.0, 1.0, 0.5 * SEQ ** 0.5], jnp.float32)[:, None, None]
    attn_new, attn_m_new, attn_v_new = adamw(attn_w, attn_m, attn_v, attn_grad * factor, attn_rates, DECAY)
    ffn_new, ffn_m_new, ffn_v_new = adamw(ffn_w, ffn_m, ffn_v, ffn_grad * factor, RATE, DECAY)
    small_new, small_m_new, small_v_new = adamw(small_w, small_m, small_v, small_grad * factor, SMALL_RATE, 0.0)
    return (output, frames_grad, grad_norm, attn_new, attn_m_new, attn_v_new, ffn_new, ffn_m_new, ffn_v_new, small_new, small_m_new, small_v_new)
```

```python
import functools
import math

import jax
import jax.numpy as jnp
from jax import lax
from jax.experimental import pallas as pl
from jax.experimental.pallas import tpu as pltpu
from jax.sharding import PartitionSpec as P

HD = 64
D = 768
FF = 3072
SEQ = 512
HALF = SEQ // 2
STEP = 10
SMALL = 9216
PAIRS = 6
BLOCKS = 16
ROWS = D // BLOCKS

EPS_NORM = 1e-05
MASK_FILL = -1e30
BETA_ONE = 0.9
BETA_TWO = 0.999
ADAM_EPS = 1e-08
CLIP_NORM = 0.1
RATE = 0.1
SMALL_RATE = 1.5
DECAY = 0.01

BF = jnp.bfloat16
F32 = jnp.float32

STEP_A = (2, 1)
STEP_B = (1, 2)
Z_MASKS = (0, 4, 8, 12)
MASKS = tuple(
    (
        tuple(z for z in Z_MASKS) + tuple(z + near for z in Z_MASKS),
        tuple(z + far for z in Z_MASKS) + tuple(z + near + far for z in Z_MASKS),
    )
    for near, far in (STEP_A, STEP_B)
)


def dot(left, right):
    return jnp.dot(left, right, preferred_element_type=F32)


def dot_t(left, right):
    return lax.dot_general(left, right, (((1,), (1,)), ((), ())), preferred_element_type=F32)


ERF_P = 0.35
ERF_Q = (
    0.19402205421243862,
    0.2385478098291166,
    -0.017756407016771347,
    0.7010874955540375,
    -0.6969262406496157,
    0.7808055624011503,
    -0.1997802807385829,
)


def gelu_pair(u):
    t = 1.0 / (1.0 + (ERF_P * math.sqrt(0.5)) * jnp.abs(u))
    bell = jnp.exp(-0.5 * u * u)
    acc = ERF_Q[6] * t + ERF_Q[5]
    for k in (4, 3, 2, 1, 0):
        acc = acc * t + ERF_Q[k]
    tail = 0.5 * (acc * t) * bell
    phi = jnp.where(u >= 0.0, 1.0 - tail, tail)
    return u * phi, phi + (u * bell) * (1.0 / math.sqrt(2.0 * math.pi))


def spec(kind):
    if kind == "s":
        return pl.BlockSpec(memory_space=pltpu.SMEM)
    if kind == "v":
        return pl.BlockSpec(memory_space=pltpu.VMEM)
    return pl.BlockSpec(memory_space=pl.ANY)


def kernel_call(body, name, in_kinds, outs, scratch, vmem_mib, flops, moved):
    return pl.pallas_call(
        body,
        name=name,
        in_specs=[spec(k) for k in in_kinds],
        out_specs=[spec(k) for k, _, _ in outs],
        out_shape=[jax.ShapeDtypeStruct(s, d) for _, s, d in outs],
        scratch_shapes=scratch,
        compiler_params=pltpu.CompilerParams(vmem_limit_bytes=vmem_mib * 2**20),
        cost_estimate=pl.CostEstimate(flops=flops, bytes_accessed=moved, transcendentals=0),
    )


W_SHAPE = (4, D, D)


def place_start(meta, pieces, w, sems):
    d = meta[0]
    for part in range(4):
        rel, half = divmod(part, 2)
        for sel in range(2):
            src = pieces[half * 4 + rel * 2 + sel]
            for j in range(8):
                row = pl.multiple_of((d ^ MASKS[half][sel][j]) * ROWS, 16)
                pltpu.make_async_copy(
                    src.at[j], w.at[part, pl.ds(row, ROWS)], sems.at[part]
                ).start()


def place_wait(w, sems, part):
    pltpu.make_async_copy(w.at[part], w.at[part], sems.at[part]).wait()


def attn_fwd_body(meta, xo, xr, *refs):
    pieces = refs[:8]
    s12, s24 = refs[8:10]
    q_ref, k_ref, v_ref, p_out, ot_ref, o0, o1, yh_ref, rs_ref, hb_ref = refs[10:20]
    w, p_buf, w_sems, p_sems = refs[20:]
    place_start(meta, pieces, w, w_sems)
    t, length = meta[1], meta[2]
    for rel in range(2):
        h = t ^ rel
        place_wait(w, w_sems, rel * 2)
        place_wait(w, w_sems, rel * 2 + 1)
        bq = s24[pl.ds(h, 1), :]
        bv = s24[pl.ds(2 + h, 1), :]
        for r, x in ((0, xo), (1, xr)):
            rows = pl.ds(r * HALF, HALF)
            qk = dot(x[...], w[rel * 2])
            q = (qk[:, :384] + bq).astype(BF) * jnp.asarray(HD**-0.5, BF)
            k = qk[:, 384:].astype(BF)
            v = (dot(x[...], w[rel * 2 + 1, :, :384]) + bv).astype(BF)
            for i in range(3):
                cols = slice(i * 128, (i + 1) * 128)
                q_ref[rel * 3 + i, rows, :] = q[:, cols]
                k_ref[rel * 3 + i, rows, :] = k[:, cols]
                v_ref[rel * 3 + i, rows, :] = v[:, cols]
    row = lax.broadcasted_iota(jnp.int32, (SEQ, 1), 0)
    first = row < HALF
    position = jnp.where(first, row + t * HALF, row + (1 - t) * HALF - HALF)
    valid = position < length
    lane = lax.broadcasted_iota(jnp.int32, (SEQ, 128), 1)
    for rel in range(2):
        o_ref = (o0, o1)[rel]

        def pair(i, carry, rel=rel, o_ref=o_ref):
            p = rel * 3 + i
            keys = k_ref[p]
            q_t = q_ref[p].T
            v_t = v_ref[p].T
            halves = []
            for hh in range(2):
                own = (lane < HD) if hh == 0 else (lane >= HD)
                s = dot(jnp.where(own, keys, jnp.zeros_like(keys)), q_t)
                s = jnp.where(valid, s, MASK_FILL)
                e = jnp.exp(s - jnp.max(s, 0, keepdims=True))
                prob = (e * (1.0 / jnp.sum(e, 0, keepdims=True))).astype(BF)
                p_buf[2 * p + hh] = prob
                pltpu.make_async_copy(
                    p_buf.at[2 * p + hh], p_out.at[2 * p + hh], p_sems.at[2 * p + hh]
                ).start()
                halves.append(dot(v_t[hh * HD : (hh + 1) * HD], prob))
            o_t = jnp.concatenate(halves, 0).astype(BF)
            ot_ref[p] = o_t
            o_ref[:, pl.ds(pl.multiple_of(i * 128, 128), 128)] = o_t.T
            return carry

        lax.fori_loop(0, 3, pair, 0)
    bo, g1, c1 = s12[2:3, :], s12[4:5, :], s12[5:6, :]
    for r, x in ((0, xo), (1, xr)):
        rows = pl.ds(r * HALF, HALF)
        a = dot_t(o0[rows, :], w[1, :, 384:]) + dot_t(o1[rows, :], w[3, :, 384:])
        y = x[...].astype(F32) + a + bo
        centred = y - jnp.mean(y, -1, keepdims=True)
        inv = lax.rsqrt(jnp.mean(centred * centred, -1, keepdims=True) + EPS_NORM)
        hat = centred * inv
        yh_ref[rows, :] = hat
        rs_ref[rows, :] = inv
        hb_ref[rows, :] = (hat * g1 + c1).astype(BF)
    for i in range(12):
        pltpu.make_async_copy(p_buf.at[i], p_out.at[i], p_sems.at[i]).wait()


def attn_fwd(meta, xo, xr, pieces, s12, s24):
    return kernel_call(
        attn_fwd_body,
        "attn_fwd",
        "svv" + "a" * 8 + "vv",
        [
            ("v", (PAIRS, SEQ, 128), BF),
            ("v", (PAIRS, SEQ, 128), BF),
            ("v", (PAIRS, SEQ, 128), BF),
            ("a", (12, SEQ, SEQ), BF),
            ("v", (PAIRS, 128, SEQ), BF),
            ("v", (SEQ, 384), BF),
            ("v", (SEQ, 384), BF),
            ("v", (SEQ, D), F32),
            ("v", (SEQ, 1), F32),
            ("v", (SEQ, D), BF),
        ],
        [
            pltpu.VMEM(W_SHAPE, BF),
            pltpu.VMEM((12, SEQ, SEQ), BF),
            pltpu.SemaphoreType.DMA((4,)),
            pltpu.SemaphoreType.DMA((12,)),
        ],
        40,
        6 * 10**9,
        20 * 10**6,
    )(meta, xo, xr, *pieces, s12, s24)


CHUNK = 256
PER_PART = D // CHUNK


def chunk_of(c):
    return pl.ds(pl.multiple_of((c % PER_PART) * CHUNK, CHUNK), CHUNK)


def ffn_up_body(meta, hb, *refs):
    pieces = refs[:8]
    b1, f0, f1, gp, w, sems = refs[8:]
    c = pl.program_id(0)

    @pl.when(c == 0)
    def _():
        place_start(meta, pieces, w, sems)

    part = c // PER_PART

    @pl.when(c % PER_PART == 0)
    def _():
        place_wait(w, sems, part)

    u = dot(hb[...], w[part, :, chunk_of(c)]) + b1[0]
    f, slope = gelu_pair(u)
    gp[0] = slope.astype(BF)

    @pl.when(part < 2)
    def _():
        f0[...] = f.astype(BF)

    @pl.when(part >= 2)
    def _():
        f1[...] = f.astype(BF)


N_CHUNKS = FF // CHUNK
SIDE = N_CHUNKS // 2


def grid_call(body, name, in_specs, out_specs, out_shape, scratch, vmem_mib, flops, moved):
    return pl.pallas_call(
        body,
        name=name,
        grid_spec=pltpu.PrefetchScalarGridSpec(
            num_scalar_prefetch=1,
            grid=(N_CHUNKS,),
            in_specs=in_specs,
            out_specs=out_specs,
            scratch_shapes=scratch,
        ),
        out_shape=out_shape,
        compiler_params=pltpu.CompilerParams(
            vmem_limit_bytes=vmem_mib * 2**20, dimension_semantics=("arbitrary",)
        ),
        cost_estimate=pl.CostEstimate(flops=flops, bytes_accessed=moved, transcendentals=0),
    )


def whole(shape):
    return pl.BlockSpec(shape, lambda c, meta: (0,) * len(shape))


ANY = pl.BlockSpec(memory_space=pl.ANY)
SIDE_SPECS = [
    pl.BlockSpec((SEQ, CHUNK), lambda c, meta: (0, jnp.minimum(c, SIDE - 1))),
    pl.BlockSpec((SEQ, CHUNK), lambda c, meta: (0, jnp.maximum(c - SIDE, 0))),
]
BIAS_SPEC = pl.BlockSpec((1, 1, CHUNK), lambda c, meta: (meta[1] ^ (c // SIDE), 0, c % SIDE))
BOTH_SPEC = pl.BlockSpec((1, SEQ, CHUNK), lambda c, meta: (c // SIDE, 0, c % SIDE))


def ffn_up(meta, hb, pieces, b1):
    return grid_call(
        ffn_up_body,
        "ffn_up",
        [whole((SEQ, D))] + [ANY] * 8 + [BIAS_SPEC],
        SIDE_SPECS + [BOTH_SPEC],
        [
            jax.ShapeDtypeStruct((SEQ, FF // 2), BF),
            jax.ShapeDtypeStruct((SEQ, FF // 2), BF),
            jax.ShapeDtypeStruct((2, SEQ, FF // 2), BF),
        ],
        [pltpu.VMEM(W_SHAPE, BF), pltpu.SemaphoreType.DMA((4,))],
        24,
        5 * 10**9,
        12 * 10**6,
    )(meta, hb, *pieces, b1)


def norm_back(grad, hat, inv, gain):
    scaled = grad * gain
    return inv * (
        scaled
        - jnp.mean(scaled, -1, keepdims=True)
        - hat * jnp.mean(scaled * hat, -1, keepdims=True)
    )


def row_sum(v):
    return jnp.sum(v, 0, keepdims=True)


def ffn_down_body(meta, f0, f1, *refs):
    pieces = refs[:8]
    yh, co, cr, s12, out_o, out_r, dz, dy2, sums, w, sems = refs[8:]
    place_start(meta, pieces, w, sems)
    t, length = meta[1], meta[2]
    b2 = s12[3:4, :]
    g1, c1, g2, c2 = s12[4:5, :], s12[5:6, :], s12[6:7, :], s12[7:8, :]
    for part in range(4):
        place_wait(w, sems, part)
    totals = [jnp.zeros((1, D), F32)] * 3
    for r, cot, out in ((0, co, out_o), (1, cr, out_r)):
        rows = pl.ds(r * HALF, HALF)
        z = dot_t(f0[rows, :D], w[0])
        z = z + dot_t(f0[rows, D:], w[1])
        z = z + dot_t(f1[rows, :D], w[2])
        z = z + dot_t(f1[rows, D:], w[3])
        y = yh[rows, :] * g1 + c1 + z + b2
        centred = y - jnp.mean(y, -1, keepdims=True)
        inv = lax.rsqrt(jnp.mean(centred * centred, -1, keepdims=True) + EPS_NORM)
        hat = centred * inv
        out[...] = (hat * g2 + c2).astype(BF)
        row = lax.broadcasted_iota(jnp.int32, (HALF, 1), 0)
        valid = row + (t ^ r) * HALF < length
        dout = jnp.where(valid, cot[...].astype(F32), 0.0)
        grad = norm_back(dout, hat, inv, g2)
        dy2[rows, :] = grad
        dz[rows, :] = grad.astype(BF)
        totals = [
            a + row_sum(b) for a, b in zip(totals, (grad, dout * hat, dout), strict=True)
        ]
    for i in range(3):
        sums[i : i + 1, :] = totals[i]


def ffn_down(meta, f0, f1, pieces, yh, co, cr, s12):
    return kernel_call(
        ffn_down_body,
        "ffn_down",
        "svv" + "a" * 8 + "vvvv",
        [
            ("v", (HALF, D), BF),
            ("v", (HALF, D), BF),
            ("v", (SEQ, D), BF),
            ("v", (SEQ, D), F32),
            ("v", (8, D), F32),
        ],
        [pltpu.VMEM(W_SHAPE, BF), pltpu.SemaphoreType.DMA((4,))],
        28,
        3 * 10**9,
        12 * 10**6,
    )(meta, f0, f1, *pieces, yh, co, cr, s12)


def ffn_back_body(meta, dz, *refs):
    pieces = refs[:8]
    gp, du0, du1, db1, w, sems = refs[8:]
    c = pl.program_id(0)

    @pl.when(c == 0)
    def _():
        place_start(meta, pieces, w, sems)

    part = c // PER_PART

    @pl.when(c % PER_PART == 0)
    def _():
        place_wait(w, sems, part)

    du = dot(dz[...], w[part, :, chunk_of(c)]) * gp[0].astype(F32)
    db1[0] = row_sum(du)

    @pl.when(part < 2)
    def _():
        du0[...] = du.astype(BF)

    @pl.when(part >= 2)
    def _():
        du1[...] = du.astype(BF)


def ffn_back(meta, dz, pieces, gp):
    return grid_call(
        ffn_back_body,
        "ffn_back",
        [whole((SEQ, D))] + [ANY] * 8 + [BOTH_SPEC],
        SIDE_SPECS + [BIAS_SPEC],
        [
            jax.ShapeDtypeStruct((SEQ, FF // 2), BF),
            jax.ShapeDtypeStruct((SEQ, FF // 2), BF),
            jax.ShapeDtypeStruct((2, 1, FF // 2), F32),
        ],
        [pltpu.VMEM(W_SHAPE, BF), pltpu.SemaphoreType.DMA((4,))],
        24,
        3 * 10**9,
        12 * 10**6,
    )(meta, dz, *pieces, gp)


def hidden_back_body(meta, du0, du1, *refs):
    pieces = refs[:8]
    dy2, yh, inv, s12, dy1, da, sums, w, sems = refs[8:]
    place_start(meta, pieces, w, sems)
    g1 = s12[4:5, :]
    for part in range(4):
        place_wait(w, sems, part)
    totals = [jnp.zeros((1, D), F32)] * 3
    for r in range(2):
        rows = pl.ds(r * HALF, HALF)
        dh = dy2[rows, :] + dot_t(du0[rows, :D], w[0])
        dh = dh + dot_t(du0[rows, D:], w[1])
        dh = dh + dot_t(du1[rows, :D], w[2])
        dh = dh + dot_t(du1[rows, D:], w[3])
        hat = yh[rows, :]
        grad = norm_back(dh, hat, inv[rows, :], g1)
        dy1[rows, :] = grad
        da[rows, :] = grad.astype(BF)
        totals = [a + row_sum(b) for a, b in zip(totals, (grad, dh * hat, dh), strict=True)]
    for i in range(3):
        sums[i : i + 1, :] = totals[i]


def hidden_back(meta, du0, du1, pieces, dy2, yh, inv, s12):
    return kernel_call(
        hidden_back_body,
        "hidden_back",
        "svv" + "a" * 8 + "vvvv",
        [("v", (SEQ, D), F32), ("v", (SEQ, D), BF), ("v", (8, D), F32)],
        [pltpu.VMEM(W_SHAPE, BF), pltpu.SemaphoreType.DMA((4,))],
        28,
        3 * 10**9,
        12 * 10**6,
    )(meta, du0, du1, *pieces, dy2, yh, inv, s12)


def attn_back_body(meta, da, dy1, *refs):
    pieces = refs[:8]
    q_ref, k_ref, v_ref, p_in, ot_ref = refs[8:13]
    dq0, dk0, dv0, dq1, dk1, dv1, dx_o, dx_r, sums = refs[13:22]
    w, p_buf, do_ref, w_sems, p_sems = refs[22:]
    place_start(meta, pieces, w, w_sems)
    for i in range(12):
        pltpu.make_async_copy(p_in.at[i], p_buf.at[i], p_sems.at[i]).start()
    t = meta[1]
    for rel in range(2):
        place_wait(w, w_sems, rel * 2 + 1)
        do = dot(da[...], w[rel * 2 + 1, :, 384:]).astype(BF)
        for i in range(3):
            do_ref[rel * 3 + i] = do[:, i * 128 : (i + 1) * 128]
    lane = lax.broadcasted_iota(jnp.int32, (SEQ, 128), 1)
    low_lane = lane < HD
    for rel in range(2):
        dq_ref, dk_ref, dv_ref = ((dq0, dk0, dv0), (dq1, dk1, dv1))[rel]

        def pair(i, carry, rel=rel, dq_ref=dq_ref, dk_ref=dk_ref, dv_ref=dv_ref):
            p = rel * 3 + i
            dop = do_ref[p]
            qp = q_ref[p]
            vp = v_ref[p]
            k_t = k_ref[p].T
            do_t = dop.T
            both = do_t.astype(F32) * ot_ref[p].astype(F32)
            parts = []
            for hh in range(2):
                own = low_lane if hh == 0 else (lane >= HD)
                inside = slice(hh * HD, (hh + 1) * HD)
                delta = row_sum(both[inside])
                slope = dot(jnp.where(own, vp, jnp.zeros_like(vp)), do_t)
                pltpu.make_async_copy(
                    p_in.at[2 * p + hh], p_buf.at[2 * p + hh], p_sems.at[2 * p + hh]
                ).wait()
                prob = p_buf[2 * p + hh]
                ds = (prob.astype(F32) * (slope - delta)).astype(BF)
                parts.append((dot(prob, dop), dot(ds, qp), dot(k_t[inside], ds)))
            cols = pl.ds(pl.multiple_of(i * 128, 128), 128)
            dv_ref[:, cols] = jnp.where(low_lane, parts[0][0], parts[1][0]).astype(BF)
            dk_ref[:, cols] = jnp.where(low_lane, parts[0][1], parts[1][1]).astype(BF)
            dq_t = jnp.concatenate([parts[0][2], parts[1][2]], 0) * (HD**-0.5)
            dq_ref[:, cols] = dq_t.T.astype(BF)
            return carry

        lax.fori_loop(0, 3, pair, 0)
        h = t ^ rel
        sums[pl.ds(h, 1), :] = row_sum(dq_ref[...].astype(F32))
        sums[pl.ds(2 + h, 1), :] = row_sum(dv_ref[...].astype(F32))
    place_wait(w, w_sems, 0)
    place_wait(w, w_sems, 2)
    for r, dx in ((0, dx_o), (1, dx_r)):
        rows = pl.ds(r * HALF, HALF)
        total = dy1[rows, :]
        for rel in range(2):
            dq_ref, dk_ref, dv_ref = ((dq0, dk0, dv0), (dq1, dk1, dv1))[rel]
            total = total + dot_t(dq_ref[rows, :], w[rel * 2, :, :384])
            total = total + dot_t(dk_ref[rows, :], w[rel * 2, :, 384:])
            total = total + dot_t(dv_ref[rows, :], w[rel * 2 + 1, :, :384])
        dx[...] = total


def attn_back(meta, da, dy1, pieces, q, k, v, prob, o_t):
    return kernel_call(
        attn_back_body,
        "attn_back",
        "svv" + "a" * 8 + "vvvav",
        [("v", (SEQ, 384), BF)] * 6 + [("v", (HALF, D), F32)] * 2 + [("v", (8, 384), F32)],
        [
            pltpu.VMEM(W_SHAPE, BF),
            pltpu.VMEM((12, SEQ, SEQ), BF),
            pltpu.VMEM((PAIRS, SEQ, 128), BF),
            pltpu.SemaphoreType.DMA((4,)),
            pltpu.SemaphoreType.DMA((12,)),
        ],
        40,
        8 * 10**9,
        20 * 10**6,
    )(meta, da, dy1, *pieces, q, k, v, prob, o_t)


def put_out(meta, acc, outs, sems):
    d = meta[0]
    for half in range(2):
        for sel in range(2):
            out = outs[half * 2 + sel]
            for j in range(8):
                row = pl.multiple_of((d ^ MASKS[half][sel][j]) * ROWS, 16)
                pltpu.make_async_copy(
                    acc.at[half, pl.ds(row, ROWS)], out.at[j], sems.at[half]
                ).start()


def put_wait(acc, sems):
    for half in range(2):
        pltpu.make_async_copy(acc.at[half], acc.at[half], sems.at[half]).wait()


GRAD_OUTS = [("a", (8, ROWS, D), BF)] * 4


def ffn_grad_body(meta, left_o, left_r, right_o, right_r, *refs):
    outs = refs[:4]
    left_t, acc, sems = refs[4:]
    left_t[:, :SEQ] = left_o[...].T
    left_t[:, SEQ:] = left_r[...].T
    for half in range(2):
        cols = slice(half * D, (half + 1) * D)
        for m in range(3):
            rows = pl.ds(m * 256, 256)
            total = dot(left_t[rows, :SEQ], right_o[:, cols])
            total = total + dot(left_t[rows, SEQ:], right_r[:, cols])
            acc[half, rows, :] = total.astype(BF)
    put_out(meta, acc, outs, sems)
    put_wait(acc, sems)


def ffn_grad(meta, left_o, left_r, right_o, right_r):
    return kernel_call(
        ffn_grad_body,
        "ffn_grad",
        "svvvv",
        GRAD_OUTS,
        [
            pltpu.VMEM((D, 2 * SEQ), BF),
            pltpu.VMEM((2, D, D), BF),
            pltpu.SemaphoreType.DMA((2,)),
        ],
        24,
        3 * 10**9,
        8 * 10**6,
    )(meta, left_o, left_r, right_o, right_r)


def attn_grad_body(meta, xo, xr, zo, zr, dao, dar, *refs):
    dq0, dk0, dv0, oo, dqr, dkr, dvr, orr = refs[:8]
    outs = refs[8:12]
    x_t, da_t, acc, sems = refs[12:]
    x_t[:, :HALF] = xo[...].T
    x_t[:, HALF:SEQ] = xr[...].T
    x_t[:, SEQ : SEQ + HALF] = zo[...].T
    x_t[:, SEQ + HALF :] = zr[...].T
    da_t[:, :SEQ] = dao[...].T
    da_t[:, SEQ:] = dar[...].T
    for half, side, left_t, own, other in (
        (0, 0, x_t, dq0, dqr),
        (0, 1, x_t, dk0, dkr),
        (1, 0, x_t, dv0, dvr),
        (1, 1, da_t, oo, orr),
    ):
        for m in range(3):
            rows = pl.ds(m * 256, 256)
            total = dot(left_t[rows, :SEQ], own[...]) + dot(left_t[rows, SEQ:], other[...])
            acc[half, rows, side * 384 : (side + 1) * 384] = total.astype(BF)
    put_out(meta, acc, outs, sems)
    put_wait(acc, sems)


def attn_grad(meta, xs, das, own, other):
    return kernel_call(
        attn_grad_body,
        "attn_grad",
        "s" + "v" * 14,
        GRAD_OUTS,
        [
            pltpu.VMEM((D, 2 * SEQ), BF),
            pltpu.VMEM((D, 2 * SEQ), BF),
            pltpu.VMEM((2, D, D), BF),
            pltpu.SemaphoreType.DMA((2,)),
        ],
        24,
        3 * 10**9,
        8 * 10**6,
    )(meta, *xs, *das, *own, *other)


def adamw(weight, moment_one, moment_two, grad, rate, decay):
    new_one = BETA_ONE * moment_one + (1.0 - BETA_ONE) * grad
    new_two = BETA_TWO * moment_two + (1.0 - BETA_TWO) * grad * grad
    fixed_one = new_one / (1.0 - BETA_ONE**STEP)
    fixed_two = new_two / (1.0 - BETA_TWO**STEP)
    update = fixed_one / (jnp.sqrt(fixed_two) + ADAM_EPS) + decay * weight
    return (weight - rate * update, new_one, new_two)


def other_core(v):
    return lax.ppermute(v, "tensor", [(0, 1), (1, 0)])


def shift(v, mask, n):
    return lax.ppermute(v, "dp", [(i, i ^ mask) for i in range(n)])


def gather_half(block, half, n):
    near, far = (STEP_A, STEP_B)[half]
    own = jnp.stack([block] + [shift(block, z, n) for z in Z_MASKS[1:]])
    own = jnp.concatenate([own, shift(own, near, n)])
    far_side = shift(own, far, n)
    return [own, far_side, other_core(own), other_core(far_side)]


def gather(halves, n):
    if n == BLOCKS:
        return gather_half(halves[0], 0, n) + gather_half(halves[1], 1, n)
    result = []
    for half in range(2):
        full = lax.all_gather(halves[half], "dp", axis=0, tiled=True)
        blocks = full.reshape(BLOCKS, ROWS, D)
        own = [blocks[jnp.array(m)] for m in MASKS[half]]
        result += own + [other_core(v) for v in own]
    return result


def added(*parts):
    total = parts[0].astype(F32)
    for p in parts[1:]:
        total = total + p.astype(F32)
    return total


def scatter_half(keep, send, half, n):
    near, far = (STEP_A, STEP_B)[half]
    came = shift(send, far, n)
    send = added(keep[4:], came[4:]).astype(BF)
    keep = added(keep[:4], came[:4]).astype(BF)
    came = shift(send, near, n)
    sends = [added(keep[i], came[i]).astype(BF) for i in range(1, 4)]
    arrived = [shift(s, z, n) for s, z in zip(sends, Z_MASKS[1:], strict=True)]
    return added(keep[0], came[0], *arrived)


def scatter(pieces, n):
    result = []
    for half in range(2):
        keep, send = pieces[2 * half], pieces[2 * half + 1]
        if n == BLOCKS:
            result.append(scatter_half(keep, send, half, n))
            continue
        order = MASKS[half][0] + MASKS[half][1]
        back = [order.index(i) for i in range(BLOCKS)]
        full = jnp.concatenate([keep, send])[jnp.array(back)].reshape(D, D).astype(F32)
        result.append(lax.psum_scatter(full, "dp", scatter_dimension=0, tiled=True))
    return result


def total_over_all(v, n):
    if n != BLOCKS:
        return lax.psum(v, ("dp", "tensor"))
    v = v + other_core(v)
    for masks in ((1, 2, 3), (4, 8, 12)):
        a, b, c = [shift(v, m, n) for m in masks]
        v = (v + a) + (b + c)
    return v


def per_device(
    frames,
    cotangent,
    lengths,
    attn_w,
    attn_m,
    attn_v,
    ffn_w,
    ffn_m,
    ffn_v,
    small_w,
    small_m,
    small_v,
):
    n = lax.axis_size("dp")
    t = lax.axis_index("tensor")
    d = lax.axis_index("dp") if n == BLOCKS else 0
    length = lax.dynamic_index_in_dim(lengths[:, 0], t, 0, keepdims=False)
    meta = jnp.stack([jnp.asarray(d, jnp.int32), jnp.asarray(t, jnp.int32), length])
    s12 = small_w.reshape(12, D)
    s24 = small_w.reshape(24, 384)
    b1 = small_w[8 * D :].reshape(2, 1, FF // 2)

    aw = attn_w.astype(BF)
    fw = ffn_w.astype(BF)
    attn_pieces = gather(
        [jnp.concatenate([aw[0], aw[1]], 1), jnp.concatenate([aw[2], aw[3]], 1)], n
    )
    up_pieces = gather([fw[0, :, :D], fw[0, :, D:]], n)
    down_pieces = gather([fw[1, :, :D], fw[1, :, D:]], n)

    def mine(v):
        return lax.dynamic_index_in_dim(v[:, 0], t, 0, keepdims=False)

    def theirs(v):
        return lax.dynamic_index_in_dim(v[:, 0], 1 - t, 0, keepdims=False)

    xo, zr = mine(frames), theirs(frames)
    xr = other_core(zr)
    zo = other_core(xo)
    co = mine(cotangent)
    cr = other_core(theirs(cotangent))

    q, k, v, prob, o_t, o0, o1, yh, inv, hb = attn_fwd(meta, xo, xr, attn_pieces, s12, s24)
    hb_r = other_core(hb)
    o_r = other_core(o1)
    f0, f1, gp = ffn_up(meta, hb, up_pieces, b1)
    f_r = other_core(f1)
    out_o, out_r, dz, dy2, sums_two = ffn_down(meta, f0, f1, down_pieces, yh, co, cr, s12)
    dz_r = other_core(dz)
    du0, du1, db1 = ffn_back(meta, dz, down_pieces, gp)
    du_r = other_core(du1)
    down_grads = scatter(ffn_grad(meta, dz, dz_r, f0, f_r), n)
    up_grads = scatter(ffn_grad(meta, hb, hb_r, du0, du_r), n)
    dy1, da, sums_one = hidden_back(meta, du0, du1, up_pieces, dy2, yh, inv, s12)
    da_r = other_core(da)
    early = jnp.concatenate(
        [
            sums_one[:1].reshape(-1),
            sums_two[:1].reshape(-1),
            sums_one[1:3].reshape(-1),
            sums_two[1:3].reshape(-1),
            db1.reshape(-1),
        ]
    )
    early = total_over_all(early, n)
    dq0, dk0, dv0, dq1, dk1, dv1, dx_o, dx_r, sums_qv = attn_back(
        meta, da, dy1, attn_pieces, q, k, v, prob, o_t
    )
    attn_grads = scatter(
        attn_grad(
            meta,
            (xo, xr, zo, zr),
            (da, da_r),
            (dq0, dk0, dv0, o0),
            (other_core(dq1), other_core(dk1), other_core(dv1), o_r),
        ),
        n,
    )

    def joined(own, other):
        return jnp.where(t == 0, jnp.stack([own, other]), jnp.stack([other, own]))[:, None]

    output = joined(out_o, other_core(out_r))
    frames_grad = joined(dx_o, other_core(dx_r))

    attn_g = jnp.stack(
        [
            attn_grads[0][:, :384],
            attn_grads[0][:, 384:],
            attn_grads[1][:, :384],
            attn_grads[1][:, 384:],
        ]
    )
    ffn_g = jnp.stack(
        [jnp.concatenate(up_grads, 1), jnp.concatenate(down_grads, 1)]
    )
    half = SEQ // lax.axis_size("tensor")
    count_part = jnp.sum(jnp.clip(lengths - t * half, 0, half)).astype(F32)
    square_part = sum(jnp.sum(g * g) for g in attn_grads + up_grads + down_grads)
    late = jnp.concatenate(
        [sums_qv[:4].reshape(-1), jnp.stack([square_part, count_part]), jnp.zeros((126,), F32)]
    )
    late = total_over_all(late, n)
    small_sum = jnp.concatenate([late[: 2 * D], early])
    square_sum, frame_count = late[2 * D], late[2 * D + 1]
    grad_norm = jnp.sqrt(square_sum + jnp.sum(small_sum * small_sum)) / frame_count
    factor = jnp.minimum(1.0, CLIP_NORM / grad_norm) / frame_count
    attn_rates = RATE * jnp.array([1.0, 1.0, 1.0, 0.5 * SEQ**0.5], F32)[:, None, None]
    attn_new, attn_m_new, attn_v_new = adamw(
        attn_w, attn_m, attn_v, attn_g * factor, attn_rates, DECAY
    )
    ffn_new, ffn_m_new, ffn_v_new = adamw(ffn_w, ffn_m, ffn_v, ffn_g * factor, RATE, DECAY)
    small_new, small_m_new, small_v_new = adamw(
        small_w, small_m, small_v, small_sum * factor, SMALL_RATE, 0.0
    )
    return (
        output,
        frames_grad,
        grad_norm,
        attn_new,
        attn_m_new,
        attn_v_new,
        ffn_new,
        ffn_m_new,
        ffn_v_new,
        small_new,
        small_m_new,
        small_v_new,
    )


def solution(mesh):
    rows = P(None, "dp", "tensor", None)
    weights = P(None, "dp", "tensor")
    in_specs = (rows, rows, P(None, "dp")) + (weights,) * 6 + (P(),) * 3
    out_specs = (rows, rows, P()) + (weights,) * 6 + (P(),) * 3
    return jax.shard_map(
        per_device, mesh=mesh, in_specs=in_specs, out_specs=out_specs, check_vma=False
    )
```

```python
import math

import jax
import jax.numpy as jnp
from jax import lax
from jax.experimental import pallas as pl
from jax.experimental.pallas import tpu as pltpu
from jax.sharding import PartitionSpec as P

HD = 64
D = 768
FF = 3072
SEQ = 512
HALF = SEQ // 2
STEP = 10
SMALL = 9216
PAIRS = 6
BLOCKS = 16
ROWS = D // BLOCKS

EPS_NORM = 1e-05
MASK_FILL = -1e30
BETA_ONE = 0.9
BETA_TWO = 0.999
ADAM_EPS = 1e-08
CLIP_NORM = 0.1
RATE = 0.1
SMALL_RATE = 1.5
DECAY = 0.01

BF = jnp.bfloat16
F32 = jnp.float32

STEP_A = (2, 1)
STEP_B = (1, 2)
Z_MASKS = (0, 4, 8, 12)
MASKS = tuple(
    (
        tuple(z for z in Z_MASKS) + tuple(z + near for z in Z_MASKS),
        tuple(z + far for z in Z_MASKS) + tuple(z + near + far for z in Z_MASKS),
    )
    for near, far in (STEP_A, STEP_B)
)


def dot(left, right):
    return jnp.dot(left, right, preferred_element_type=F32)


def dot_t(left, right):
    return lax.dot_general(left, right, (((1,), (1,)), ((), ())), preferred_element_type=F32)


def gelu_pair(u):
    phi = 0.5 * lax.erf(u * math.sqrt(0.5)) + 0.5
    return u * phi, phi + u * jnp.exp(-0.5 * u * u) * (1.0 / math.sqrt(2.0 * math.pi))


HBM = pl.BlockSpec(memory_space=pltpu.HBM)
SMEM = pl.BlockSpec(memory_space=pltpu.SMEM)


VMEM = pl.BlockSpec(memory_space=pltpu.VMEM)


def kernel_call(body, name, meta, raw, ins, outs, raw_outs, scratch, micros):
    n_raw, n_in, n_out, n_raw_out = len(raw), len(ins), len(outs), len(raw_outs)

    def run(meta_ref, *refs):
        cuts = [0, n_raw, n_in, n_out, n_raw_out]
        for i in range(1, 5):
            cuts[i] += cuts[i - 1]
        groups = [refs[cuts[i] : cuts[i + 1]] for i in range(4)]
        body(meta_ref, *groups, *refs[cuts[4] :])

    held = sum(
        math.prod(v.shape) * (2 if v.dtype == BF else 4) for v in scratch if v.dtype in (BF, F32)
    )
    return pl.pallas_call(
        run,
        name=name,
        in_specs=[SMEM] + [HBM] * n_raw + [VMEM] * n_in,
        out_specs=[VMEM] * n_out + [HBM] * n_raw_out,
        out_shape=[jax.ShapeDtypeStruct(s, d) for s, d in outs]
        + [pltpu.HBM(s, d) for s, d in raw_outs],
        scratch_shapes=scratch,
        compiler_params=pltpu.CompilerParams(vmem_limit_bytes=held + SPARE),
        cost_estimate=pl.CostEstimate(
            flops=int(micros * 1.15e9), bytes_accessed=0, transcendentals=0
        ),
    )(meta, *[pltpu.with_memory_space_constraint(v, pltpu.HBM) for v in raw], *ins)


SPARE = 8 * 2**20
W_SHAPE = (4, D, D)


def place(meta, pieces, w):
    d = meta[0]
    for part in range(4):
        rel, half = divmod(part, 2)
        for sel in range(2):
            src = pieces[half * 4 + rel * 2 + sel]
            for j in range(8):
                row = pl.multiple_of((d ^ MASKS[half][sel][j]) * ROWS, 16)
                w[part, pl.ds(row, ROWS), :] = src[j]


def chunk(c):
    return pl.ds(pl.multiple_of(c * CHUNK, CHUNK), CHUNK)


CHUNK = 256
PER_PART = D // CHUNK


def row_sum(v):
    return jnp.sum(v, 0, keepdims=True)


def attn_fwd_body(meta, _, ins, outs, raw_outs, q_ref, o_ref, w, p_buf, p_sems, w_sem, sems, *head_refs):
    xo, xr, s12, *pieces = ins
    yh, rs, hb, shared = outs
    place(meta, pieces, w)
    w_copy = pltpu.make_async_copy(w, raw_outs[10], w_sem.at[0])
    w_copy.start()
    head_copies = [
        pltpu.make_async_copy(head_refs[i], raw_outs[i], sems.at[i]) for i in range(8)
    ]
    t, length = meta[1], meta[2]
    row = lax.broadcasted_iota(jnp.int32, (SEQ, 1), 0)
    position = jnp.where(row < HALF, row + t * HALF, row + (1 - t) * HALF - HALF)
    valid = position < length
    lane = lax.broadcasted_iota(jnp.int32, (SEQ, 128), 1)
    for rel in range(2):
        k_ref, v_ref, qt_ref, ot_ref = head_refs[rel * 4 : rel * 4 + 4]
        p_out = raw_outs[8 + rel]
        cols = pl.ds(pl.multiple_of((t ^ rel) * 384, 128), 384)
        bq = s12[0:1, cols]
        bv = s12[1:2, cols]
        for r, x in ((0, xo), (1, xr)):
            rows = pl.ds(r * HALF, HALF)
            qk = dot(x[...], w[rel * 2])
            q = (qk[:, :384] + bq).astype(BF) * jnp.asarray(HD**-0.5, BF)
            k = qk[:, 384:].astype(BF)
            v = (dot(x[...], w[rel * 2 + 1, :, :384]) + bv).astype(BF)
            for i in range(3):
                part = slice(i * 128, (i + 1) * 128)
                q_ref[i, rows, :] = q[:, part]
                k_ref[i, rows, :] = k[:, part]
                v_ref[i, rows, :] = v[:, part]

        def pair(i, carry, rel=rel, k_ref=k_ref, v_ref=v_ref, qt_ref=qt_ref, ot_ref=ot_ref, p_out=p_out):
            keys = k_ref[i]
            q_t = q_ref[i].T
            lines = pl.ds(pl.multiple_of(i * 128, 128), 128)
            qt_ref[lines, :] = q_t
            v_t = v_ref[i].T
            halves = []
            for hh in range(2):
                own = (lane < HD) if hh == 0 else (lane >= HD)
                s = dot(jnp.where(own, keys, jnp.zeros_like(keys)), q_t)
                s = jnp.where(valid, s, MASK_FILL)
                e = jnp.exp(s - jnp.max(s, 0, keepdims=True))
                prob = (e * (1.0 / jnp.sum(e, 0, keepdims=True))).astype(BF)
                head = 2 * i + hh
                slot = rel * 6 + head
                p_buf[slot] = prob
                pltpu.make_async_copy(p_buf.at[slot], p_out.at[head], p_sems.at[slot]).start()
                halves.append(dot(v_t[hh * HD : (hh + 1) * HD], prob))
            o_t = jnp.concatenate(halves, 0).astype(BF)
            ot_ref[lines, :] = o_t
            o_ref[rel, :, lines] = o_t.T
            return carry

        lax.fori_loop(0, 3, pair, 0)
        for c in head_copies[rel * 4 : rel * 4 + 4]:
            c.start()
    bo, g1, c1 = s12[2:3, :], s12[4:5, :], s12[5:6, :]
    for r, x in ((0, xo), (1, xr)):
        rows = pl.ds(r * HALF, HALF)
        a = dot_t(o_ref[0, rows, :], w[1, :, 384:]) + dot_t(o_ref[1, rows, :], w[3, :, 384:])
        y = x[...].astype(F32) + a + bo
        centred = y - jnp.mean(y, -1, keepdims=True)
        inv = lax.rsqrt(jnp.mean(centred * centred, -1, keepdims=True) + EPS_NORM)
        hat = centred * inv
        yh[rows, :] = hat
        rs[rows, :] = inv
        hb[rows, :] = (hat * g1 + c1).astype(BF)
    shared[0] = head_refs[7][...]
    for i in range(2):
        shared[1 + i] = hb[:, i * 384 : (i + 1) * 384].T
    for i in range(12):
        pltpu.make_async_copy(
            p_buf.at[i], raw_outs[8 + i // 6].at[i % 6], p_sems.at[i]
        ).wait()
    w_copy.wait()
    for c in head_copies:
        c.wait()


TURNED = ((384, SEQ), BF)
HEADS = [((3, SEQ, 128), BF), ((3, SEQ, 128), BF), TURNED, TURNED]


def attn_fwd(meta, xo, xr, pieces, s12):
    return kernel_call(
        attn_fwd_body,
        "attn_fwd",
        meta,
        [],
        [xo, xr, s12, *pieces],
        [((SEQ, D), F32), ((SEQ, 1), F32), ((SEQ, D), BF), ((3, 384, SEQ), BF)],
        HEADS * 2 + [((6, SEQ, SEQ), BF)] * 2 + [(W_SHAPE, BF)],
        [
            pltpu.VMEM((3, SEQ, 128), BF),
            pltpu.VMEM((2, SEQ, 384), BF),
            pltpu.VMEM(W_SHAPE, BF),
            pltpu.VMEM((12, SEQ, SEQ), BF),
            pltpu.SemaphoreType.DMA((12,)),
            pltpu.SemaphoreType.DMA((1,)),
            pltpu.SemaphoreType.DMA((8,)),
        ]
        + [pltpu.VMEM(*h) for h in HEADS * 2],
        16.0,
    )


def ffn_up_body(meta, _, ins, outs, __):
    hb, s12, *pieces = ins
    f0, f1, gp, w = outs
    place(meta, pieces, w)
    for part in range(4):
        rel, half = divmod(part, 2)
        bias_row = pl.ds(8 + 2 * (meta[1] ^ rel) + half, 1)
        f_ref = (f0, f1)[rel]
        for c in range(PER_PART):
            cols = slice(c * CHUNK, (c + 1) * CHUNK)
            u = dot(hb[...], w[part, :, cols]) + s12[bias_row, cols]
            f, slope = gelu_pair(u)
            f_ref[half, :, cols] = f.astype(BF)
            gp[part, :, cols] = slope.astype(BF)


SIDE = ((2, SEQ, D), BF)
SLABS = ((2, 384, SEQ), BF)


def ffn_up(meta, hb, pieces, s12):
    return kernel_call(
        ffn_up_body,
        "ffn_up",
        meta,
        [],
        [hb, s12, *pieces],
        [SIDE, SIDE, ((4, SEQ, D), BF), (W_SHAPE, BF)],
        [],
        [],
        5.0,
    )


def norm_back(grad, hat, inv, gain):
    scaled = grad * gain
    return inv * (
        scaled
        - jnp.mean(scaled, -1, keepdims=True)
        - hat * jnp.mean(scaled * hat, -1, keepdims=True)
    )


def ffn_down_body(meta, _, ins, outs, __):
    f0, f1, yh, co, cr, s12, *pieces = ins
    out_o, out_r, dz, dz_t, dy2, sums, w = outs
    place(meta, pieces, w)
    t, length = meta[1], meta[2]
    b2 = s12[3:4, :]
    g1, c1, g2, c2 = s12[4:5, :], s12[5:6, :], s12[6:7, :], s12[7:8, :]
    fs = (f0, f1)
    for part in range(4):
        rel, half = divmod(part, 2)
        z = dot_t(fs[rel][half], w[part])
        dy2[...] = z if part == 0 else dy2[...] + z
    totals = [jnp.zeros((1, D), F32)] * 3
    for r, cot, out in ((0, co, out_o), (1, cr, out_r)):
        rows = pl.ds(r * HALF, HALF)
        y = yh[rows, :] * g1 + c1 + dy2[rows, :] + b2
        centred = y - jnp.mean(y, -1, keepdims=True)
        inv = lax.rsqrt(jnp.mean(centred * centred, -1, keepdims=True) + EPS_NORM)
        hat = centred * inv
        out[...] = (hat * g2 + c2).astype(BF)
        row = lax.broadcasted_iota(jnp.int32, (HALF, 1), 0)
        valid = row + (t ^ r) * HALF < length
        dout = jnp.where(valid, cot[...].astype(F32), 0.0)
        grad = norm_back(dout, hat, inv, g2)
        dy2[rows, :] = grad
        dz[rows, :] = grad.astype(BF)
        totals = [a + row_sum(b) for a, b in zip(totals, (grad, dout * hat, dout))]
    for i in range(3):
        sums[i : i + 1, :] = totals[i]
    for i in range(2):
        dz_t[i] = dz[:, i * 384 : (i + 1) * 384].T


def ffn_down(meta, f0, f1, pieces, yh, co, cr, s12):
    return kernel_call(
        ffn_down_body,
        "ffn_down",
        meta,
        [],
        [f0, f1, yh, co, cr, s12, *pieces],
        [
            ((HALF, D), BF),
            ((HALF, D), BF),
            ((SEQ, D), BF),
            SLABS,
            ((SEQ, D), F32),
            ((8, D), F32),
            (W_SHAPE, BF),
        ],
        [],
        [],
        5.0,
    )


def ffn_back_body(meta, _, ins, outs, __):
    dz, gp, w = ins
    du0, du1, db1 = outs
    for part in (2, 3, 0, 1):
        rel, half = divmod(part, 2)
        bias_row = pl.ds(2 * (meta[1] ^ rel) + half, 1)
        du_ref = (du0, du1)[rel]
        for c in range(PER_PART):
            cols = slice(c * CHUNK, (c + 1) * CHUNK)
            du = dot(dz[...], w[part, :, cols]) * gp[part, :, cols].astype(F32)
            db1[bias_row, cols] = row_sum(du)
            du_ref[half, :, cols] = du.astype(BF)


def ffn_back(meta, dz, w, gp):
    return kernel_call(
        ffn_back_body,
        "ffn_back",
        meta,
        [],
        [dz, gp, w],
        [SIDE, SIDE, ((4, D), F32)],
        [],
        [],
        3.5,
    )


def hidden_back(ins, outs):
    du0, du1, dy2, yh, inv, small, w = ins
    dy1, da, sums = outs
    dus = (du0, du1)
    for part in range(4):
        rel, half = divmod(part, 2)
        before = dy2 if part == 0 else dy1
        dy1[...] = before[...] + dot_t(dus[rel][half], w[part])
    g1 = small[4:5, :]
    totals = [jnp.zeros((1, D), F32)] * 3
    for r in range(2):
        rows = pl.ds(r * HALF, HALF)
        dh = dy1[rows, :]
        hat = yh[rows, :]
        grad = norm_back(dh, hat, inv[rows, :], g1)
        dy1[rows, :] = grad
        da[rows, :] = grad.astype(BF)
        totals = [a + row_sum(b) for a, b in zip(totals, (grad, dh * hat, dh))]
    for i in range(3):
        sums[i : i + 1, :] = totals[i]


class AttnBack:
    SCRATCH = [
        pltpu.VMEM((D, D), BF),
        pltpu.VMEM((6, SEQ, SEQ), BF),
        pltpu.SemaphoreType.DMA((6,)),
        pltpu.SemaphoreType.DMA((5,)),
        pltpu.VMEM((3, 128, SEQ), BF),
        pltpu.VMEM((3, 128, SEQ), BF),
    ] + [pltpu.VMEM(*h) for h in HEADS]

    def __init__(self, rel, raw, scratch):
        *head_in, w_in, self.p_in = raw
        self.w, self.p_buf, self.p_sems, sems, self.do_t, self.k_t, *self.heads = scratch
        self.copies = [pltpu.make_async_copy(w_in.at[rel * 2 + 1], self.w, sems.at[4])]
        self.copies += [
            pltpu.make_async_copy(a, b, sems.at[i])
            for i, (a, b) in enumerate(zip(head_in, self.heads))
        ]

    def start(self):
        for c in self.copies:
            c.start()
        for i in range(6):
            pltpu.make_async_copy(self.p_in.at[i], self.p_buf.at[i], self.p_sems.at[i]).start()

    def run(self, da, dq, dk, dv, sums):
        w, do_t_ref, k_t_ref = self.w, self.do_t, self.k_t
        k_ref, v_ref, qt_ref, ot_ref = self.heads
        for c in self.copies:
            c.wait()
        do = dot(da[...], w[:, 384:]).astype(BF)
        for i in range(3):
            do_t_ref[i] = do[:, i * 128 : (i + 1) * 128].T
            k_t_ref[i] = k_ref[i].T
        lane = lax.broadcasted_iota(jnp.int32, (SEQ, 128), 1)

        def pair(i, carry):
            vp = v_ref[i]
            do_t = do_t_ref[i]
            base = pl.multiple_of(i * 128, 128)
            both = do_t.astype(F32) * ot_ref[pl.ds(base, 128), :].astype(F32)
            for hh in range(2):
                own = (lane < HD) if hh == 0 else (lane >= HD)
                inside = slice(hh * HD, (hh + 1) * HD)
                delta = row_sum(both[inside])
                slope = dot(jnp.where(own, vp, jnp.zeros_like(vp)), do_t)
                head = 2 * i + hh
                pltpu.make_async_copy(
                    self.p_in.at[head], self.p_buf.at[head], self.p_sems.at[head]
                ).wait()
                prob = self.p_buf[head]
                ds = (prob.astype(F32) * (slope - delta)).astype(BF)
                lines = pl.ds(base + hh * HD, HD)
                dv[lines, :] = dot_t(do_t[inside], prob).astype(BF)
                dk[lines, :] = dot_t(qt_ref[lines, :], ds).astype(BF)
                dq[lines, :] = (dot(k_t_ref[i, inside, :], ds) * (HD**-0.5)).astype(BF)
            return carry

        lax.fori_loop(0, 3, pair, 0)
        ones = jnp.ones((8, SEQ), BF)
        sums[0:8, :] = dot_t(ones, dq[...])
        sums[8:16, :] = dot_t(ones, dv[...])


def frames_back_body(meta, raw, ins, outs, _, total, w, dy1, sem):
    grads = ins
    copies = [pltpu.make_async_copy(raw[0].at[i], w.at[i], sem.at[i]) for i in range(4)]
    copies.append(pltpu.make_async_copy(raw[1], dy1, sem.at[4]))
    for c in copies:
        c.start()
    for c in copies:
        c.wait()
    for m in range(3):
        rows = pl.ds(m * 256, 256)
        acc = None
        for rel in range(2):
            for side, left in enumerate(
                (w[rel * 2, rows, :384], w[rel * 2, rows, 384:], w[rel * 2 + 1, rows, :384])
            ):
                term = dot(left, grads[rel][side])
                acc = term if acc is None else acc + term
        total[rows, :] = acc
    for r in range(2):
        rows = pl.ds(r * HALF, HALF)
        outs[r][...] = dy1[rows, :] + total[:, r * HALF : (r + 1) * HALF].T


def frames_back(meta, dy1, turned, w):
    return kernel_call(
        frames_back_body,
        "frames_back",
        meta,
        [w, dy1],
        turned,
        [((HALF, D), F32)] * 2,
        [],
        [
            pltpu.VMEM((D, SEQ), F32),
            pltpu.VMEM(W_SHAPE, BF),
            pltpu.VMEM((SEQ, D), F32),
            pltpu.SemaphoreType.DMA((5,)),
        ],
        3.5,
    )


def put_out(meta, acc, outs, half):
    d = meta[0]
    for sel in range(2):
        for j in range(8):
            row = pl.multiple_of((d ^ MASKS[half][sel][j]) * ROWS, 16)
            outs[half * 2 + sel][j] = acc[half, pl.ds(row, ROWS), :]


GRAD_OUTS = [((8, ROWS, D), BF)] * 4
GRAD_SCRATCH = [pltpu.VMEM((2, D, D), BF)]


def ffn_grad(meta, left_o, left_r, right_o, right_r, outs, acc):
    for half in range(2):
        for i in range(2):
            total = dot(left_o[i], right_o[half]) + dot(left_r[i], right_r[half])
            acc[half, i * 384 : (i + 1) * 384, :] = total.astype(BF)
        put_out(meta, acc, outs, half)


def down_grad_body(meta, _, ins, outs, __, acc):
    dz_o, dz_r, f_o, f_r = ins
    ffn_grad(meta, dz_o, dz_r, f_o, f_r, outs, acc)


def down_grad_call(meta, *ins):
    return kernel_call(
        down_grad_body, "down_grad", meta, [], ins, GRAD_OUTS, [], GRAD_SCRATCH, 4.0
    )


def middle_body(meta, raw, ins, outs, raw_outs, acc, grads, dy1, da, out_sems, *scratch):
    attn = AttnBack(1, raw, scratch)
    attn.start()
    shared, shared_r, du0, du_r, *rest = ins
    sums_one, sent, qv = outs
    copies = [
        pltpu.make_async_copy(a, b, out_sems.at[i])
        for i, (a, b) in enumerate(zip([*[grads.at[i] for i in range(4)], dy1, da], raw_outs))
    ]
    ffn_grad(
        meta,
        shared.at[pl.ds(1, 2)],
        shared_r.at[pl.ds(1, 2)],
        du0,
        du_r,
        [grads.at[i] for i in range(4)],
        acc,
    )
    for c in copies[:4]:
        c.start()
    hidden_back([du0, *rest], (dy1, da, sums_one))
    for c in copies[4:]:
        c.start()
    for i in range(2):
        sent[3 + i] = da[:, i * 384 : (i + 1) * 384].T
    attn.run(da, sent.at[0], sent.at[1], sent.at[2], qv)
    for c in copies:
        c.wait()


def middle(meta, heads, w_attn, prob, shared, shared_r, du0, du_r, du1, dy2, yh, inv, s12, w):
    return kernel_call(
        middle_body,
        "up_grad_hidden_back_attn_back",
        meta,
        [*heads, w_attn, prob],
        [shared, shared_r, du0, du_r, du1, dy2, yh, inv, s12, w],
        [((8, D), F32), ((5, 384, SEQ), BF), ((16, 384), F32)],
        GRAD_OUTS + [((SEQ, D), F32), ((SEQ, D), BF)],
        GRAD_SCRATCH
        + [
            pltpu.VMEM((4, 8, ROWS, D), BF),
            pltpu.VMEM((SEQ, D), F32),
            pltpu.VMEM((SEQ, D), BF),
            pltpu.SemaphoreType.DMA((6,)),
        ]
        + AttnBack.SCRATCH,
        14.0,
    )


def attn_back_body(meta, raw, ins, outs, _, da, da_sem, *scratch):
    da_copy = pltpu.make_async_copy(raw[0], da, da_sem.at[0])
    da_copy.start()
    attn = AttnBack(0, raw[1:], scratch)
    attn.start()
    turned, qv = outs
    da_copy.wait()
    attn.run(da, turned.at[0], turned.at[1], turned.at[2], qv)


def attn_back(meta, heads, w_attn, prob, da):
    return kernel_call(
        attn_back_body,
        "attn_back",
        meta,
        [da, *heads, w_attn, prob],
        [],
        [((3, 384, SEQ), BF), ((16, 384), F32)],
        [],
        [pltpu.VMEM((SEQ, D), BF), pltpu.SemaphoreType.DMA((1,))] + AttnBack.SCRATCH,
        7.0,
    )


def attn_grad_body(meta, _, ins, outs, __, acc, x_t):
    xo, xr, zo, zr, turned, sent, sent_r, o_own, shared_r = ins
    for i, v in enumerate((xo, xr, zo, zr)):
        x_t[:, i * HALF : (i + 1) * HALF] = v[...].T
    for half, side, k in ((1, 0, 2), (0, 0, 0), (0, 1, 1)):
        for m in range(3):
            rows = pl.ds(m * 256, 256)
            total = dot_t(x_t[rows, :SEQ], turned[k]) + dot_t(x_t[rows, SEQ:], sent_r[k])
            acc[half, rows, side * 384 : (side + 1) * 384] = total.astype(BF)
    for i in range(2):
        total = dot_t(sent[3 + i], o_own[...]) + dot_t(sent_r[3 + i], shared_r[0])
        acc[1, i * 384 : (i + 1) * 384, 384:] = total.astype(BF)
    for half in range(2):
        put_out(meta, acc, outs, half)


def attn_grad(meta, xs, turned, sent, sent_r, o_own, shared_r):
    return kernel_call(
        attn_grad_body,
        "attn_grad",
        meta,
        [],
        [*xs, turned, sent, sent_r, o_own, shared_r],
        GRAD_OUTS,
        [],
        GRAD_SCRATCH + [pltpu.VMEM((D, 2 * SEQ), BF)],
        5.0,
    )


def adamw(weight, moment_one, moment_two, grad, rate, decay):
    new_one = BETA_ONE * moment_one + (1.0 - BETA_ONE) * grad
    new_two = BETA_TWO * moment_two + (1.0 - BETA_TWO) * grad * grad
    fixed_one = new_one / (1.0 - BETA_ONE**STEP)
    fixed_two = new_two / (1.0 - BETA_TWO**STEP)
    update = fixed_one / (jnp.sqrt(fixed_two) + ADAM_EPS) + decay * weight
    return (weight - rate * update, new_one, new_two)


def after(v, *deps):
    return lax.optimization_barrier((v, *deps))[0]


def other_core(v):
    return lax.ppermute(v, "tensor", [(0, 1), (1, 0)])


def shift(v, mask, n):
    return lax.ppermute(v, "dp", [(i, i ^ mask) for i in range(n)])


class Gather:
    def __init__(self, shard, n):
        self.n, self.shard, self.mark = n, shard, shard

    def z_all(self, *deps):
        if self.n == BLOCKS:
            shard = after(self.shard, *deps)
            self.z = [shard] + [shift(shard, z, self.n) for z in Z_MASKS[1:]]
            self.mark = shard

    def z_wait(self, *deps):
        if self.n == BLOCKS:
            self.z = after(tuple(self.z), *deps)
            self.mark = self.z[1:]

    def far_wait(self, *deps):
        if self.n == BLOCKS:
            self.far_side = after(tuple(self.far_side), *deps)
            self.mark = tuple(self.far_side)

    def near_wait(self, *deps):
        if self.n == BLOCKS:
            self.came = after(tuple(self.came), *deps)
            self.mark = tuple(self.came)

    def near(self, *deps):
        if self.n != BLOCKS:
            return
        parts = after(tuple(self.z), *deps)
        self.own = [
            jnp.stack([v[:, half * D : (half + 1) * D] for v in parts]) for half in range(2)
        ]
        self.mark = tuple(self.own)
        self.came = [shift(s, step[0], self.n) for s, step in zip(self.own, (STEP_A, STEP_B))]

    def far(self, *deps):
        if self.n != BLOCKS:
            return
        came = after(tuple(self.came), *deps)
        self.own = [jnp.concatenate([s, c]) for s, c in zip(self.own, came)]
        self.mark = tuple(self.own)
        self.far_side = [shift(o, step[1], self.n) for o, step in zip(self.own, (STEP_A, STEP_B))]

    def core(self, *deps):
        if self.n == BLOCKS:
            self.own_other = [other_core(o) for o in after(tuple(self.own), *deps)]
            self.mark = tuple(self.own_other)

    def pieces(self, *deps):
        if self.n == BLOCKS:
            far = after(tuple(self.far_side), *deps)
            result = []
            for half in range(2):
                far_other = other_core(far[half])
                result += [self.own[half], far[half], self.own_other[half], far_other]
            self.mark = far[1]
            return result
        full = lax.all_gather(self.shard, "dp", axis=0, tiled=True)
        blocks = full.reshape(BLOCKS, ROWS, 2 * D)
        result = []
        for half in range(2):
            cols = slice(half * D, (half + 1) * D)
            own = [blocks[jnp.array(m), :, cols] for m in MASKS[half]]
            result += own + [other_core(v) for v in own]
        return result


def added(*parts):
    total = parts[0].astype(F32)
    for p in parts[1:]:
        total = total + p.astype(F32)
    return total


class Scatter:
    def __init__(self, pieces, n):
        self.n, self.pieces, self.mark = n, pieces, pieces[0]
        if n == BLOCKS:
            self.keep = [pieces[0], pieces[2]]
            self.came = [
                shift(v, step[1], n) for v, step in zip((pieces[1], pieces[3]), (STEP_A, STEP_B))
            ]

    def near(self, *deps):
        if self.n != BLOCKS:
            return
        came = after(tuple(self.came), *deps)
        send = [added(k[4:], c[4:]).astype(BF) for k, c in zip(self.keep, came)]
        self.keep = [added(k[:4], c[:4]).astype(BF) for k, c in zip(self.keep, came)]
        self.came = [shift(s, step[0], self.n) for s, step in zip(send, (STEP_A, STEP_B))]
        self.mark = tuple(send)

    def wait(self, *deps):
        if self.n == BLOCKS:
            self.came = after(tuple(self.came), *deps)
            self.mark = tuple(self.came)

    def rows(self, *deps):
        came = after(tuple(self.came), *deps)
        return [
            jnp.concatenate([added(k[i], c[i]) for k, c in zip(self.keep, came)], 1)
            for i in range(4)
        ]

    def z_all(self, *deps):
        if self.n != BLOCKS:
            return
        self.row, *rest = self.rows(*deps)
        sends = [r.astype(BF) for r in rest]
        self.mark = tuple(sends)
        self.came = [shift(s, z, self.n) for s, z in zip(sends, Z_MASKS[1:])]

    def z_two(self, *deps):
        if self.n != BLOCKS:
            return
        rows = self.rows(*deps)
        self.row = jnp.stack(rows[:2])
        self.mark = jnp.stack(rows[2:]).astype(BF)
        self.came = [shift(self.mark, Z_MASKS[2], self.n)]

    def z_one(self, *deps):
        if self.n != BLOCKS:
            return
        (came,) = after(tuple(self.came), *deps)
        self.row, send = added(self.row[0], came[0]), added(self.row[1], came[1]).astype(BF)
        self.mark = send
        self.came = [shift(send, Z_MASKS[1], self.n)]

    def total(self, *deps):
        if self.n == BLOCKS:
            return added(self.row, *after(tuple(self.came), *deps))
        result = []
        for half in range(2):
            order = MASKS[half][0] + MASKS[half][1]
            back = [order.index(i) for i in range(BLOCKS)]
            full = jnp.concatenate(self.pieces[2 * half : 2 * half + 2])[jnp.array(back)]
            full = full.reshape(D, D).astype(F32)
            result.append(lax.psum_scatter(full, "dp", scatter_dimension=0, tiled=True))
        return jnp.concatenate(result, 1)


class Everywhere:
    def __init__(self, v, n):
        self.n, self.v = n, v

    def core(self, *deps):
        if self.n == BLOCKS:
            v = after(self.v, *deps)
            self.v = v + other_core(v)

    def step(self, masks, *deps):
        if self.n == BLOCKS:
            v = after(self.v, *deps)
            came = [shift(v, m, self.n) for m in masks]
            self.v = v + came[0] if len(came) == 1 else (v + came[0]) + (came[1] + came[2])

    def total(self):
        return self.v if self.n == BLOCKS else lax.psum(self.v, ("dp", "tensor"))


XY_MASKS = (1, 2, 3)


def per_device(
    frames,
    cotangent,
    lengths,
    attn_w,
    attn_m,
    attn_v,
    ffn_w,
    ffn_m,
    ffn_v,
    small_w,
    small_m,
    small_v,
):
    n = lax.axis_size("dp")
    t = lax.axis_index("tensor")
    d = lax.axis_index("dp") if n == BLOCKS else 0
    length = lax.dynamic_index_in_dim(lengths[:, 0], t, 0, keepdims=False)
    meta = jnp.stack([jnp.asarray(d, jnp.int32), jnp.asarray(t, jnp.int32), length])
    s12 = small_w.reshape(12, D)

    def pick(v, i):
        return lax.dynamic_index_in_dim(v[:, 0], i, 0, keepdims=False)

    def joined(own, other):
        return jnp.where(t == 0, jnp.stack([own, other]), jnp.stack([other, own]))[:, None]

    attn = Gather(jnp.concatenate([attn_w[i] for i in range(4)], 1).astype(BF), n)
    up = Gather(ffn_w[0].astype(BF), n)
    down = Gather(ffn_w[1].astype(BF), n)
    attn.z_all()
    frames_r = other_core(frames)
    xo, zr = pick(frames, t), pick(frames, 1 - t)
    xr, zo = pick(frames_r, t), pick(frames_r, 1 - t)
    cotangent_r = other_core(cotangent)
    co, cr = pick(cotangent, t), pick(cotangent_r, t)
    attn.near(xr, cr)
    up.z_all(attn.mark)
    attn.far()
    up.near(attn.mark)
    attn.core()
    attn_pieces = attn.pieces(up.mark)
    down.z_all(attn.mark)
    up.far(attn.mark)
    attn_out = attn_fwd(after(meta, up.mark, down.mark), xo, xr, attn_pieces, s12)
    yh, inv, hb, shared = attn_out[:4]
    heads = (attn_out[4:8], attn_out[8:12])
    prob, w_attn = attn_out[12:14], attn_out[14]
    down.near(inv)
    up.far_wait(inv)
    up.core(down.mark)
    up_pieces = up.pieces()
    down.far()
    down_far = down.mark
    f0, f1, gp, w_up = ffn_up(after(meta, down_far), hb, up_pieces, s12)
    down.far_wait(gp)
    down.core(down.mark)
    down_pieces = down.pieces()
    f_r = other_core(after(f1, down.mark))
    shared_r = other_core(after(shared, down.mark))
    out_o, out_r, dz, dz_t, dy2, sums_two, w_down = ffn_down(
        meta, f0, f1, down_pieces, yh, co, cr, s12
    )
    dz_r = other_core(dz_t)
    out_other = other_core(after(out_r, dz_t))
    du0, du1, db1 = ffn_back(meta, dz, w_down, gp)
    du_r = other_core(after(du1, dz_r))
    down_sum = Scatter(
        down_grad_call(after(meta, db1, out_other, f_r, shared_r), dz_t, dz_r, f0, f_r), n
    )
    *up_grad, dy1, da = middle(
        after(meta, down_sum.mark),
        heads[1],
        w_attn,
        prob[1],
        shared,
        shared_r,
        du0,
        du_r,
        du1,
        dy2,
        yh,
        inv,
        s12,
        w_up,
    )
    sums_one, sent, qv1, *up_grad = up_grad
    down_sum.wait(qv1)
    up_sum = Scatter(after(tuple(up_grad), down_sum.mark), n)
    down_sum.near()
    sent_r = other_core(after(sent, down_sum.mark))
    turned0, qv0 = attn_back(after(meta, down_sum.mark), heads[0], w_attn, prob[0], da)
    down_sum.z_all(qv0, sent_r)
    attn_grads = attn_grad(
        after(meta, down_sum.mark),
        (xo, xr, zo, zr),
        turned0,
        sent,
        sent_r,
        heads[0][3],
        shared_r,
    )
    down_sum.wait(attn_grads[0])
    up_sum.wait(attn_grads[0])
    up_sum.near()
    up_sum.wait(down_sum.mark)
    attn_sum = Scatter(after(tuple(attn_grads), up_sum.mark, down_sum.mark), n)
    up_sum.z_all()
    output = joined(out_o, after(out_other, qv0))
    half = SEQ // lax.axis_size("tensor")
    count_part = jnp.sum(jnp.clip(lengths - t * half, 0, half)).astype(F32)
    qv = jnp.where(
        t == 0,
        jnp.stack([qv0[0], qv1[0], qv0[8], qv1[8]]),
        jnp.stack([qv1[0], qv0[0], qv1[8], qv0[8]]),
    )
    vector = jnp.concatenate(
        [
            qv.reshape(-1),
            sums_one[0],
            sums_two[0],
            sums_one[1],
            sums_one[2],
            sums_two[1],
            sums_two[2],
            db1.reshape(-1),
        ]
    )
    dx_o, dx_r = frames_back(
        after(meta, up_sum.mark, output, vector, count_part), dy1, (turned0, sent), w_attn
    )
    up_sum.wait(dx_o)
    attn_sum.near(dx_o, up_sum.mark)
    down_g = down_sum.total(attn_sum.mark)
    up_g = up_sum.total(attn_sum.mark)
    dx_other = other_core(after(dx_r, attn_sum.mark))
    attn_sum.z_all(up_g, down_g, dx_other)
    frames_grad = joined(dx_o, dx_other)
    attn_g = attn_sum.total(frames_grad)
    square_part = sum(jnp.sum(g * g) for g in (attn_g, up_g, down_g))
    extra = jnp.stack([square_part, count_part])
    every = Everywhere(jnp.concatenate([vector, extra, jnp.zeros((126,), F32)]), n)
    every.core()
    every.step(XY_MASKS)
    every.step(Z_MASKS[1:])
    small_all = every.total()
    small_sum, square_sum, frame_count = small_all[:SMALL], small_all[SMALL], small_all[SMALL + 1]
    grad_norm = jnp.sqrt(square_sum + jnp.sum(small_sum * small_sum)) / frame_count
    factor = jnp.minimum(1.0, CLIP_NORM / grad_norm) / frame_count
    attn_rates = RATE * jnp.array([1.0, 1.0, 1.0, 0.5 * SEQ**0.5], F32)[:, None, None]
    attn_parts = jnp.stack([attn_g[:, i * 384 : (i + 1) * 384] for i in range(4)])
    attn_new, attn_m_new, attn_v_new = adamw(
        attn_w, attn_m, attn_v, attn_parts * factor, attn_rates, DECAY
    )
    ffn_new, ffn_m_new, ffn_v_new = adamw(
        ffn_w, ffn_m, ffn_v, jnp.stack([up_g, down_g]) * factor, RATE, DECAY
    )
    small_new, small_m_new, small_v_new = adamw(
        small_w, small_m, small_v, small_sum * factor, SMALL_RATE, 0.0
    )
    return (
        output,
        frames_grad,
        grad_norm,
        attn_new,
        attn_m_new,
        attn_v_new,
        ffn_new,
        ffn_m_new,
        ffn_v_new,
        small_new,
        small_m_new,
        small_v_new,
    )


def solution(mesh):
    rows = P(None, "dp", "tensor", None)
    weights = P(None, "dp", "tensor")
    in_specs = (rows, rows, P(None, "dp")) + (weights,) * 6 + (P(),) * 3
    out_specs = (rows, rows, P()) + (weights,) * 6 + (P(),) * 3
    return jax.shard_map(
        per_device, mesh=mesh, in_specs=in_specs, out_specs=out_specs, check_vma=False
    )
```

```python
import math

import jax
import jax.numpy as jnp
from jax import lax
from jax.experimental import pallas as pl
from jax.experimental.pallas import tpu as pltpu
from jax.sharding import PartitionSpec as P

HD = 64
D = 768
FF = 3072
SEQ = 512
HALF = SEQ // 2
STEP = 10
SMALL = 9216
PAIRS = 6
BLOCKS = 16
ROWS = D // BLOCKS

EPS_NORM = 1e-05
MASK_FILL = -1e30
BETA_ONE = 0.9
BETA_TWO = 0.999
ADAM_EPS = 1e-08
CLIP_NORM = 0.1
RATE = 0.1
SMALL_RATE = 1.5
DECAY = 0.01

BF = jnp.bfloat16
F32 = jnp.float32

STEP_A = (2, 1)
STEP_B = (1, 2)
Z_MASKS = (0, 4, 8, 12)
MASKS = tuple(
    (
        tuple(z for z in Z_MASKS) + tuple(z + near for z in Z_MASKS),
        tuple(z + far for z in Z_MASKS) + tuple(z + near + far for z in Z_MASKS),
    )
    for near, far in (STEP_A, STEP_B)
)


def dot(left, right):
    return jnp.dot(left, right, preferred_element_type=F32)


def dot_t(left, right):
    return lax.dot_general(left, right, (((1,), (1,)), ((), ())), preferred_element_type=F32)


def gelu_pair(u):
    phi = 0.5 * lax.erf(u * math.sqrt(0.5)) + 0.5
    return u * phi, phi + u * jnp.exp(-0.5 * u * u) * (1.0 / math.sqrt(2.0 * math.pi))


HBM = pl.BlockSpec(memory_space=pltpu.HBM)
SMEM = pl.BlockSpec(memory_space=pltpu.SMEM)


VMEM = pl.BlockSpec(memory_space=pltpu.VMEM)


def kernel_call(body, name, meta, raw, ins, outs, raw_outs, scratch, micros):
    n_raw, n_in, n_out, n_raw_out = len(raw), len(ins), len(outs), len(raw_outs)

    def run(meta_ref, *refs):
        cuts = [0, n_raw, n_in, n_out, n_raw_out]
        for i in range(1, 5):
            cuts[i] += cuts[i - 1]
        groups = [refs[cuts[i] : cuts[i + 1]] for i in range(4)]
        body(meta_ref, *groups, *refs[cuts[4] :])

    held = sum(
        math.prod(v.shape) * (2 if v.dtype == BF else 4) for v in scratch if v.dtype in (BF, F32)
    )
    return pl.pallas_call(
        run,
        name=name,
        in_specs=[SMEM] + [HBM] * n_raw + [VMEM] * n_in,
        out_specs=[VMEM] * n_out + [HBM] * n_raw_out,
        out_shape=[jax.ShapeDtypeStruct(s, d) for s, d in outs]
        + [pltpu.HBM(s, d) for s, d in raw_outs],
        scratch_shapes=scratch,
        compiler_params=pltpu.CompilerParams(vmem_limit_bytes=held + SPARE),
        cost_estimate=pl.CostEstimate(
            flops=int(micros * 1.15e9), bytes_accessed=0, transcendentals=0
        ),
    )(meta, *[pltpu.with_memory_space_constraint(v, pltpu.HBM) for v in raw], *ins)


SPARE = 8 * 2**20
W_SHAPE = (4, D, D)


def place(meta, pieces, w):
    d = meta[0]
    for part in range(4):
        rel, half = divmod(part, 2)
        for sel in range(2):
            src = pieces[half * 4 + rel * 2 + sel]
            for j in range(8):
                row = pl.multiple_of((d ^ MASKS[half][sel][j]) * ROWS, 16)
                w[part, pl.ds(row, ROWS), :] = src[j]


def chunk(c):
    return pl.ds(pl.multiple_of(c * CHUNK, CHUNK), CHUNK)


CHUNK = 256
PER_PART = D // CHUNK


def row_sum(v):
    return jnp.sum(v, 0, keepdims=True)


def attn_fwd_body(meta, _, ins, outs, raw_outs, q_ref, o_ref, w, p_buf, p_sems, w_sem, sems, *head_refs):
    xo, xr, s12, *pieces = ins
    yh, rs, hb, shared = outs
    place(meta, pieces, w)
    w_copy = pltpu.make_async_copy(w, raw_outs[10], w_sem.at[0])
    w_copy.start()
    head_copies = [
        pltpu.make_async_copy(head_refs[i], raw_outs[i], sems.at[i]) for i in range(8)
    ]
    t, length = meta[1], meta[2]
    row = lax.broadcasted_iota(jnp.int32, (SEQ, 1), 0)
    position = jnp.where(row < HALF, row + t * HALF, row + (1 - t) * HALF - HALF)
    valid = position < length
    lane = lax.broadcasted_iota(jnp.int32, (SEQ, 128), 1)
    for rel in range(2):
        k_ref, v_ref, qt_ref, ot_ref = head_refs[rel * 4 : rel * 4 + 4]
        p_out = raw_outs[8 + rel]
        cols = pl.ds(pl.multiple_of((t ^ rel) * 384, 128), 384)
        bq = s12[0:1, cols]
        bv = s12[1:2, cols]
        for r, x in ((0, xo), (1, xr)):
            rows = pl.ds(r * HALF, HALF)
            qk = dot(x[...], w[rel * 2])
            q = (qk[:, :384] + bq).astype(BF) * jnp.asarray(HD**-0.5, BF)
            k = qk[:, 384:].astype(BF)
            v = (dot(x[...], w[rel * 2 + 1, :, :384]) + bv).astype(BF)
            for i in range(3):
                part = slice(i * 128, (i + 1) * 128)
                q_ref[i, rows, :] = q[:, part]
                k_ref[i, rows, :] = k[:, part]
                v_ref[i, rows, :] = v[:, part]

        def pair(i, carry, rel=rel, k_ref=k_ref, v_ref=v_ref, qt_ref=qt_ref, ot_ref=ot_ref, p_out=p_out):
            keys = k_ref[i]
            q_t = q_ref[i].T
            lines = pl.ds(pl.multiple_of(i * 128, 128), 128)
            qt_ref[lines, :] = q_t
            v_t = v_ref[i].T
            halves = []
            for hh in range(2):
                own = (lane < HD) if hh == 0 else (lane >= HD)
                s = dot(jnp.where(own, keys, jnp.zeros_like(keys)), q_t)
                s = jnp.where(valid, s, MASK_FILL)
                e = jnp.exp(s - jnp.max(s, 0, keepdims=True))
                prob = (e * (1.0 / jnp.sum(e, 0, keepdims=True))).astype(BF)
                head = 2 * i + hh
                slot = rel * 6 + head
                p_buf[slot] = prob
                pltpu.make_async_copy(p_buf.at[slot], p_out.at[head], p_sems.at[slot]).start()
                halves.append(dot(v_t[hh * HD : (hh + 1) * HD], prob))
            o_t = jnp.concatenate(halves, 0).astype(BF)
            ot_ref[lines, :] = o_t
            o_ref[rel, :, lines] = o_t.T
            return carry

        lax.fori_loop(0, 3, pair, 0)
        for c in head_copies[rel * 4 : rel * 4 + 4]:
            c.start()
    bo, g1, c1 = s12[2:3, :], s12[4:5, :], s12[5:6, :]
    for r, x in ((0, xo), (1, xr)):
        rows = pl.ds(r * HALF, HALF)
        a = dot_t(o_ref[0, rows, :], w[1, :, 384:]) + dot_t(o_ref[1, rows, :], w[3, :, 384:])
        y = x[...].astype(F32) + a + bo
        centred = y - jnp.mean(y, -1, keepdims=True)
        inv = lax.rsqrt(jnp.mean(centred * centred, -1, keepdims=True) + EPS_NORM)
        hat = centred * inv
        yh[rows, :] = hat
        rs[rows, :] = inv
        hb[rows, :] = (hat * g1 + c1).astype(BF)
    shared[0] = head_refs[7][...]
    for i in range(2):
        shared[1 + i] = hb[:, i * 384 : (i + 1) * 384].T
    for i in range(12):
        pltpu.make_async_copy(
            p_buf.at[i], raw_outs[8 + i // 6].at[i % 6], p_sems.at[i]
        ).wait()
    w_copy.wait()
    for c in head_copies:
        c.wait()


TURNED = ((384, SEQ), BF)
HEADS = [((3, SEQ, 128), BF), ((3, SEQ, 128), BF), TURNED, TURNED]


def attn_fwd(meta, xo, xr, pieces, s12):
    return kernel_call(
        attn_fwd_body,
        "attn_fwd",
        meta,
        [],
        [xo, xr, s12, *pieces],
        [((SEQ, D), F32), ((SEQ, 1), F32), ((SEQ, D), BF), ((3, 384, SEQ), BF)],
        HEADS * 2 + [((6, SEQ, SEQ), BF)] * 2 + [(W_SHAPE, BF)],
        [
            pltpu.VMEM((3, SEQ, 128), BF),
            pltpu.VMEM((2, SEQ, 384), BF),
            pltpu.VMEM(W_SHAPE, BF),
            pltpu.VMEM((12, SEQ, SEQ), BF),
            pltpu.SemaphoreType.DMA((12,)),
            pltpu.SemaphoreType.DMA((1,)),
            pltpu.SemaphoreType.DMA((8,)),
        ]
        + [pltpu.VMEM(*h) for h in HEADS * 2],
        16.0,
    )


def ffn_up_body(meta, _, ins, outs, __):
    hb, s12, *pieces = ins
    f0, f1, gp, w = outs
    place(meta, pieces, w)
    for part in range(4):
        rel, half = divmod(part, 2)
        bias_row = pl.ds(8 + 2 * (meta[1] ^ rel) + half, 1)
        f_ref = (f0, f1)[rel]
        for c in range(PER_PART):
            cols = slice(c * CHUNK, (c + 1) * CHUNK)
            u = dot(hb[...], w[part, :, cols]) + s12[bias_row, cols]
            f, slope = gelu_pair(u)
            f_ref[half, :, cols] = f.astype(BF)
            gp[part, :, cols] = slope.astype(BF)


SIDE = ((2, SEQ, D), BF)
SLABS = ((2, 384, SEQ), BF)


def ffn_up(meta, hb, pieces, s12):
    return kernel_call(
        ffn_up_body,
        "ffn_up",
        meta,
        [],
        [hb, s12, *pieces],
        [SIDE, SIDE, ((4, SEQ, D), BF), (W_SHAPE, BF)],
        [],
        [],
        5.0,
    )


def norm_back(grad, hat, inv, gain):
    scaled = grad * gain
    return inv * (
        scaled
        - jnp.mean(scaled, -1, keepdims=True)
        - hat * jnp.mean(scaled * hat, -1, keepdims=True)
    )


def ffn_down_body(meta, _, ins, outs, __):
    f0, f1, yh, co, cr, s12, *pieces = ins
    out_o, out_r, dz, dz_t, dy2, sums, w = outs
    place(meta, pieces, w)
    t, length = meta[1], meta[2]
    b2 = s12[3:4, :]
    g1, c1, g2, c2 = s12[4:5, :], s12[5:6, :], s12[6:7, :], s12[7:8, :]
    fs = (f0, f1)
    for part in range(4):
        rel, half = divmod(part, 2)
        z = dot_t(fs[rel][half], w[part])
        dy2[...] = z if part == 0 else dy2[...] + z
    totals = [jnp.zeros((1, D), F32)] * 3
    for r, cot, out in ((0, co, out_o), (1, cr, out_r)):
        rows = pl.ds(r * HALF, HALF)
        y = yh[rows, :] * g1 + c1 + dy2[rows, :] + b2
        centred = y - jnp.mean(y, -1, keepdims=True)
        inv = lax.rsqrt(jnp.mean(centred * centred, -1, keepdims=True) + EPS_NORM)
        hat = centred * inv
        out[...] = (hat * g2 + c2).astype(BF)
        row = lax.broadcasted_iota(jnp.int32, (HALF, 1), 0)
        valid = row + (t ^ r) * HALF < length
        dout = jnp.where(valid, cot[...].astype(F32), 0.0)
        grad = norm_back(dout, hat, inv, g2)
        dy2[rows, :] = grad
        dz[rows, :] = grad.astype(BF)
        totals = [a + row_sum(b) for a, b in zip(totals, (grad, dout * hat, dout))]
    for i in range(3):
        sums[i : i + 1, :] = totals[i]
    for i in range(2):
        dz_t[i] = dz[:, i * 384 : (i + 1) * 384].T


def ffn_down(meta, f0, f1, pieces, yh, co, cr, s12):
    return kernel_call(
        ffn_down_body,
        "ffn_down",
        meta,
        [],
        [f0, f1, yh, co, cr, s12, *pieces],
        [
            ((HALF, D), BF),
            ((HALF, D), BF),
            ((SEQ, D), BF),
            SLABS,
            ((SEQ, D), F32),
            ((8, D), F32),
            (W_SHAPE, BF),
        ],
        [],
        [],
        5.0,
    )


def ffn_back_body(meta, _, ins, outs, __):
    dz, gp, w = ins
    du0, du1, db1 = outs
    for part in (2, 3, 0, 1):
        rel, half = divmod(part, 2)
        bias_row = pl.ds(2 * (meta[1] ^ rel) + half, 1)
        du_ref = (du0, du1)[rel]
        for c in range(PER_PART):
            cols = slice(c * CHUNK, (c + 1) * CHUNK)
            du = dot(dz[...], w[part, :, cols]) * gp[part, :, cols].astype(F32)
            db1[bias_row, cols] = row_sum(du)
            du_ref[half, :, cols] = du.astype(BF)


def ffn_back(meta, dz, w, gp):
    return kernel_call(
        ffn_back_body,
        "ffn_back",
        meta,
        [],
        [dz, gp, w],
        [SIDE, SIDE, ((4, D), F32)],
        [],
        [],
        3.5,
    )


def hidden_back(ins, outs):
    du0, du1, dy2, yh, inv, small, w = ins
    dy1, da, sums = outs
    dus = (du0, du1)
    for part in range(4):
        rel, half = divmod(part, 2)
        before = dy2 if part == 0 else dy1
        dy1[...] = before[...] + dot_t(dus[rel][half], w[part])
    g1 = small[4:5, :]
    totals = [jnp.zeros((1, D), F32)] * 3
    for r in range(2):
        rows = pl.ds(r * HALF, HALF)
        dh = dy1[rows, :]
        hat = yh[rows, :]
        grad = norm_back(dh, hat, inv[rows, :], g1)
        dy1[rows, :] = grad
        da[rows, :] = grad.astype(BF)
        totals = [a + row_sum(b) for a, b in zip(totals, (grad, dh * hat, dh))]
    for i in range(3):
        sums[i : i + 1, :] = totals[i]


class AttnBack:
    SCRATCH = [
        pltpu.VMEM((D, D), BF),
        pltpu.VMEM((6, SEQ, SEQ), BF),
        pltpu.SemaphoreType.DMA((6,)),
        pltpu.SemaphoreType.DMA((5,)),
        pltpu.VMEM((3, 128, SEQ), BF),
        pltpu.VMEM((3, 128, SEQ), BF),
    ] + [pltpu.VMEM(*h) for h in HEADS]

    def __init__(self, rel, raw, scratch):
        *head_in, w_in, self.p_in = raw
        self.w, self.p_buf, self.p_sems, sems, self.do_t, self.k_t, *self.heads = scratch
        self.copies = [pltpu.make_async_copy(w_in.at[rel * 2 + 1], self.w, sems.at[4])]
        self.copies += [
            pltpu.make_async_copy(a, b, sems.at[i])
            for i, (a, b) in enumerate(zip(head_in, self.heads))
        ]

    def start(self):
        for c in self.copies:
            c.start()
        for i in range(6):
            pltpu.make_async_copy(self.p_in.at[i], self.p_buf.at[i], self.p_sems.at[i]).start()

    def run(self, da, dq, dk, dv, sums):
        w, do_t_ref, k_t_ref = self.w, self.do_t, self.k_t
        k_ref, v_ref, qt_ref, ot_ref = self.heads
        for c in self.copies:
            c.wait()
        do = dot(da[...], w[:, 384:]).astype(BF)
        for i in range(3):
            do_t_ref[i] = do[:, i * 128 : (i + 1) * 128].T
            k_t_ref[i] = k_ref[i].T
        lane = lax.broadcasted_iota(jnp.int32, (SEQ, 128), 1)

        def pair(i, carry):
            vp = v_ref[i]
            do_t = do_t_ref[i]
            base = pl.multiple_of(i * 128, 128)
            both = do_t.astype(F32) * ot_ref[pl.ds(base, 128), :].astype(F32)
            for hh in range(2):
                own = (lane < HD) if hh == 0 else (lane >= HD)
                inside = slice(hh * HD, (hh + 1) * HD)
                delta = row_sum(both[inside])
                slope = dot(jnp.where(own, vp, jnp.zeros_like(vp)), do_t)
                head = 2 * i + hh
                pltpu.make_async_copy(
                    self.p_in.at[head], self.p_buf.at[head], self.p_sems.at[head]
                ).wait()
                prob = self.p_buf[head]
                ds = (prob.astype(F32) * (slope - delta)).astype(BF)
                lines = pl.ds(base + hh * HD, HD)
                dv[lines, :] = dot_t(do_t[inside], prob).astype(BF)
                dk[lines, :] = dot_t(qt_ref[lines, :], ds).astype(BF)
                dq[lines, :] = (dot(k_t_ref[i, inside, :], ds) * (HD**-0.5)).astype(BF)
            return carry

        lax.fori_loop(0, 3, pair, 0)
        ones = jnp.ones((8, SEQ), BF)
        sums[0:8, :] = dot_t(ones, dq[...])
        sums[8:16, :] = dot_t(ones, dv[...])


LINES = SMALL // 128


def put_lines(vec, first, row):
    for i in range(row.shape[1] // 128):
        vec[pl.ds(first + i, 1), :] = row[:, i * 128 : (i + 1) * 128]


def frames_back_body(meta, raw, ins, outs, _, total, w, dy1, sem):
    grads = ins
    copies = [pltpu.make_async_copy(raw[0].at[i], w.at[i], sem.at[i]) for i in range(4)]
    copies.append(pltpu.make_async_copy(raw[1], dy1, sem.at[4]))
    for c in copies:
        c.start()
    for c in copies:
        c.wait()
    for m in range(3):
        rows = pl.ds(m * 256, 256)
        acc = None
        for rel in range(2):
            for side, left in enumerate(
                (w[rel * 2, rows, :384], w[rel * 2, rows, 384:], w[rel * 2 + 1, rows, :384])
            ):
                term = dot(left, grads[rel][side])
                acc = term if acc is None else acc + term
        total[rows, :] = acc
    for r in range(2):
        rows = pl.ds(r * HALF, HALF)
        outs[r][...] = dy1[rows, :] + total[:, r * HALF : (r + 1) * HALF].T


def frames_back(meta, dy1, turned, w):
    return kernel_call(
        frames_back_body,
        "frames_back",
        meta,
        [w, dy1],
        turned,
        [((HALF, D), F32)] * 2,
        [],
        [
            pltpu.VMEM((D, SEQ), F32),
            pltpu.VMEM(W_SHAPE, BF),
            pltpu.VMEM((SEQ, D), F32),
            pltpu.SemaphoreType.DMA((5,)),
        ],
        3.5,
    )


def near_body(meta, _, ins, outs, __):
    for half in range(2):
        keep, came = ins[half], ins[2 + half]
        for i in range(4):
            outs[2 + half][i] = (keep[4 + i].astype(F32) + came[4 + i].astype(F32)).astype(BF)
            outs[half][i] = (keep[i].astype(F32) + came[i].astype(F32)).astype(BF)


def near_sums(meta, keep, came):
    outs = kernel_call(
        near_body, "near_sums", meta, [], [*keep, *came], [((4, ROWS, D), BF)] * 4, [], [], 0.5
    )
    return outs[:2], outs[2:]


def z_body(meta, _, ins, outs, __):
    for half in range(2):
        keep, came = ins[half], ins[2 + half]
        cols = slice(half * D, (half + 1) * D)
        for i in range(4):
            outs[i][:, cols] = (keep[i].astype(F32) + came[i].astype(F32)).astype(outs[i].dtype)


ROW = (ROWS, 2 * D)


def z_sums(meta, keep, came):
    return kernel_call(
        z_body, "z_sums", meta, [], [*keep, *came], [(ROW, F32)] + [(ROW, BF)] * 3, [], [], 0.5
    )


def totals_body(meta, _, ins, outs, __):
    count = ins[0]
    grads, vec = outs
    square = jnp.zeros((1, 1), F32)
    for k in range(3):
        row, *came = ins[1 + 4 * k : 5 + 4 * k]
        total = row[...]
        for c in came:
            total = total + c[...].astype(F32)
        grads[k] = total
        square = square + jnp.sum(row_sum(total * total), 1, keepdims=True)
    lane = lax.broadcasted_iota(jnp.int32, (8, 128), 1)
    vec[...] = jnp.where(lane == 0, square, jnp.where(lane == 1, count[...], 0.0))


def totals(meta, count, parts):
    return kernel_call(
        totals_body,
        "totals",
        meta,
        [],
        [count, *parts],
        [((3, *parts[0].shape), F32), ((8, 128), F32)],
        [],
        [],
        1.0,
    )


def adamw_body(meta, raw, ins, outs, raw_outs, *scratch):
    square, vec, grads, small_w, small_m, small_v, aw, am, av, fw, fm, fv = ins
    norm_out, small_out = outs[0], outs[1:]
    new_a, new_f, sems = scratch
    frame_count = square[0:1, 1:2]
    small = vec[...]
    squares = square[0:1, 0:1] + jnp.sum(row_sum(small * small), 1, keepdims=True)
    norm = jnp.sqrt(squares) / frame_count
    norm_out[...] = norm
    factor = jnp.minimum(1.0, CLIP_NORM / norm) / frame_count
    copies = []
    for i in range(4):
        cols = slice((i % 2) * 384 + (i // 2) * D, (i % 2) * 384 + (i // 2) * D + 384)
        rate = RATE * 0.5 * SEQ**0.5 if i == 3 else RATE
        for k, v in enumerate(adamw(aw[i], am[i], av[i], grads[0, :, cols] * factor, rate, DECAY)):
            new_a[k, i] = v
    for k in range(3):
        copies.append(pltpu.make_async_copy(new_a.at[k], raw_outs[k], sems.at[k]))
        copies[-1].start()
    for i in range(2):
        for k, v in enumerate(adamw(fw[i], fm[i], fv[i], grads[1 + i] * factor, RATE, DECAY)):
            new_f[k, i] = v
    for k in range(3):
        copies.append(pltpu.make_async_copy(new_f.at[k], raw_outs[3 + k], sems.at[3 + k]))
        copies[-1].start()
    new_small = adamw(small_w[...], small_m[...], small_v[...], small * factor, SMALL_RATE, 0.0)
    for out, v in zip(small_out, new_small):
        out[...] = v
    for c in copies:
        c.wait()


def adamw_call(meta, square, vec, grads, small, state):
    shapes = [v.shape for v in state]
    return kernel_call(
        adamw_body,
        "adamw",
        meta,
        [],
        [square, vec, grads, *small, *state],
        [((1, 1), F32)] + [((LINES, 128), F32)] * 3,
        [(s, F32) for s in shapes],
        [
            pltpu.VMEM((3, *shapes[0]), F32),
            pltpu.VMEM((3, *shapes[3]), F32),
            pltpu.SemaphoreType.DMA((6,)),
        ],
        3.0,
    )


def put_out(meta, acc, outs, half):
    d = meta[0]
    for sel in range(2):
        for j in range(8):
            row = pl.multiple_of((d ^ MASKS[half][sel][j]) * ROWS, 16)
            outs[half * 2 + sel][j] = acc[half, pl.ds(row, ROWS), :]


GRAD_OUTS = [((8, ROWS, D), BF)] * 4
GRAD_SCRATCH = [pltpu.VMEM((2, D, D), BF)]


def ffn_grad(meta, left_o, left_r, right_o, right_r, outs, acc):
    for half in range(2):
        for i in range(2):
            total = dot(left_o[i], right_o[half]) + dot(left_r[i], right_r[half])
            acc[half, i * 384 : (i + 1) * 384, :] = total.astype(BF)
        put_out(meta, acc, outs, half)


def down_grad_body(meta, _, ins, outs, __, acc):
    dz_o, dz_r, f_o, f_r = ins
    ffn_grad(meta, dz_o, dz_r, f_o, f_r, outs, acc)


def down_grad_call(meta, *ins):
    return kernel_call(
        down_grad_body, "down_grad", meta, [], ins, GRAD_OUTS, [], GRAD_SCRATCH, 4.0
    )


def middle_body(meta, raw, ins, outs, raw_outs, acc, grads, dy1, da, out_sems, *scratch):
    attn = AttnBack(1, raw, scratch)
    attn.start()
    shared, shared_r, du0, du_r, *rest = ins
    sums_one, sent, qv = outs
    copies = [
        pltpu.make_async_copy(a, b, out_sems.at[i])
        for i, (a, b) in enumerate(zip([*[grads.at[i] for i in range(4)], dy1, da], raw_outs))
    ]
    ffn_grad(
        meta,
        shared.at[pl.ds(1, 2)],
        shared_r.at[pl.ds(1, 2)],
        du0,
        du_r,
        [grads.at[i] for i in range(4)],
        acc,
    )
    for c in copies[:4]:
        c.start()
    hidden_back([du0, *rest], (dy1, da, sums_one))
    for c in copies[4:]:
        c.start()
    for i in range(2):
        sent[3 + i] = da[:, i * 384 : (i + 1) * 384].T
    attn.run(da, sent.at[0], sent.at[1], sent.at[2], qv)
    for c in copies:
        c.wait()


def middle(meta, heads, w_attn, prob, shared, shared_r, du0, du_r, du1, dy2, yh, inv, s12, w):
    return kernel_call(
        middle_body,
        "up_grad_hidden_back_attn_back",
        meta,
        [*heads, w_attn, prob],
        [shared, shared_r, du0, du_r, du1, dy2, yh, inv, s12, w],
        [((8, D), F32), ((5, 384, SEQ), BF), ((16, 384), F32)],
        GRAD_OUTS + [((SEQ, D), F32), ((SEQ, D), BF)],
        GRAD_SCRATCH
        + [
            pltpu.VMEM((4, 8, ROWS, D), BF),
            pltpu.VMEM((SEQ, D), F32),
            pltpu.VMEM((SEQ, D), BF),
            pltpu.SemaphoreType.DMA((6,)),
        ]
        + AttnBack.SCRATCH,
        14.0,
    )


def attn_back_body(meta, raw, ins, outs, _, da, da_sem, *scratch):
    da_copy = pltpu.make_async_copy(raw[0], da, da_sem.at[0])
    da_copy.start()
    attn = AttnBack(0, raw[1:], scratch)
    attn.start()
    turned, qv = outs
    da_copy.wait()
    attn.run(da, turned.at[0], turned.at[1], turned.at[2], qv)


def attn_back(meta, heads, w_attn, prob, da):
    return kernel_call(
        attn_back_body,
        "attn_back",
        meta,
        [da, *heads, w_attn, prob],
        [],
        [((3, 384, SEQ), BF), ((16, 384), F32)],
        [],
        [pltpu.VMEM((SEQ, D), BF), pltpu.SemaphoreType.DMA((1,))] + AttnBack.SCRATCH,
        7.0,
    )


def attn_grad_body(meta, _, ins, outs, __, acc, x_t):
    xo, xr, zo, zr, turned, sent, sent_r, o_own, shared_r = ins[:9]
    qv0, qv1, sums_one, sums_two, db1 = ins[9:]
    vec = outs[4]
    for rel, qv in ((0, qv0), (1, qv1)):
        h = meta[1] ^ rel
        put_lines(vec, 3 * h, qv[0:1, :])
        put_lines(vec, 6 + 3 * h, qv[8:9, :])
    for line, sums, row in (
        (2, sums_one, 0),
        (3, sums_two, 0),
        (4, sums_one, 1),
        (5, sums_one, 2),
        (6, sums_two, 1),
        (7, sums_two, 2),
    ):
        put_lines(vec, 6 * line, sums[row : row + 1, :])
    for i in range(4):
        put_lines(vec, 48 + 6 * i, db1[i : i + 1, :])
    for i, v in enumerate((xo, xr, zo, zr)):
        x_t[:, i * HALF : (i + 1) * HALF] = v[...].T
    for half, side, k in ((1, 0, 2), (0, 0, 0), (0, 1, 1)):
        for m in range(3):
            rows = pl.ds(m * 256, 256)
            total = dot_t(x_t[rows, :SEQ], turned[k]) + dot_t(x_t[rows, SEQ:], sent_r[k])
            acc[half, rows, side * 384 : (side + 1) * 384] = total.astype(BF)
    for i in range(2):
        total = dot_t(sent[3 + i], o_own[...]) + dot_t(sent_r[3 + i], shared_r[0])
        acc[1, i * 384 : (i + 1) * 384, 384:] = total.astype(BF)
    for half in range(2):
        put_out(meta, acc, outs, half)


def attn_grad(meta, xs, turned, sent, sent_r, o_own, shared_r, small):
    return kernel_call(
        attn_grad_body,
        "attn_grad",
        meta,
        [],
        [*xs, turned, sent, sent_r, o_own, shared_r, *small],
        GRAD_OUTS + [((LINES, 128), F32)],
        [],
        GRAD_SCRATCH + [pltpu.VMEM((D, 2 * SEQ), BF)],
        5.0,
    )


def adamw(weight, moment_one, moment_two, grad, rate, decay):
    new_one = BETA_ONE * moment_one + (1.0 - BETA_ONE) * grad
    new_two = BETA_TWO * moment_two + (1.0 - BETA_TWO) * grad * grad
    fixed_one = new_one / (1.0 - BETA_ONE**STEP)
    fixed_two = new_two / (1.0 - BETA_TWO**STEP)
    update = fixed_one / (jnp.sqrt(fixed_two) + ADAM_EPS) + decay * weight
    return (weight - rate * update, new_one, new_two)


def after(v, *deps):
    return lax.optimization_barrier((v, *deps))[0]


def other_core(v):
    return lax.ppermute(v, "tensor", [(0, 1), (1, 0)])


def shift(v, mask, n):
    return lax.ppermute(v, "dp", [(i, i ^ mask) for i in range(n)])


class Gather:
    def __init__(self, shard, n):
        self.n, self.shard, self.mark = n, shard, shard

    def z_all(self, *deps):
        if self.n == BLOCKS:
            shard = after(self.shard, *deps)
            self.z = [shard] + [shift(shard, z, self.n) for z in Z_MASKS[1:]]
            self.mark = shard

    def z_wait(self, *deps):
        if self.n == BLOCKS:
            self.z = after(tuple(self.z), *deps)
            self.mark = self.z[1:]

    def far_wait(self, *deps):
        if self.n == BLOCKS:
            self.far_side = after(tuple(self.far_side), *deps)
            self.mark = tuple(self.far_side)

    def near_wait(self, *deps):
        if self.n == BLOCKS:
            self.came = after(tuple(self.came), *deps)
            self.mark = tuple(self.came)

    def near(self, *deps):
        if self.n != BLOCKS:
            return
        parts = after(tuple(self.z), *deps)
        self.own = [
            jnp.stack([v[:, half * D : (half + 1) * D] for v in parts]) for half in range(2)
        ]
        self.mark = tuple(self.own)
        self.came = [shift(s, step[0], self.n) for s, step in zip(self.own, (STEP_A, STEP_B))]

    def far(self, *deps):
        if self.n != BLOCKS:
            return
        came = after(tuple(self.came), *deps)
        self.own = [jnp.concatenate([s, c]) for s, c in zip(self.own, came)]
        self.mark = tuple(self.own)
        self.far_side = [shift(o, step[1], self.n) for o, step in zip(self.own, (STEP_A, STEP_B))]

    def core(self, *deps):
        if self.n == BLOCKS:
            self.own_other = [other_core(o) for o in after(tuple(self.own), *deps)]
            self.mark = tuple(self.own_other)

    def pieces(self, *deps):
        if self.n == BLOCKS:
            far = after(tuple(self.far_side), *deps)
            result = []
            for half in range(2):
                far_other = other_core(far[half])
                result += [self.own[half], far[half], self.own_other[half], far_other]
            self.mark = far[1]
            return result
        full = lax.all_gather(self.shard, "dp", axis=0, tiled=True)
        blocks = full.reshape(BLOCKS, ROWS, 2 * D)
        result = []
        for half in range(2):
            cols = slice(half * D, (half + 1) * D)
            own = [blocks[jnp.array(m), :, cols] for m in MASKS[half]]
            result += own + [other_core(v) for v in own]
        return result


def added(*parts):
    total = parts[0].astype(F32)
    for p in parts[1:]:
        total = total + p.astype(F32)
    return total


class Scatter:
    def __init__(self, meta, pieces, n):
        self.meta = meta
        self.n, self.pieces, self.mark = n, pieces, pieces[0]
        if n == BLOCKS:
            self.keep = [pieces[0], pieces[2]]
            self.came = [
                shift(v, step[1], n) for v, step in zip((pieces[1], pieces[3]), (STEP_A, STEP_B))
            ]

    def near(self, *deps):
        if self.n != BLOCKS:
            return
        came = after(tuple(self.came), *deps)
        self.keep, send = near_sums(self.meta, self.keep, came)
        self.came = [shift(s, step[0], self.n) for s, step in zip(send, (STEP_A, STEP_B))]
        self.mark = tuple(send)

    def wait(self, *deps):
        if self.n == BLOCKS:
            self.came = after(tuple(self.came), *deps)
            self.mark = tuple(self.came)

    def z_all(self, *deps):
        if self.n != BLOCKS:
            return
        came = after(tuple(self.came), *deps)
        self.row, *sends = z_sums(self.meta, self.keep, came)
        self.mark = tuple(sends)
        self.came = [shift(s, z, self.n) for s, z in zip(sends, Z_MASKS[1:])]

    def parts(self, *deps):
        if self.n == BLOCKS:
            return [self.row, *after(tuple(self.came), *deps)]
        whole = self.whole()
        zero = jnp.zeros(whole.shape, BF)
        return [whole, zero, zero, zero]

    def whole(self):
        result = []
        for half in range(2):
            order = MASKS[half][0] + MASKS[half][1]
            back = [order.index(i) for i in range(BLOCKS)]
            full = jnp.concatenate(self.pieces[2 * half : 2 * half + 2])[jnp.array(back)]
            full = full.reshape(D, D).astype(F32)
            result.append(lax.psum_scatter(full, "dp", scatter_dimension=0, tiled=True))
        return jnp.concatenate(result, 1)


class Everywhere:
    def __init__(self, v, n):
        self.n, self.v = n, v

    def core(self, *deps):
        if self.n == BLOCKS:
            v = after(self.v, *deps)
            self.v = v + other_core(v)

    def step(self, masks, *deps):
        if self.n == BLOCKS:
            v = after(self.v, *deps)
            came = [shift(v, m, self.n) for m in masks]
            self.v = v + came[0] if len(came) == 1 else (v + came[0]) + (came[1] + came[2])

    def total(self):
        return self.v if self.n == BLOCKS else lax.psum(self.v, ("dp", "tensor"))


XY_MASKS = (1, 2, 3)


def per_device(
    frames,
    cotangent,
    lengths,
    attn_w,
    attn_m,
    attn_v,
    ffn_w,
    ffn_m,
    ffn_v,
    small_w,
    small_m,
    small_v,
):
    n = lax.axis_size("dp")
    t = lax.axis_index("tensor")
    d = lax.axis_index("dp") if n == BLOCKS else 0
    length = lax.dynamic_index_in_dim(lengths[:, 0], t, 0, keepdims=False)
    meta = jnp.stack([jnp.asarray(d, jnp.int32), jnp.asarray(t, jnp.int32), length])
    s12 = small_w.reshape(12, D)
    half = SEQ // lax.axis_size("tensor")
    count = jnp.sum(jnp.clip(lengths - t * half, 0, half)).astype(F32).reshape(1, 1)

    def pick(v, i):
        return lax.dynamic_index_in_dim(v[:, 0], i, 0, keepdims=False)

    def joined(own, other):
        return jnp.where(t == 0, jnp.stack([own, other]), jnp.stack([other, own]))[:, None]

    attn = Gather(jnp.concatenate([attn_w[i] for i in range(4)], 1).astype(BF), n)
    up = Gather(ffn_w[0].astype(BF), n)
    down = Gather(ffn_w[1].astype(BF), n)
    attn.z_all()
    frames_r = other_core(frames)
    xo, zr = pick(frames, t), pick(frames, 1 - t)
    xr, zo = pick(frames_r, t), pick(frames_r, 1 - t)
    cotangent_r = other_core(cotangent)
    co, cr = pick(cotangent, t), pick(cotangent_r, t)
    attn.near(xr, cr)
    up.z_all(attn.mark)
    attn.far()
    up.near(attn.mark)
    attn.core()
    attn_pieces = attn.pieces(up.mark)
    down.z_all(attn.mark)
    up.far(attn.mark)
    attn_out = attn_fwd(after(meta, up.mark, down.mark, count), xo, xr, attn_pieces, s12)
    yh, inv, hb, shared = attn_out[:4]
    heads = (attn_out[4:8], attn_out[8:12])
    prob, w_attn = attn_out[12:14], attn_out[14]
    down.near(inv)
    up.far_wait(inv)
    up.core(down.mark)
    up_pieces = up.pieces()
    down.far()
    down_far = down.mark
    down.core(up_pieces[1], up_pieces[3])
    f0, f1, gp, w_up = ffn_up(after(meta, down_far), hb, up_pieces, s12)
    down.far_wait(gp)
    down_pieces = down.pieces()
    f_r = other_core(after(f1, *down_pieces))
    shared_r = other_core(after(shared, *down_pieces))
    out_o, out_r, dz, dz_t, dy2, sums_two, w_down = ffn_down(
        meta, f0, f1, down_pieces, yh, co, cr, s12
    )
    dz_r = other_core(after(dz_t, f_r, shared_r))
    du0, du1, db1 = ffn_back(after(meta, f_r, shared_r), dz, w_down, gp)
    du_r = other_core(after(du1, dz_r))
    down_sum = Scatter(
        meta,
        down_grad_call(after(meta, db1), dz_t, dz_r, f0, f_r), n
    )
    *up_grad, dy1, da = middle(
        after(meta, down_sum.mark),
        heads[1],
        w_attn,
        prob[1],
        shared,
        shared_r,
        du0,
        du_r,
        du1,
        dy2,
        yh,
        inv,
        s12,
        w_up,
    )
    sums_one, sent, qv1, *up_grad = up_grad
    down_sum.wait(qv1)
    up_sum = Scatter(meta, after(tuple(up_grad), down_sum.mark), n)
    down_sum.near()
    sent_r = other_core(after(sent, down_sum.mark))
    turned0, qv0 = attn_back(after(meta, down_sum.mark), heads[0], w_attn, prob[0], da)
    down_sum.z_all(qv0, sent_r)
    *attn_grads, vec = attn_grad(
        after(meta, down_sum.mark),
        (xo, xr, zo, zr),
        turned0,
        sent,
        sent_r,
        heads[0][3],
        shared_r,
        (qv0, qv1, sums_one, sums_two, db1),
    )
    up_sum.wait(attn_grads[0])
    up_sum.near()
    down_sum.wait(up_sum.mark)
    small = Everywhere(vec, n)
    attn_sum = Scatter(meta, after(tuple(attn_grads), down_sum.mark), n)
    small.core(down_sum.mark)
    small.step((4,))
    small.step((8,))
    up_sum.wait()
    up_sum.z_all(small.v)
    small_state = [v.reshape(LINES, 128) for v in (small_w, small_m, small_v)]
    dx_o, dx_r = frames_back(
        after(meta, up_sum.mark),
        dy1,
        (turned0, sent),
        w_attn,
    )
    attn_sum.near(dx_o)
    up_sum.wait(attn_sum.mark)
    dx_other = other_core(after(dx_r, up_sum.mark))
    out_other = other_core(after(out_r, up_sum.mark))
    attn_sum.z_all(dx_other, out_other)
    small.step((1,), attn_sum.mark)
    frames_grad = joined(dx_o, after(dx_other, small.v))
    output = joined(out_o, after(out_other, small.v))
    small.step((2,))
    small_all = small.total()
    grads, square = totals(
        meta, count, attn_sum.parts(frames_grad, output, small_all) + up_sum.parts() + down_sum.parts()
    )
    every = Everywhere(square, n)
    every.core()
    every.step(XY_MASKS)
    every.step(Z_MASKS[1:])
    state = (attn_w, attn_m, attn_v, ffn_w, ffn_m, ffn_v)
    norm, small_new, small_m_new, small_v_new, *new_state = adamw_call(
        meta, every.total(), small_all, grads, small_state, state
    )
    attn_new, attn_m_new, attn_v_new, ffn_new, ffn_m_new, ffn_v_new = new_state
    grad_norm = norm[0, 0]
    small_new, small_m_new, small_v_new = [
        v.reshape(SMALL) for v in (small_new, small_m_new, small_v_new)
    ]
    return (
        output,
        frames_grad,
        grad_norm,
        attn_new,
        attn_m_new,
        attn_v_new,
        ffn_new,
        ffn_m_new,
        ffn_v_new,
        small_new,
        small_m_new,
        small_v_new,
    )


def solution(mesh):
    rows = P(None, "dp", "tensor", None)
    weights = P(None, "dp", "tensor")
    in_specs = (rows, rows, P(None, "dp")) + (weights,) * 6 + (P(),) * 3
    out_specs = (rows, rows, P()) + (weights,) * 6 + (P(),) * 3
    return jax.shard_map(
        per_device, mesh=mesh, in_specs=in_specs, out_specs=out_specs, check_vma=False
    )
```

```python
import math

import jax
import jax.numpy as jnp
from jax import lax
from jax.experimental import pallas as pl
from jax.experimental.pallas import tpu as pltpu
from jax.sharding import PartitionSpec as P

HD = 64
D = 768
FF = 3072
SEQ = 512
HALF = SEQ // 2
STEP = 10
SMALL = 9216
PAIRS = 6
BLOCKS = 16
ROWS = D // BLOCKS

EPS_NORM = 1e-05
MASK_FILL = -1e30
BETA_ONE = 0.9
BETA_TWO = 0.999
ADAM_EPS = 1e-08
CLIP_NORM = 0.1
RATE = 0.1
SMALL_RATE = 1.5
DECAY = 0.01

BF = jnp.bfloat16
F32 = jnp.float32

STEP_A = (2, 1)
STEP_B = (1, 2)
Z_MASKS = (0, 4, 8, 12)
MASKS = tuple(
    (
        tuple(z for z in Z_MASKS) + tuple(z + near for z in Z_MASKS),
        tuple(z + far for z in Z_MASKS) + tuple(z + near + far for z in Z_MASKS),
    )
    for near, far in (STEP_A, STEP_B)
)


def dot(left, right):
    return jnp.dot(left, right, preferred_element_type=F32)


def dot_t(left, right):
    return lax.dot_general(left, right, (((1,), (1,)), ((), ())), preferred_element_type=F32)


def gelu_pair(u):
    phi = 0.5 * lax.erf(u * math.sqrt(0.5)) + 0.5
    return u * phi, phi + u * jnp.exp(-0.5 * u * u) * (1.0 / math.sqrt(2.0 * math.pi))


HBM = pl.BlockSpec(memory_space=pltpu.HBM)
SMEM = pl.BlockSpec(memory_space=pltpu.SMEM)


VMEM = pl.BlockSpec(memory_space=pltpu.VMEM)


def kernel_call(body, name, meta, raw, ins, outs, raw_outs, scratch, micros):
    n_raw, n_in, n_out, n_raw_out = len(raw), len(ins), len(outs), len(raw_outs)

    def run(meta_ref, *refs):
        cuts = [0, n_raw, n_in, n_out, n_raw_out]
        for i in range(1, 5):
            cuts[i] += cuts[i - 1]
        groups = [refs[cuts[i] : cuts[i + 1]] for i in range(4)]
        body(meta_ref, *groups, *refs[cuts[4] :])

    held = sum(
        math.prod(v.shape) * (2 if v.dtype == BF else 4) for v in scratch if v.dtype in (BF, F32)
    )
    return pl.pallas_call(
        run,
        name=name,
        in_specs=[SMEM] + [HBM] * n_raw + [VMEM] * n_in,
        out_specs=[VMEM] * n_out + [HBM] * n_raw_out,
        out_shape=[jax.ShapeDtypeStruct(s, d) for s, d in outs]
        + [pltpu.HBM(s, d) for s, d in raw_outs],
        scratch_shapes=scratch,
        compiler_params=pltpu.CompilerParams(vmem_limit_bytes=held + SPARE),
        cost_estimate=pl.CostEstimate(
            flops=int(micros * 1.15e9), bytes_accessed=0, transcendentals=0
        ),
    )(meta, *[pltpu.with_memory_space_constraint(v, pltpu.HBM) for v in raw], *ins)


SPARE = 8 * 2**20
W_SHAPE = (4, D, D)


def place(meta, pieces, w):
    d = meta[0]
    for part in range(4):
        rel, half = divmod(part, 2)
        for sel in range(2):
            src = pieces[half * 4 + rel * 2 + sel]
            for j in range(8):
                row = pl.multiple_of((d ^ MASKS[half][sel][j]) * ROWS, 16)
                w[part, pl.ds(row, ROWS), :] = src[j]


def chunk(c):
    return pl.ds(pl.multiple_of(c * CHUNK, CHUNK), CHUNK)


CHUNK = 256
PER_PART = D // CHUNK


def row_sum(v):
    return jnp.sum(v, 0, keepdims=True)


def attend(meta, q_ref, k_ref, v_ref, qt_ref, ot_ref, o_ref, p_buf, p_out, p_sems):
    t, length = meta[1], meta[2]
    row = lax.broadcasted_iota(jnp.int32, (SEQ, 1), 0)
    position = jnp.where(row < HALF, row + t * HALF, row + (1 - t) * HALF - HALF)
    valid = position < length
    lane = lax.broadcasted_iota(jnp.int32, (SEQ, 128), 1)

    def pair(i, carry):
        keys = k_ref[i]
        q_t = q_ref[i].T
        lines = pl.ds(pl.multiple_of(i * 128, 128), 128)
        qt_ref[lines, :] = q_t
        v_t = v_ref[i].T
        halves = []
        for hh in range(2):
            own = (lane < HD) if hh == 0 else (lane >= HD)
            s = dot(jnp.where(own, keys, jnp.zeros_like(keys)), q_t)
            s = jnp.where(valid, s, MASK_FILL)
            e = jnp.exp(s - jnp.max(s, 0, keepdims=True))
            prob = (e * (1.0 / jnp.sum(e, 0, keepdims=True))).astype(BF)
            head = 2 * i + hh
            p_buf[head] = prob
            pltpu.make_async_copy(p_buf.at[head], p_out.at[head], p_sems.at[head]).start()
            halves.append(dot(v_t[hh * HD : (hh + 1) * HD], prob))
        o_t = jnp.concatenate(halves, 0).astype(BF)
        ot_ref[lines, :] = o_t
        o_ref[:, lines] = o_t.T
        return carry

    lax.fori_loop(0, 3, pair, 0)


def attend_wait(p_buf, p_out, p_sems):
    for i in range(6):
        pltpu.make_async_copy(p_buf.at[i], p_out.at[i], p_sems.at[i]).wait()


TURNED = ((384, SEQ), BF)
HEADS = [((3, SEQ, 128), BF), ((3, SEQ, 128), BF), TURNED, TURNED]
ATTEND_SCRATCH = [
    pltpu.VMEM((6, SEQ, SEQ), BF),
    pltpu.SemaphoreType.DMA((6,)),
    pltpu.SemaphoreType.DMA((5,)),
]


def attn_first_body(meta, _, ins, outs, raw_outs, p_buf, p_sems, sems, w, q_ref, *head_refs):
    xo, xr, s12, *pieces = ins
    later, o_ref, out_w = outs
    place(meta, pieces, w)
    copies = [
        pltpu.make_async_copy(a, raw_outs[i], sems.at[i]) for i, a in enumerate([*head_refs, w])
    ]
    copies[4].start()
    t = meta[1]
    for rel in range(2):
        if rel == 0:
            targets = q_ref, head_refs[0], head_refs[1]
        else:
            targets = later.at[0], later.at[1], later.at[2]
        cols = pl.ds(pl.multiple_of((t ^ rel) * 384, 128), 384)
        bq = s12[0:1, cols]
        bv = s12[1:2, cols]
        for r, x in ((0, xo), (1, xr)):
            rows = pl.ds(r * HALF, HALF)
            qk = dot(x[...], w[rel * 2])
            q = (qk[:, :384] + bq).astype(BF) * jnp.asarray(HD**-0.5, BF)
            k = qk[:, 384:].astype(BF)
            v = (dot(x[...], w[rel * 2 + 1, :, :384]) + bv).astype(BF)
            for ref, value in zip(targets, (q, k, v)):
                for i in range(3):
                    ref[i, rows, :] = value[:, i * 128 : (i + 1) * 128]
        out_w[rel] = w[rel * 2 + 1, :, 384:]
    k_ref, v_ref, qt_ref, ot_ref = head_refs
    attend(meta, q_ref, k_ref, v_ref, qt_ref, ot_ref, o_ref, p_buf, raw_outs[5], p_sems)
    for c in copies[:4]:
        c.start()
    for c in copies:
        c.wait()
    attend_wait(p_buf, raw_outs[5], p_sems)


def attn_first(meta, xo, xr, pieces, s12):
    return kernel_call(
        attn_first_body,
        "attn_first",
        meta,
        [],
        [xo, xr, s12, *pieces],
        [((3, 3, SEQ, 128), BF), ((SEQ, 384), BF), ((2, D, 384), BF)],
        HEADS + [(W_SHAPE, BF), ((6, SEQ, SEQ), BF)],
        ATTEND_SCRATCH
        + [pltpu.VMEM(W_SHAPE, BF), pltpu.VMEM((3, SEQ, 128), BF)]
        + [pltpu.VMEM(*h) for h in HEADS],
        9.0,
    )


def attn_second_body(meta, _, ins, outs, raw_outs, p_buf, p_sems, sems, o_ref, qt_ref, ot_ref):
    xo, xr, s12, later, o_first, out_w = ins
    yh, rs, hb, shared = outs
    held = later.at[1], later.at[2], qt_ref, ot_ref
    copies = [pltpu.make_async_copy(a, raw_outs[i], sems.at[i]) for i, a in enumerate(held)]
    for c in copies[:2]:
        c.start()
    attend(
        meta,
        later.at[0],
        later.at[1],
        later.at[2],
        qt_ref,
        ot_ref,
        o_ref,
        p_buf,
        raw_outs[4],
        p_sems,
    )
    for c in copies[2:]:
        c.start()
    bo, g1, c1 = s12[2:3, :], s12[4:5, :], s12[5:6, :]
    for r, x in ((0, xo), (1, xr)):
        rows = pl.ds(r * HALF, HALF)
        a = dot_t(o_first[rows, :], out_w[0]) + dot_t(o_ref[rows, :], out_w[1])
        y = x[...].astype(F32) + a + bo
        centred = y - jnp.mean(y, -1, keepdims=True)
        inv = lax.rsqrt(jnp.mean(centred * centred, -1, keepdims=True) + EPS_NORM)
        hat = centred * inv
        yh[rows, :] = hat
        rs[rows, :] = inv
        hb[rows, :] = (hat * g1 + c1).astype(BF)
    shared[0] = ot_ref[...]
    for i in range(2):
        shared[1 + i] = hb[:, i * 384 : (i + 1) * 384].T
    for c in copies:
        c.wait()
    attend_wait(p_buf, raw_outs[4], p_sems)


def attn_second(meta, xo, xr, s12, later, o_first, out_w):
    return kernel_call(
        attn_second_body,
        "attn_second",
        meta,
        [],
        [xo, xr, s12, later, o_first, out_w],
        [((SEQ, D), F32), ((SEQ, 1), F32), ((SEQ, D), BF), ((3, 384, SEQ), BF)],
        HEADS + [((6, SEQ, SEQ), BF)],
        ATTEND_SCRATCH + [pltpu.VMEM((SEQ, 384), BF), pltpu.VMEM(*TURNED), pltpu.VMEM(*TURNED)],
        8.0,
    )


def ffn_up_body(meta, _, ins, outs, __):
    hb, s12, *pieces = ins
    f0, f1, gp, w = outs
    place(meta, pieces, w)
    for part in range(4):
        rel, half = divmod(part, 2)
        bias_row = pl.ds(8 + 2 * (meta[1] ^ rel) + half, 1)
        f_ref = (f0, f1)[rel]
        for c in range(PER_PART):
            cols = slice(c * CHUNK, (c + 1) * CHUNK)
            u = dot(hb[...], w[part, :, cols]) + s12[bias_row, cols]
            f, slope = gelu_pair(u)
            f_ref[half, :, cols] = f.astype(BF)
            gp[part, :, cols] = slope.astype(BF)


SIDE = ((2, SEQ, D), BF)
SLABS = ((2, 384, SEQ), BF)


def ffn_up(meta, hb, pieces, s12):
    return kernel_call(
        ffn_up_body,
        "ffn_up",
        meta,
        [],
        [hb, s12, *pieces],
        [SIDE, SIDE, ((4, SEQ, D), BF), (W_SHAPE, BF)],
        [],
        [],
        5.0,
    )


def norm_back(grad, hat, inv, gain):
    scaled = grad * gain
    return inv * (
        scaled
        - jnp.mean(scaled, -1, keepdims=True)
        - hat * jnp.mean(scaled * hat, -1, keepdims=True)
    )


def ffn_down_body(meta, _, ins, outs, __):
    f0, f1, yh, co, cr, s12, *pieces = ins
    out_o, out_r, dz, dz_t, dy2, sums, w = outs
    place(meta, pieces, w)
    t, length = meta[1], meta[2]
    b2 = s12[3:4, :]
    g1, c1, g2, c2 = s12[4:5, :], s12[5:6, :], s12[6:7, :], s12[7:8, :]
    fs = (f0, f1)
    for part in range(4):
        rel, half = divmod(part, 2)
        z = dot_t(fs[rel][half], w[part])
        dy2[...] = z if part == 0 else dy2[...] + z
    totals = [jnp.zeros((1, D), F32)] * 3
    for r, cot, out in ((0, co, out_o), (1, cr, out_r)):
        rows = pl.ds(r * HALF, HALF)
        y = yh[rows, :] * g1 + c1 + dy2[rows, :] + b2
        centred = y - jnp.mean(y, -1, keepdims=True)
        inv = lax.rsqrt(jnp.mean(centred * centred, -1, keepdims=True) + EPS_NORM)
        hat = centred * inv
        out[...] = (hat * g2 + c2).astype(BF)
        row = lax.broadcasted_iota(jnp.int32, (HALF, 1), 0)
        valid = row + (t ^ r) * HALF < length
        dout = jnp.where(valid, cot[...].astype(F32), 0.0)
        grad = norm_back(dout, hat, inv, g2)
        dy2[rows, :] = grad
        dz[rows, :] = grad.astype(BF)
        totals = [a + row_sum(b) for a, b in zip(totals, (grad, dout * hat, dout))]
    for i in range(3):
        sums[i : i + 1, :] = totals[i]
    for i in range(2):
        dz_t[i] = dz[:, i * 384 : (i + 1) * 384].T


def ffn_down(meta, f0, f1, pieces, yh, co, cr, s12):
    return kernel_call(
        ffn_down_body,
        "ffn_down",
        meta,
        [],
        [f0, f1, yh, co, cr, s12, *pieces],
        [
            ((HALF, D), BF),
            ((HALF, D), BF),
            ((SEQ, D), BF),
            SLABS,
            ((SEQ, D), F32),
            ((8, D), F32),
            (W_SHAPE, BF),
        ],
        [],
        [],
        5.0,
    )


def ffn_back_body(meta, _, ins, outs, __):
    dz, gp, w = ins
    du0, du1, db1 = outs
    for part in (2, 3, 0, 1):
        rel, half = divmod(part, 2)
        bias_row = pl.ds(2 * (meta[1] ^ rel) + half, 1)
        du_ref = (du0, du1)[rel]
        for c in range(PER_PART):
            cols = slice(c * CHUNK, (c + 1) * CHUNK)
            du = dot(dz[...], w[part, :, cols]) * gp[part, :, cols].astype(F32)
            db1[bias_row, cols] = row_sum(du)
            du_ref[half, :, cols] = du.astype(BF)


def ffn_back(meta, dz, w, gp):
    return kernel_call(
        ffn_back_body,
        "ffn_back",
        meta,
        [],
        [dz, gp, w],
        [SIDE, SIDE, ((4, D), F32)],
        [],
        [],
        3.5,
    )


def hidden_back(ins, outs):
    du0, du1, dy2, yh, inv, small, w = ins
    dy1, da, sums = outs
    dus = (du0, du1)
    for part in range(4):
        rel, half = divmod(part, 2)
        before = dy2 if part == 0 else dy1
        dy1[...] = before[...] + dot_t(dus[rel][half], w[part])
    g1 = small[4:5, :]
    totals = [jnp.zeros((1, D), F32)] * 3
    for r in range(2):
        rows = pl.ds(r * HALF, HALF)
        dh = dy1[rows, :]
        hat = yh[rows, :]
        grad = norm_back(dh, hat, inv[rows, :], g1)
        dy1[rows, :] = grad
        da[rows, :] = grad.astype(BF)
        totals = [a + row_sum(b) for a, b in zip(totals, (grad, dh * hat, dh))]
    for i in range(3):
        sums[i : i + 1, :] = totals[i]


class AttnBack:
    SCRATCH = [
        pltpu.VMEM((D, D), BF),
        pltpu.VMEM((6, SEQ, SEQ), BF),
        pltpu.SemaphoreType.DMA((6,)),
        pltpu.SemaphoreType.DMA((5,)),
        pltpu.VMEM((3, 128, SEQ), BF),
        pltpu.VMEM((3, 128, SEQ), BF),
    ] + [pltpu.VMEM(*h) for h in HEADS]

    def __init__(self, rel, raw, scratch):
        *head_in, w_in, self.p_in = raw
        self.w, self.p_buf, self.p_sems, sems, self.do_t, self.k_t, *self.heads = scratch
        self.copies = [pltpu.make_async_copy(w_in.at[rel * 2 + 1], self.w, sems.at[4])]
        self.copies += [
            pltpu.make_async_copy(a, b, sems.at[i])
            for i, (a, b) in enumerate(zip(head_in, self.heads))
        ]

    def start(self):
        for c in self.copies:
            c.start()
        for i in range(6):
            pltpu.make_async_copy(self.p_in.at[i], self.p_buf.at[i], self.p_sems.at[i]).start()

    def run(self, da, dq, dk, dv, sums):
        w, do_t_ref, k_t_ref = self.w, self.do_t, self.k_t
        k_ref, v_ref, qt_ref, ot_ref = self.heads
        for c in self.copies:
            c.wait()
        do = dot(da[...], w[:, 384:]).astype(BF)
        for i in range(3):
            do_t_ref[i] = do[:, i * 128 : (i + 1) * 128].T
            k_t_ref[i] = k_ref[i].T
        lane = lax.broadcasted_iota(jnp.int32, (SEQ, 128), 1)

        def pair(i, carry):
            vp = v_ref[i]
            do_t = do_t_ref[i]
            base = pl.multiple_of(i * 128, 128)
            both = do_t.astype(F32) * ot_ref[pl.ds(base, 128), :].astype(F32)
            for hh in range(2):
                own = (lane < HD) if hh == 0 else (lane >= HD)
                inside = slice(hh * HD, (hh + 1) * HD)
                delta = row_sum(both[inside])
                slope = dot(jnp.where(own, vp, jnp.zeros_like(vp)), do_t)
                head = 2 * i + hh
                pltpu.make_async_copy(
                    self.p_in.at[head], self.p_buf.at[head], self.p_sems.at[head]
                ).wait()
                prob = self.p_buf[head]
                ds = (prob.astype(F32) * (slope - delta)).astype(BF)
                lines = pl.ds(base + hh * HD, HD)
                dv[lines, :] = dot_t(do_t[inside], prob).astype(BF)
                dk[lines, :] = dot_t(qt_ref[lines, :], ds).astype(BF)
                dq[lines, :] = (dot(k_t_ref[i, inside, :], ds) * (HD**-0.5)).astype(BF)
            return carry

        lax.fori_loop(0, 3, pair, 0)
        ones = jnp.ones((8, SEQ), BF)
        sums[0:8, :] = dot_t(ones, dq[...])
        sums[8:16, :] = dot_t(ones, dv[...])


LINES = SMALL // 128


def put_lines(vec, first, row):
    for i in range(row.shape[1] // 128):
        vec[pl.ds(first + i, 1), :] = row[:, i * 128 : (i + 1) * 128]


def frames_back_body(meta, raw, ins, outs, _, total, w, dy1, sem):
    grads = ins
    copies = [pltpu.make_async_copy(raw[0].at[i], w.at[i], sem.at[i]) for i in range(4)]
    copies.append(pltpu.make_async_copy(raw[1], dy1, sem.at[4]))
    for c in copies:
        c.start()
    for c in copies:
        c.wait()
    for m in range(3):
        rows = pl.ds(m * 256, 256)
        acc = None
        for rel in range(2):
            for side, left in enumerate(
                (w[rel * 2, rows, :384], w[rel * 2, rows, 384:], w[rel * 2 + 1, rows, :384])
            ):
                term = dot(left, grads[rel][side])
                acc = term if acc is None else acc + term
        total[rows, :] = acc
    for r in range(2):
        rows = pl.ds(r * HALF, HALF)
        outs[r][...] = dy1[rows, :] + total[:, r * HALF : (r + 1) * HALF].T


def frames_back(meta, dy1, turned, w):
    return kernel_call(
        frames_back_body,
        "frames_back",
        meta,
        [w, dy1],
        turned,
        [((HALF, D), F32)] * 2,
        [],
        [
            pltpu.VMEM((D, SEQ), F32),
            pltpu.VMEM(W_SHAPE, BF),
            pltpu.VMEM((SEQ, D), F32),
            pltpu.SemaphoreType.DMA((5,)),
        ],
        3.5,
    )


def near_body(meta, _, ins, outs, __):
    for half in range(2):
        keep, came = ins[half], ins[2 + half]
        for i in range(4):
            outs[2 + half][i] = (keep[4 + i].astype(F32) + came[4 + i].astype(F32)).astype(BF)
            outs[half][i] = (keep[i].astype(F32) + came[i].astype(F32)).astype(BF)


def near_sums(meta, keep, came):
    outs = kernel_call(
        near_body, "near_sums", meta, [], [*keep, *came], [((4, ROWS, D), BF)] * 4, [], [], 0.5
    )
    return outs[:2], outs[2:]


def z_body(meta, _, ins, outs, __):
    for half in range(2):
        keep, came = ins[half], ins[2 + half]
        cols = slice(half * D, (half + 1) * D)
        for i in range(4):
            outs[i][:, cols] = (keep[i].astype(F32) + came[i].astype(F32)).astype(outs[i].dtype)


ROW = (ROWS, 2 * D)


def z_sums(meta, keep, came):
    return kernel_call(
        z_body, "z_sums", meta, [], [*keep, *came], [(ROW, F32)] + [(ROW, BF)] * 3, [], [], 4.0
    )


def totals_body(meta, _, ins, outs, __):
    count = ins[0]
    grads, vec = outs
    square = jnp.zeros((1, 1), F32)
    for k in range(3):
        row, *came = ins[1 + 4 * k : 5 + 4 * k]
        total = row[...]
        for c in came:
            total = total + c[...].astype(F32)
        grads[k] = total
        square = square + jnp.sum(row_sum(total * total), 1, keepdims=True)
    lane = lax.broadcasted_iota(jnp.int32, (8, 128), 1)
    vec[...] = jnp.where(lane == 0, square, jnp.where(lane == 1, count[...], 0.0))


def totals(meta, count, parts):
    return kernel_call(
        totals_body,
        "totals",
        meta,
        [],
        [count, *parts],
        [((3, *parts[0].shape), F32), ((8, 128), F32)],
        [],
        [],
        1.0,
    )


def adamw_body(meta, raw, ins, outs, raw_outs, *scratch):
    square, vec, grads, small_w, small_m, small_v, aw, am, av, fw, fm, fv = ins
    norm_out, small_out = outs[0], outs[1:]
    new_a, new_f, sems = scratch
    frame_count = square[0:1, 1:2]
    small = vec[...]
    squares = square[0:1, 0:1] + jnp.sum(row_sum(small * small), 1, keepdims=True)
    norm = jnp.sqrt(squares) / frame_count
    norm_out[...] = norm
    factor = jnp.minimum(1.0, CLIP_NORM / norm) / frame_count
    copies = []
    for i in range(4):
        cols = slice((i % 2) * 384 + (i // 2) * D, (i % 2) * 384 + (i // 2) * D + 384)
        rate = RATE * 0.5 * SEQ**0.5 if i == 3 else RATE
        for k, v in enumerate(adamw(aw[i], am[i], av[i], grads[0, :, cols] * factor, rate, DECAY)):
            new_a[k, i] = v
    for k in range(3):
        copies.append(pltpu.make_async_copy(new_a.at[k], raw_outs[k], sems.at[k]))
        copies[-1].start()
    for i in range(2):
        for k, v in enumerate(adamw(fw[i], fm[i], fv[i], grads[1 + i] * factor, RATE, DECAY)):
            new_f[k, i] = v
    for k in range(3):
        copies.append(pltpu.make_async_copy(new_f.at[k], raw_outs[3 + k], sems.at[3 + k]))
        copies[-1].start()
    new_small = adamw(small_w[...], small_m[...], small_v[...], small * factor, SMALL_RATE, 0.0)
    for out, v in zip(small_out, new_small):
        out[...] = v
    for c in copies:
        c.wait()


def adamw_call(meta, square, vec, grads, small, state):
    shapes = [v.shape for v in state]
    return kernel_call(
        adamw_body,
        "adamw",
        meta,
        [],
        [square, vec, grads, *small, *state],
        [((1, 1), F32)] + [((LINES, 128), F32)] * 3,
        [(s, F32) for s in shapes],
        [
            pltpu.VMEM((3, *shapes[0]), F32),
            pltpu.VMEM((3, *shapes[3]), F32),
            pltpu.SemaphoreType.DMA((6,)),
        ],
        3.0,
    )


def put_out(meta, acc, outs, half):
    d = meta[0]
    for sel in range(2):
        for j in range(8):
            row = pl.multiple_of((d ^ MASKS[half][sel][j]) * ROWS, 16)
            outs[half * 2 + sel][j] = acc[half, pl.ds(row, ROWS), :]


GRAD_OUTS = [((8, ROWS, D), BF)] * 4
GRAD_SCRATCH = [pltpu.VMEM((2, D, D), BF)]


def ffn_grad(meta, left_o, left_r, right_o, right_r, outs, acc):
    for half in range(2):
        for i in range(2):
            total = dot(left_o[i], right_o[half]) + dot(left_r[i], right_r[half])
            acc[half, i * 384 : (i + 1) * 384, :] = total.astype(BF)
        put_out(meta, acc, outs, half)


def down_grad_body(meta, _, ins, outs, __, acc):
    dz_o, dz_r, f_o, f_r = ins
    ffn_grad(meta, dz_o, dz_r, f_o, f_r, outs, acc)


def down_grad_call(meta, *ins):
    return kernel_call(
        down_grad_body, "down_grad", meta, [], ins, GRAD_OUTS, [], GRAD_SCRATCH, 4.0
    )


def middle_body(meta, raw, ins, outs, raw_outs, acc, grads, dy1, da, out_sems, *scratch):
    attn = AttnBack(1, raw, scratch)
    attn.start()
    shared, shared_r, du0, du_r, *rest = ins
    sums_one, sent, qv = outs
    copies = [
        pltpu.make_async_copy(a, b, out_sems.at[i])
        for i, (a, b) in enumerate(zip([*[grads.at[i] for i in range(4)], dy1, da], raw_outs))
    ]
    ffn_grad(
        meta,
        shared.at[pl.ds(1, 2)],
        shared_r.at[pl.ds(1, 2)],
        du0,
        du_r,
        [grads.at[i] for i in range(4)],
        acc,
    )
    for c in copies[:4]:
        c.start()
    hidden_back([du0, *rest], (dy1, da, sums_one))
    for c in copies[4:]:
        c.start()
    for i in range(2):
        sent[3 + i] = da[:, i * 384 : (i + 1) * 384].T
    attn.run(da, sent.at[0], sent.at[1], sent.at[2], qv)
    for c in copies:
        c.wait()


def middle(meta, heads, w_attn, prob, shared, shared_r, du0, du_r, du1, dy2, yh, inv, s12, w):
    return kernel_call(
        middle_body,
        "up_grad_hidden_back_attn_back",
        meta,
        [*heads, w_attn, prob],
        [shared, shared_r, du0, du_r, du1, dy2, yh, inv, s12, w],
        [((8, D), F32), ((5, 384, SEQ), BF), ((16, 384), F32)],
        GRAD_OUTS + [((SEQ, D), F32), ((SEQ, D), BF)],
        GRAD_SCRATCH
        + [
            pltpu.VMEM((4, 8, ROWS, D), BF),
            pltpu.VMEM((SEQ, D), F32),
            pltpu.VMEM((SEQ, D), BF),
            pltpu.SemaphoreType.DMA((6,)),
        ]
        + AttnBack.SCRATCH,
        14.0,
    )


def attn_back_body(meta, raw, ins, outs, _, da, da_sem, *scratch):
    da_copy = pltpu.make_async_copy(raw[0], da, da_sem.at[0])
    da_copy.start()
    attn = AttnBack(0, raw[1:], scratch)
    attn.start()
    turned, qv = outs
    da_copy.wait()
    attn.run(da, turned.at[0], turned.at[1], turned.at[2], qv)


def attn_back(meta, heads, w_attn, prob, da):
    return kernel_call(
        attn_back_body,
        "attn_back",
        meta,
        [da, *heads, w_attn, prob],
        [],
        [((3, 384, SEQ), BF), ((16, 384), F32)],
        [],
        [pltpu.VMEM((SEQ, D), BF), pltpu.SemaphoreType.DMA((1,))] + AttnBack.SCRATCH,
        7.0,
    )


def attn_grad_body(meta, _, ins, outs, __, acc, x_t):
    xo, xr, zo, zr, turned, sent, sent_r, o_own, shared_r = ins[:9]
    qv0, qv1, sums_one, sums_two, db1 = ins[9:]
    vec = outs[4]
    for rel, qv in ((0, qv0), (1, qv1)):
        h = meta[1] ^ rel
        put_lines(vec, 3 * h, qv[0:1, :])
        put_lines(vec, 6 + 3 * h, qv[8:9, :])
    for line, sums, row in (
        (2, sums_one, 0),
        (3, sums_two, 0),
        (4, sums_one, 1),
        (5, sums_one, 2),
        (6, sums_two, 1),
        (7, sums_two, 2),
    ):
        put_lines(vec, 6 * line, sums[row : row + 1, :])
    for i in range(4):
        put_lines(vec, 48 + 6 * i, db1[i : i + 1, :])
    for i, v in enumerate((xo, xr, zo, zr)):
        x_t[:, i * HALF : (i + 1) * HALF] = v[...].T
    for half, side, k in ((1, 0, 2), (0, 0, 0), (0, 1, 1)):
        for m in range(3):
            rows = pl.ds(m * 256, 256)
            total = dot_t(x_t[rows, :SEQ], turned[k]) + dot_t(x_t[rows, SEQ:], sent_r[k])
            acc[half, rows, side * 384 : (side + 1) * 384] = total.astype(BF)
    for i in range(2):
        total = dot_t(sent[3 + i], o_own[...]) + dot_t(sent_r[3 + i], shared_r[0])
        acc[1, i * 384 : (i + 1) * 384, 384:] = total.astype(BF)
    for half in range(2):
        put_out(meta, acc, outs, half)


def attn_grad(meta, xs, turned, sent, sent_r, o_own, shared_r, small):
    return kernel_call(
        attn_grad_body,
        "attn_grad",
        meta,
        [],
        [*xs, turned, sent, sent_r, o_own, shared_r, *small],
        GRAD_OUTS + [((LINES, 128), F32)],
        [],
        GRAD_SCRATCH + [pltpu.VMEM((D, 2 * SEQ), BF)],
        5.0,
    )


def adamw(weight, moment_one, moment_two, grad, rate, decay):
    new_one = BETA_ONE * moment_one + (1.0 - BETA_ONE) * grad
    new_two = BETA_TWO * moment_two + (1.0 - BETA_TWO) * grad * grad
    fixed_one = new_one / (1.0 - BETA_ONE**STEP)
    fixed_two = new_two / (1.0 - BETA_TWO**STEP)
    update = fixed_one / (jnp.sqrt(fixed_two) + ADAM_EPS) + decay * weight
    return (weight - rate * update, new_one, new_two)


def after(v, *deps):
    return lax.optimization_barrier((v, *deps))[0]


def other_core(v):
    return lax.ppermute(v, "tensor", [(0, 1), (1, 0)])


def shift(v, mask, n):
    return lax.ppermute(v, "dp", [(i, i ^ mask) for i in range(n)])


class Gather:
    def __init__(self, shard, n):
        self.n, self.shard, self.mark = n, shard, shard

    def z_all(self, *deps):
        if self.n == BLOCKS:
            shard = after(self.shard, *deps)
            self.z = [shard] + [shift(shard, z, self.n) for z in Z_MASKS[1:]]
            self.mark = shard

    def z_wait(self, *deps):
        if self.n == BLOCKS:
            self.z = after(tuple(self.z), *deps)
            self.mark = self.z[1:]

    def far_wait(self, *deps):
        if self.n == BLOCKS:
            self.far_side = after(tuple(self.far_side), *deps)
            self.mark = tuple(self.far_side)

    def near_wait(self, *deps):
        if self.n == BLOCKS:
            self.came = after(tuple(self.came), *deps)
            self.mark = tuple(self.came)

    def near(self, *deps):
        if self.n != BLOCKS:
            return
        parts = after(tuple(self.z), *deps)
        self.own = [
            jnp.stack([v[:, half * D : (half + 1) * D] for v in parts]) for half in range(2)
        ]
        self.mark = tuple(self.own)
        self.came = [shift(s, step[0], self.n) for s, step in zip(self.own, (STEP_A, STEP_B))]

    def far(self, *deps):
        if self.n != BLOCKS:
            return
        came = after(tuple(self.came), *deps)
        self.own = [jnp.concatenate([s, c]) for s, c in zip(self.own, came)]
        self.mark = tuple(self.own)
        self.far_side = [shift(o, step[1], self.n) for o, step in zip(self.own, (STEP_A, STEP_B))]

    def core(self, *deps):
        if self.n == BLOCKS:
            self.own_other = [other_core(o) for o in after(tuple(self.own), *deps)]
            self.mark = tuple(self.own_other)

    def pieces(self, *deps):
        if self.n == BLOCKS:
            far = after(tuple(self.far_side), *deps)
            result = []
            for half in range(2):
                far_other = other_core(far[half])
                result += [self.own[half], far[half], self.own_other[half], far_other]
            self.mark = far[1]
            return result
        full = lax.all_gather(self.shard, "dp", axis=0, tiled=True)
        blocks = full.reshape(BLOCKS, ROWS, 2 * D)
        result = []
        for half in range(2):
            cols = slice(half * D, (half + 1) * D)
            own = [blocks[jnp.array(m), :, cols] for m in MASKS[half]]
            result += own + [other_core(v) for v in own]
        return result


def added(*parts):
    total = parts[0].astype(F32)
    for p in parts[1:]:
        total = total + p.astype(F32)
    return total


class Scatter:
    def __init__(self, meta, pieces, n):
        self.meta = meta
        self.n, self.pieces, self.mark = n, pieces, pieces[0]
        if n == BLOCKS:
            self.keep = [pieces[0], pieces[2]]
            self.came = [
                shift(v, step[1], n) for v, step in zip((pieces[1], pieces[3]), (STEP_A, STEP_B))
            ]

    def near(self, *deps):
        if self.n != BLOCKS:
            return
        came = after(tuple(self.came), *deps)
        self.keep, send = near_sums(self.meta, self.keep, came)
        self.came = [shift(s, step[0], self.n) for s, step in zip(send, (STEP_A, STEP_B))]
        self.mark = tuple(send)

    def wait(self, *deps):
        if self.n == BLOCKS:
            self.came = after(tuple(self.came), *deps)
            self.mark = tuple(self.came)

    def z_all(self, *deps):
        if self.n != BLOCKS:
            return
        came = after(tuple(self.came), *deps)
        self.row, *sends = z_sums(self.meta, self.keep, came)
        self.mark = tuple(sends)
        self.came = [shift(s, z, self.n) for s, z in zip(sends, Z_MASKS[1:])]

    def parts(self, *deps):
        if self.n == BLOCKS:
            return [self.row, *after(tuple(self.came), *deps)]
        whole = self.whole()
        zero = jnp.zeros(whole.shape, BF)
        return [whole, zero, zero, zero]

    def whole(self):
        result = []
        for half in range(2):
            order = MASKS[half][0] + MASKS[half][1]
            back = [order.index(i) for i in range(BLOCKS)]
            full = jnp.concatenate(self.pieces[2 * half : 2 * half + 2])[jnp.array(back)]
            full = full.reshape(D, D).astype(F32)
            result.append(lax.psum_scatter(full, "dp", scatter_dimension=0, tiled=True))
        return jnp.concatenate(result, 1)


class Everywhere:
    def __init__(self, v, n):
        self.n, self.v = n, v

    def core(self, *deps):
        if self.n == BLOCKS:
            v = after(self.v, *deps)
            self.v = v + other_core(v)

    def step(self, masks, *deps):
        if self.n == BLOCKS:
            v = after(self.v, *deps)
            came = [shift(v, m, self.n) for m in masks]
            self.v = v + came[0] if len(came) == 1 else (v + came[0]) + (came[1] + came[2])

    def total(self):
        return self.v if self.n == BLOCKS else lax.psum(self.v, ("dp", "tensor"))


XY_MASKS = (1, 2, 3)


def per_device(
    frames,
    cotangent,
    lengths,
    attn_w,
    attn_m,
    attn_v,
    ffn_w,
    ffn_m,
    ffn_v,
    small_w,
    small_m,
    small_v,
):
    n = lax.axis_size("dp")
    t = lax.axis_index("tensor")
    d = lax.axis_index("dp") if n == BLOCKS else 0
    length = lax.dynamic_index_in_dim(lengths[:, 0], t, 0, keepdims=False)
    meta = jnp.stack([jnp.asarray(d, jnp.int32), jnp.asarray(t, jnp.int32), length])
    s12 = small_w.reshape(12, D)
    half = SEQ // lax.axis_size("tensor")
    count = jnp.sum(jnp.clip(lengths - t * half, 0, half)).astype(F32).reshape(1, 1)

    def pick(v, i):
        return lax.dynamic_index_in_dim(v[:, 0], i, 0, keepdims=False)

    def joined(own, other):
        return jnp.where(t == 0, jnp.stack([own, other]), jnp.stack([other, own]))[:, None]

    attn = Gather(jnp.concatenate([attn_w[i] for i in range(4)], 1).astype(BF), n)
    up = Gather(ffn_w[0].astype(BF), n)
    down = Gather(ffn_w[1].astype(BF), n)
    attn.z_all()
    frames_r = other_core(frames)
    xo, zr = pick(frames, t), pick(frames, 1 - t)
    xr, zo = pick(frames_r, t), pick(frames_r, 1 - t)
    cotangent_r = other_core(cotangent)
    co, cr = pick(cotangent, t), pick(cotangent_r, t)
    attn.near(xr, cr)
    up.z_all(attn.mark)
    attn.far()
    up.near(attn.mark)
    attn.core()
    attn_pieces = attn.pieces(up.mark)
    down.z_all(attn.mark)
    up.far(attn.mark)
    first = attn_first(after(meta, up.mark, down.mark, count), xo, xr, attn_pieces, s12)
    later, o_first, out_w, *heads_first = first
    *heads_first, w_attn, prob_first = heads_first
    down.near(o_first)
    second = attn_second(after(meta, down.mark), xo, xr, s12, later, o_first, out_w)
    yh, inv, hb, shared, *heads_second = second
    *heads_second, prob_second = heads_second
    heads, prob = (heads_first, heads_second), (prob_first, prob_second)
    down.near_wait(inv)
    up.far_wait(inv)
    up.core(down.mark)
    up_pieces = up.pieces()
    down.far()
    down_far = down.mark
    down.core(up_pieces[1], up_pieces[3])
    f0, f1, gp, w_up = ffn_up(after(meta, down_far), hb, up_pieces, s12)
    down.far_wait(gp)
    down_pieces = down.pieces()
    f_r = other_core(after(f1, *down_pieces))
    shared_r = other_core(after(shared, *down_pieces))
    out_o, out_r, dz, dz_t, dy2, sums_two, w_down = ffn_down(
        meta, f0, f1, down_pieces, yh, co, cr, s12
    )
    dz_r = other_core(after(dz_t, f_r, shared_r))
    du0, du1, db1 = ffn_back(after(meta, f_r, shared_r), dz, w_down, gp)
    du_r = other_core(after(du1, dz_r))
    down_sum = Scatter(
        meta,
        down_grad_call(after(meta, db1), dz_t, dz_r, f0, f_r), n
    )
    *up_grad, dy1, da = middle(
        after(meta, down_sum.mark),
        heads[1],
        w_attn,
        prob[1],
        shared,
        shared_r,
        du0,
        du_r,
        du1,
        dy2,
        yh,
        inv,
        s12,
        w_up,
    )
    sums_one, sent, qv1, *up_grad = up_grad
    down_sum.wait(qv1)
    up_sum = Scatter(meta, after(tuple(up_grad), down_sum.mark), n)
    down_sum.near()
    sent_r = other_core(after(sent, down_sum.mark))
    turned0, qv0 = attn_back(after(meta, down_sum.mark), heads[0], w_attn, prob[0], da)
    down_sum.z_all(qv0, sent_r)
    *attn_grads, vec = attn_grad(
        after(meta, down_sum.mark),
        (xo, xr, zo, zr),
        turned0,
        sent,
        sent_r,
        heads[0][3],
        shared_r,
        (qv0, qv1, sums_one, sums_two, db1),
    )
    up_sum.wait(attn_grads[0])
    up_sum.near()
    down_sum.wait(up_sum.mark)
    small = Everywhere(vec, n)
    attn_sum = Scatter(meta, after(tuple(attn_grads), down_sum.mark), n)
    small.core(down_sum.mark)
    small.step((4,))
    up_sum.wait()
    up_sum.z_all(small.v)
    small_state = [v.reshape(LINES, 128) for v in (small_w, small_m, small_v)]
    attn_sum.near(up_sum.mark)
    dx_o, dx_r = frames_back(after(meta, attn_sum.mark), dy1, (turned0, sent), w_attn)
    attn_sum.wait(dx_o)
    up_sum.wait(dx_o)
    dx_other = other_core(after(dx_r, up_sum.mark, attn_sum.mark))
    out_other = other_core(after(out_r, up_sum.mark, attn_sum.mark))
    attn_sum.z_all(up_sum.mark)
    small.step((1,), attn_sum.mark, dx_other, out_other)
    frames_grad = joined(dx_o, after(dx_other, small.v))
    output = joined(out_o, after(out_other, small.v))
    small.step((2,))
    small.step((8,))
    small_all = small.total()
    grads, square = totals(
        meta, count, attn_sum.parts(frames_grad, output, small_all) + up_sum.parts() + down_sum.parts()
    )
    every = Everywhere(square, n)
    every.core()
    every.step(XY_MASKS)
    every.step(Z_MASKS[1:])
    state = (attn_w, attn_m, attn_v, ffn_w, ffn_m, ffn_v)
    norm, small_new, small_m_new, small_v_new, *new_state = adamw_call(
        meta, every.total(), small_all, grads, small_state, state
    )
    attn_new, attn_m_new, attn_v_new, ffn_new, ffn_m_new, ffn_v_new = new_state
    grad_norm = norm[0, 0]
    small_new, small_m_new, small_v_new = [
        v.reshape(SMALL) for v in (small_new, small_m_new, small_v_new)
    ]
    return (
        output,
        frames_grad,
        grad_norm,
        attn_new,
        attn_m_new,
        attn_v_new,
        ffn_new,
        ffn_m_new,
        ffn_v_new,
        small_new,
        small_m_new,
        small_v_new,
    )


def solution(mesh):
    rows = P(None, "dp", "tensor", None)
    weights = P(None, "dp", "tensor")
    in_specs = (rows, rows, P(None, "dp")) + (weights,) * 6 + (P(),) * 3
    out_specs = (rows, rows, P()) + (weights,) * 6 + (P(),) * 3
    return jax.shard_map(
        per_device, mesh=mesh, in_specs=in_specs, out_specs=out_specs, check_vma=False
    )
```

```python
import math

import jax
import jax.numpy as jnp
from jax import lax
from jax.experimental import pallas as pl
from jax.experimental.pallas import tpu as pltpu
from jax.sharding import PartitionSpec as P

HD = 64
D = 768
FF = 3072
SEQ = 512
HALF = SEQ // 2
STEP = 10
SMALL = 9216
PAIRS = 6
BLOCKS = 16
ROWS = D // BLOCKS

EPS_NORM = 1e-05
MASK_FILL = -1e30
BETA_ONE = 0.9
BETA_TWO = 0.999
ADAM_EPS = 1e-08
CLIP_NORM = 0.1
RATE = 0.1
SMALL_RATE = 1.5
DECAY = 0.01

BF = jnp.bfloat16
F32 = jnp.float32

STEP_A = (2, 1)
STEP_B = (1, 2)
Z_MASKS = (0, 4, 8, 12)
MASKS = tuple(
    (
        tuple(z for z in Z_MASKS) + tuple(z + near for z in Z_MASKS),
        tuple(z + far for z in Z_MASKS) + tuple(z + near + far for z in Z_MASKS),
    )
    for near, far in (STEP_A, STEP_B)
)


def dot(left, right):
    return jnp.dot(left, right, preferred_element_type=F32)


def dot_t(left, right):
    return lax.dot_general(left, right, (((1,), (1,)), ((), ())), preferred_element_type=F32)


def gelu_pair(u):
    phi = 0.5 * lax.erf(u * math.sqrt(0.5)) + 0.5
    return u * phi, phi + u * jnp.exp(-0.5 * u * u) * (1.0 / math.sqrt(2.0 * math.pi))


HBM = pl.BlockSpec(memory_space=pltpu.HBM)
SMEM = pl.BlockSpec(memory_space=pltpu.SMEM)


VMEM = pl.BlockSpec(memory_space=pltpu.VMEM)


def kernel_call(body, name, meta, raw, ins, outs, raw_outs, scratch, micros):
    n_raw, n_in, n_out, n_raw_out = len(raw), len(ins), len(outs), len(raw_outs)

    def run(meta_ref, *refs):
        cuts = [0, n_raw, n_in, n_out, n_raw_out]
        for i in range(1, 5):
            cuts[i] += cuts[i - 1]
        groups = [refs[cuts[i] : cuts[i + 1]] for i in range(4)]
        body(meta_ref, *groups, *refs[cuts[4] :])

    held = sum(
        math.prod(v.shape) * (2 if v.dtype == BF else 4) for v in scratch if v.dtype in (BF, F32)
    )
    return pl.pallas_call(
        run,
        name=name,
        in_specs=[SMEM] + [HBM] * n_raw + [VMEM] * n_in,
        out_specs=[VMEM] * n_out + [HBM] * n_raw_out,
        out_shape=[jax.ShapeDtypeStruct(s, d) for s, d in outs]
        + [pltpu.HBM(s, d) for s, d in raw_outs],
        scratch_shapes=scratch,
        compiler_params=pltpu.CompilerParams(vmem_limit_bytes=held + SPARE),
        cost_estimate=pl.CostEstimate(
            flops=int(micros * 1.15e9), bytes_accessed=0, transcendentals=0
        ),
    )(meta, *[pltpu.with_memory_space_constraint(v, pltpu.HBM) for v in raw], *ins)


SPARE = 8 * 2**20
W_SHAPE = (4, D, D)


def place(meta, pieces, w):
    d = meta[0]
    for part in range(4):
        rel, half = divmod(part, 2)
        for sel in range(2):
            src = pieces[half * 4 + rel * 2 + sel]
            for j in range(8):
                row = pl.multiple_of((d ^ MASKS[half][sel][j]) * ROWS, 16)
                w[part, pl.ds(row, ROWS), :] = src[j]


def chunk(c):
    return pl.ds(pl.multiple_of(c * CHUNK, CHUNK), CHUNK)


CHUNK = 256
PER_PART = D // CHUNK


def row_sum(v):
    return jnp.sum(v, 0, keepdims=True)


def attend(meta, q_ref, k_ref, v_ref, qt_ref, ot_ref, o_ref, p_buf, p_out, p_sems):
    t, length = meta[1], meta[2]
    row = lax.broadcasted_iota(jnp.int32, (SEQ, 1), 0)
    position = jnp.where(row < HALF, row + t * HALF, row + (1 - t) * HALF - HALF)
    valid = position < length
    lane = lax.broadcasted_iota(jnp.int32, (SEQ, 128), 1)

    def pair(i, carry):
        keys = k_ref[i]
        q_t = q_ref[i].T
        lines = pl.ds(pl.multiple_of(i * 128, 128), 128)
        qt_ref[lines, :] = q_t
        v_t = v_ref[i].T
        halves = []
        for hh in range(2):
            own = (lane < HD) if hh == 0 else (lane >= HD)
            s = dot(jnp.where(own, keys, jnp.zeros_like(keys)), q_t)
            s = jnp.where(valid, s, MASK_FILL)
            e = jnp.exp(s - jnp.max(s, 0, keepdims=True))
            prob = (e * (1.0 / jnp.sum(e, 0, keepdims=True))).astype(BF)
            head = 2 * i + hh
            p_buf[head] = prob
            pltpu.make_async_copy(p_buf.at[head], p_out.at[head], p_sems.at[head]).start()
            halves.append(dot(v_t[hh * HD : (hh + 1) * HD], prob))
        o_t = jnp.concatenate(halves, 0).astype(BF)
        ot_ref[lines, :] = o_t
        o_ref[:, lines] = o_t.T
        return carry

    lax.fori_loop(0, 3, pair, 0)


def attend_wait(p_buf, p_out, p_sems):
    for i in range(6):
        pltpu.make_async_copy(p_buf.at[i], p_out.at[i], p_sems.at[i]).wait()


TURNED = ((384, SEQ), BF)
HEADS = [((3, SEQ, 128), BF), ((3, SEQ, 128), BF), TURNED, TURNED]
ATTEND_SCRATCH = [
    pltpu.VMEM((6, SEQ, SEQ), BF),
    pltpu.SemaphoreType.DMA((6,)),
    pltpu.SemaphoreType.DMA((5,)),
]


def attn_first_body(meta, _, ins, outs, raw_outs, p_buf, p_sems, sems, w, q_ref, *head_refs):
    xo, xr, s12, *pieces = ins
    later, o_ref, out_w = outs
    place(meta, pieces, w)
    copies = [
        pltpu.make_async_copy(a, raw_outs[i], sems.at[i]) for i, a in enumerate([*head_refs, w])
    ]
    copies[4].start()
    t = meta[1]
    for rel in range(2):
        if rel == 0:
            targets = q_ref, head_refs[0], head_refs[1]
        else:
            targets = later.at[0], later.at[1], later.at[2]
        cols = pl.ds(pl.multiple_of((t ^ rel) * 384, 128), 384)
        bq = s12[0:1, cols]
        bv = s12[1:2, cols]
        for r, x in ((0, xo), (1, xr)):
            rows = pl.ds(r * HALF, HALF)
            qk = dot(x[...], w[rel * 2])
            q = (qk[:, :384] + bq).astype(BF) * jnp.asarray(HD**-0.5, BF)
            k = qk[:, 384:].astype(BF)
            v = (dot(x[...], w[rel * 2 + 1, :, :384]) + bv).astype(BF)
            for ref, value in zip(targets, (q, k, v)):
                for i in range(3):
                    ref[i, rows, :] = value[:, i * 128 : (i + 1) * 128]
        out_w[rel] = w[rel * 2 + 1, :, 384:]
    k_ref, v_ref, qt_ref, ot_ref = head_refs
    attend(meta, q_ref, k_ref, v_ref, qt_ref, ot_ref, o_ref, p_buf, raw_outs[5], p_sems)
    for c in copies[:4]:
        c.start()
    for c in copies:
        c.wait()
    attend_wait(p_buf, raw_outs[5], p_sems)


def attn_first(meta, xo, xr, pieces, s12):
    return kernel_call(
        attn_first_body,
        "attn_first",
        meta,
        [],
        [xo, xr, s12, *pieces],
        [((3, 3, SEQ, 128), BF), ((SEQ, 384), BF), ((2, D, 384), BF)],
        HEADS + [(W_SHAPE, BF), ((6, SEQ, SEQ), BF)],
        ATTEND_SCRATCH
        + [pltpu.VMEM(W_SHAPE, BF), pltpu.VMEM((3, SEQ, 128), BF)]
        + [pltpu.VMEM(*h) for h in HEADS],
        9.0,
    )


def attn_second_body(meta, _, ins, outs, raw_outs, p_buf, p_sems, sems, o_ref, qt_ref, ot_ref):
    xo, xr, s12, later, o_first, out_w = ins
    yh, rs, hb, shared = outs
    held = later.at[1], later.at[2], qt_ref, ot_ref
    copies = [pltpu.make_async_copy(a, raw_outs[i], sems.at[i]) for i, a in enumerate(held)]
    for c in copies[:2]:
        c.start()
    attend(
        meta,
        later.at[0],
        later.at[1],
        later.at[2],
        qt_ref,
        ot_ref,
        o_ref,
        p_buf,
        raw_outs[4],
        p_sems,
    )
    for c in copies[2:]:
        c.start()
    bo, g1, c1 = s12[2:3, :], s12[4:5, :], s12[5:6, :]
    for r, x in ((0, xo), (1, xr)):
        rows = pl.ds(r * HALF, HALF)
        a = dot_t(o_first[rows, :], out_w[0]) + dot_t(o_ref[rows, :], out_w[1])
        y = x[...].astype(F32) + a + bo
        centred = y - jnp.mean(y, -1, keepdims=True)
        inv = lax.rsqrt(jnp.mean(centred * centred, -1, keepdims=True) + EPS_NORM)
        hat = centred * inv
        yh[rows, :] = hat
        rs[rows, :] = inv
        hb[rows, :] = (hat * g1 + c1).astype(BF)
    shared[0] = ot_ref[...]
    for i in range(2):
        shared[1 + i] = hb[:, i * 384 : (i + 1) * 384].T
    for c in copies:
        c.wait()
    attend_wait(p_buf, raw_outs[4], p_sems)


def attn_second(meta, xo, xr, s12, later, o_first, out_w):
    return kernel_call(
        attn_second_body,
        "attn_second",
        meta,
        [],
        [xo, xr, s12, later, o_first, out_w],
        [((SEQ, D), F32), ((SEQ, 1), F32), ((SEQ, D), BF), ((3, 384, SEQ), BF)],
        HEADS + [((6, SEQ, SEQ), BF)],
        ATTEND_SCRATCH + [pltpu.VMEM((SEQ, 384), BF), pltpu.VMEM(*TURNED), pltpu.VMEM(*TURNED)],
        8.0,
    )


def ffn_up_body(meta, _, ins, outs, __):
    hb, s12, *pieces = ins
    f0, f1, gp, w = outs
    place(meta, pieces, w)
    for part in range(4):
        rel, half = divmod(part, 2)
        bias_row = pl.ds(8 + 2 * (meta[1] ^ rel) + half, 1)
        f_ref = (f0, f1)[rel]
        for c in range(PER_PART):
            cols = slice(c * CHUNK, (c + 1) * CHUNK)
            u = dot(hb[...], w[part, :, cols]) + s12[bias_row, cols]
            f, slope = gelu_pair(u)
            f_ref[half, :, cols] = f.astype(BF)
            gp[part, :, cols] = slope.astype(BF)


SIDE = ((2, SEQ, D), BF)
SLABS = ((2, 384, SEQ), BF)


def ffn_up(meta, hb, pieces, s12):
    return kernel_call(
        ffn_up_body,
        "ffn_up",
        meta,
        [],
        [hb, s12, *pieces],
        [SIDE, SIDE, ((4, SEQ, D), BF), (W_SHAPE, BF)],
        [],
        [],
        5.0,
    )


def norm_back(grad, hat, inv, gain):
    scaled = grad * gain
    return inv * (
        scaled
        - jnp.mean(scaled, -1, keepdims=True)
        - hat * jnp.mean(scaled * hat, -1, keepdims=True)
    )


def ffn_down_body(meta, _, ins, outs, __):
    f0, f1, yh, co, cr, s12, *pieces = ins
    out_o, out_r, dz, dz_t, dy2, sums, w = outs
    place(meta, pieces, w)
    t, length = meta[1], meta[2]
    b2 = s12[3:4, :]
    g1, c1, g2, c2 = s12[4:5, :], s12[5:6, :], s12[6:7, :], s12[7:8, :]
    fs = (f0, f1)
    for part in range(4):
        rel, half = divmod(part, 2)
        z = dot_t(fs[rel][half], w[part])
        dy2[...] = z if part == 0 else dy2[...] + z
    totals = [jnp.zeros((1, D), F32)] * 3
    for r, cot, out in ((0, co, out_o), (1, cr, out_r)):
        rows = pl.ds(r * HALF, HALF)
        y = yh[rows, :] * g1 + c1 + dy2[rows, :] + b2
        centred = y - jnp.mean(y, -1, keepdims=True)
        inv = lax.rsqrt(jnp.mean(centred * centred, -1, keepdims=True) + EPS_NORM)
        hat = centred * inv
        out[...] = (hat * g2 + c2).astype(BF)
        row = lax.broadcasted_iota(jnp.int32, (HALF, 1), 0)
        valid = row + (t ^ r) * HALF < length
        dout = jnp.where(valid, cot[...].astype(F32), 0.0)
        grad = norm_back(dout, hat, inv, g2)
        dy2[rows, :] = grad
        dz[rows, :] = grad.astype(BF)
        totals = [a + row_sum(b) for a, b in zip(totals, (grad, dout * hat, dout))]
    for i in range(3):
        sums[i : i + 1, :] = totals[i]
    for i in range(2):
        dz_t[i] = dz[:, i * 384 : (i + 1) * 384].T


def ffn_down(meta, f0, f1, pieces, yh, co, cr, s12):
    return kernel_call(
        ffn_down_body,
        "ffn_down",
        meta,
        [],
        [f0, f1, yh, co, cr, s12, *pieces],
        [
            ((HALF, D), BF),
            ((HALF, D), BF),
            ((SEQ, D), BF),
            SLABS,
            ((SEQ, D), F32),
            ((8, D), F32),
            (W_SHAPE, BF),
        ],
        [],
        [],
        5.0,
    )


def ffn_back_body(meta, _, ins, outs, __):
    dz, gp, w = ins
    du0, du1, db1 = outs
    for part in (2, 3, 0, 1):
        rel, half = divmod(part, 2)
        bias_row = pl.ds(2 * (meta[1] ^ rel) + half, 1)
        du_ref = (du0, du1)[rel]
        for c in range(PER_PART):
            cols = slice(c * CHUNK, (c + 1) * CHUNK)
            du = dot(dz[...], w[part, :, cols]) * gp[part, :, cols].astype(F32)
            db1[bias_row, cols] = row_sum(du)
            du_ref[half, :, cols] = du.astype(BF)


def ffn_back(meta, dz, w, gp):
    return kernel_call(
        ffn_back_body,
        "ffn_back",
        meta,
        [],
        [dz, gp, w],
        [SIDE, SIDE, ((4, D), F32)],
        [],
        [],
        3.5,
    )


def hidden_back(ins, outs):
    du0, du1, dy2, yh, inv, small, w = ins
    dy1, da, sums = outs
    dus = (du0, du1)
    for part in range(4):
        rel, half = divmod(part, 2)
        before = dy2 if part == 0 else dy1
        dy1[...] = before[...] + dot_t(dus[rel][half], w[part])
    g1 = small[4:5, :]
    totals = [jnp.zeros((1, D), F32)] * 3
    for r in range(2):
        rows = pl.ds(r * HALF, HALF)
        dh = dy1[rows, :]
        hat = yh[rows, :]
        grad = norm_back(dh, hat, inv[rows, :], g1)
        dy1[rows, :] = grad
        da[rows, :] = grad.astype(BF)
        totals = [a + row_sum(b) for a, b in zip(totals, (grad, dh * hat, dh))]
    for i in range(3):
        sums[i : i + 1, :] = totals[i]


class AttnBack:
    SCRATCH = [
        pltpu.VMEM((D, D), BF),
        pltpu.VMEM((6, SEQ, SEQ), BF),
        pltpu.SemaphoreType.DMA((6,)),
        pltpu.SemaphoreType.DMA((5,)),
        pltpu.VMEM((3, 128, SEQ), BF),
        pltpu.VMEM((3, 128, SEQ), BF),
    ] + [pltpu.VMEM(*h) for h in HEADS]

    def __init__(self, rel, raw, scratch):
        *head_in, w_in, self.p_in = raw
        self.w, self.p_buf, self.p_sems, sems, self.do_t, self.k_t, *self.heads = scratch
        self.copies = [pltpu.make_async_copy(w_in.at[rel * 2 + 1], self.w, sems.at[4])]
        self.copies += [
            pltpu.make_async_copy(a, b, sems.at[i])
            for i, (a, b) in enumerate(zip(head_in, self.heads))
        ]

    def start(self):
        for c in self.copies:
            c.start()
        for i in range(6):
            pltpu.make_async_copy(self.p_in.at[i], self.p_buf.at[i], self.p_sems.at[i]).start()

    def run(self, da, dq, dk, dv, sums):
        w, do_t_ref, k_t_ref = self.w, self.do_t, self.k_t
        k_ref, v_ref, qt_ref, ot_ref = self.heads
        for c in self.copies:
            c.wait()
        do = dot(da[...], w[:, 384:]).astype(BF)
        for i in range(3):
            do_t_ref[i] = do[:, i * 128 : (i + 1) * 128].T
            k_t_ref[i] = k_ref[i].T
        lane = lax.broadcasted_iota(jnp.int32, (SEQ, 128), 1)

        def pair(i, carry):
            vp = v_ref[i]
            do_t = do_t_ref[i]
            base = pl.multiple_of(i * 128, 128)
            both = do_t.astype(F32) * ot_ref[pl.ds(base, 128), :].astype(F32)
            for hh in range(2):
                own = (lane < HD) if hh == 0 else (lane >= HD)
                inside = slice(hh * HD, (hh + 1) * HD)
                delta = row_sum(both[inside])
                slope = dot(jnp.where(own, vp, jnp.zeros_like(vp)), do_t)
                head = 2 * i + hh
                pltpu.make_async_copy(
                    self.p_in.at[head], self.p_buf.at[head], self.p_sems.at[head]
                ).wait()
                prob = self.p_buf[head]
                ds = (prob.astype(F32) * (slope - delta)).astype(BF)
                lines = pl.ds(base + hh * HD, HD)
                dv[lines, :] = dot_t(do_t[inside], prob).astype(BF)
                dk[lines, :] = dot_t(qt_ref[lines, :], ds).astype(BF)
                dq[lines, :] = (dot(k_t_ref[i, inside, :], ds) * (HD**-0.5)).astype(BF)
            return carry

        lax.fori_loop(0, 3, pair, 0)
        ones = jnp.ones((8, SEQ), BF)
        sums[0:8, :] = dot_t(ones, dq[...])
        sums[8:16, :] = dot_t(ones, dv[...])


LINES = SMALL // 128


def put_lines(vec, first, row):
    for i in range(row.shape[1] // 128):
        vec[pl.ds(first + i, 1), :] = row[:, i * 128 : (i + 1) * 128]


def frames_back_body(meta, raw, ins, outs, _, total, w, dy1, sem):
    grads = ins
    copies = [pltpu.make_async_copy(raw[0].at[i], w.at[i], sem.at[i]) for i in range(4)]
    copies.append(pltpu.make_async_copy(raw[1], dy1, sem.at[4]))
    for c in copies:
        c.start()
    for c in copies:
        c.wait()
    for m in range(3):
        rows = pl.ds(m * 256, 256)
        acc = None
        for rel in range(2):
            for side, left in enumerate(
                (w[rel * 2, rows, :384], w[rel * 2, rows, 384:], w[rel * 2 + 1, rows, :384])
            ):
                term = dot(left, grads[rel][side])
                acc = term if acc is None else acc + term
        total[rows, :] = acc
    for r in range(2):
        rows = pl.ds(r * HALF, HALF)
        outs[r][...] = dy1[rows, :] + total[:, r * HALF : (r + 1) * HALF].T


def frames_back(meta, dy1, turned, w):
    return kernel_call(
        frames_back_body,
        "frames_back",
        meta,
        [w, dy1],
        turned,
        [((HALF, D), F32)] * 2,
        [],
        [
            pltpu.VMEM((D, SEQ), F32),
            pltpu.VMEM(W_SHAPE, BF),
            pltpu.VMEM((SEQ, D), F32),
            pltpu.SemaphoreType.DMA((5,)),
        ],
        3.5,
    )


def near_body(meta, _, ins, outs, __):
    for half in range(2):
        keep, came = ins[half], ins[2 + half]
        for i in range(4):
            outs[2 + half][i] = (keep[4 + i].astype(F32) + came[4 + i].astype(F32)).astype(BF)
            outs[half][i] = (keep[i].astype(F32) + came[i].astype(F32)).astype(BF)


def near_sums(meta, keep, came):
    outs = kernel_call(
        near_body, "near_sums", meta, [], [*keep, *came], [((4, ROWS, D), BF)] * 4, [], [], 0.5
    )
    return outs[:2], outs[2:]


def z_body(meta, _, ins, outs, __):
    for half in range(2):
        keep, came = ins[half], ins[2 + half]
        cols = slice(half * D, (half + 1) * D)
        for i in range(4):
            outs[i][:, cols] = (keep[i].astype(F32) + came[i].astype(F32)).astype(outs[i].dtype)


ROW = (ROWS, 2 * D)


def z_sums(meta, keep, came):
    return kernel_call(
        z_body, "z_sums", meta, [], [*keep, *came], [(ROW, F32)] + [(ROW, BF)] * 3, [], [], 4.0
    )


def totals_body(meta, _, ins, outs, __):
    count = ins[0]
    grads, vec = outs
    square = jnp.zeros((1, 1), F32)
    for k in range(3):
        row, *came = ins[1 + 4 * k : 5 + 4 * k]
        total = row[...]
        for c in came:
            total = total + c[...].astype(F32)
        grads[k] = total
        square = square + jnp.sum(row_sum(total * total), 1, keepdims=True)
    lane = lax.broadcasted_iota(jnp.int32, (8, 128), 1)
    vec[...] = jnp.where(lane == 0, square, jnp.where(lane == 1, count[...], 0.0))


def totals(meta, count, parts):
    return kernel_call(
        totals_body,
        "totals",
        meta,
        [],
        [count, *parts],
        [((3, *parts[0].shape), F32), ((8, 128), F32)],
        [],
        [],
        1.0,
    )


def adamw_body(meta, raw, ins, outs, raw_outs, *scratch):
    square, vec, grads, small_w, small_m, small_v, aw, am, av, fw, fm, fv = ins
    norm_out, small_out = outs[0], outs[1:]
    new_a, new_f, sems = scratch
    frame_count = square[0:1, 1:2]
    small = vec[...]
    squares = square[0:1, 0:1] + jnp.sum(row_sum(small * small), 1, keepdims=True)
    norm = jnp.sqrt(squares) / frame_count
    norm_out[...] = norm
    factor = jnp.minimum(1.0, CLIP_NORM / norm) / frame_count
    copies = []
    for i in range(4):
        cols = slice((i % 2) * 384 + (i // 2) * D, (i % 2) * 384 + (i // 2) * D + 384)
        rate = RATE * 0.5 * SEQ**0.5 if i == 3 else RATE
        for k, v in enumerate(adamw(aw[i], am[i], av[i], grads[0, :, cols] * factor, rate, DECAY)):
            new_a[k, i] = v
    for k in range(3):
        copies.append(pltpu.make_async_copy(new_a.at[k], raw_outs[k], sems.at[k]))
        copies[-1].start()
    for i in range(2):
        for k, v in enumerate(adamw(fw[i], fm[i], fv[i], grads[1 + i] * factor, RATE, DECAY)):
            new_f[k, i] = v
    for k in range(3):
        copies.append(pltpu.make_async_copy(new_f.at[k], raw_outs[3 + k], sems.at[3 + k]))
        copies[-1].start()
    new_small = adamw(small_w[...], small_m[...], small_v[...], small * factor, SMALL_RATE, 0.0)
    for out, v in zip(small_out, new_small):
        out[...] = v
    for c in copies:
        c.wait()


def adamw_call(meta, square, vec, grads, small, state):
    shapes = [v.shape for v in state]
    return kernel_call(
        adamw_body,
        "adamw",
        meta,
        [],
        [square, vec, grads, *small, *state],
        [((1, 1), F32)] + [((LINES, 128), F32)] * 3,
        [(s, F32) for s in shapes],
        [
            pltpu.VMEM((3, *shapes[0]), F32),
            pltpu.VMEM((3, *shapes[3]), F32),
            pltpu.SemaphoreType.DMA((6,)),
        ],
        3.0,
    )


def put_out(meta, acc, outs, half):
    d = meta[0]
    for sel in range(2):
        for j in range(8):
            row = pl.multiple_of((d ^ MASKS[half][sel][j]) * ROWS, 16)
            outs[half * 2 + sel][j] = acc[half, pl.ds(row, ROWS), :]


GRAD_OUTS = [((8, ROWS, D), BF)] * 4
GRAD_SCRATCH = [pltpu.VMEM((2, D, D), BF)]


def ffn_grad(meta, left_o, left_r, right_o, right_r, outs, acc):
    for half in range(2):
        for i in range(2):
            total = dot(left_o[i], right_o[half]) + dot(left_r[i], right_r[half])
            acc[half, i * 384 : (i + 1) * 384, :] = total.astype(BF)
        put_out(meta, acc, outs, half)


def down_grad_body(meta, _, ins, outs, __, acc):
    dz_o, dz_r, f_o, f_r = ins
    ffn_grad(meta, dz_o, dz_r, f_o, f_r, outs, acc)


def down_grad_call(meta, *ins):
    return kernel_call(
        down_grad_body, "down_grad", meta, [], ins, GRAD_OUTS, [], GRAD_SCRATCH, 4.0
    )


def middle_body(meta, raw, ins, outs, raw_outs, acc, grads, dy1, da, out_sems, *scratch):
    attn = AttnBack(1, raw, scratch)
    attn.start()
    shared, shared_r, du0, du_r, *rest = ins
    sums_one, sent, qv = outs
    copies = [
        pltpu.make_async_copy(a, b, out_sems.at[i])
        for i, (a, b) in enumerate(zip([*[grads.at[i] for i in range(4)], dy1, da], raw_outs))
    ]
    ffn_grad(
        meta,
        shared.at[pl.ds(1, 2)],
        shared_r.at[pl.ds(1, 2)],
        du0,
        du_r,
        [grads.at[i] for i in range(4)],
        acc,
    )
    for c in copies[:4]:
        c.start()
    hidden_back([du0, *rest], (dy1, da, sums_one))
    for c in copies[4:]:
        c.start()
    for i in range(2):
        sent[3 + i] = da[:, i * 384 : (i + 1) * 384].T
    attn.run(da, sent.at[0], sent.at[1], sent.at[2], qv)
    for c in copies:
        c.wait()


def middle(meta, heads, w_attn, prob, shared, shared_r, du0, du_r, du1, dy2, yh, inv, s12, w):
    return kernel_call(
        middle_body,
        "up_grad_hidden_back_attn_back",
        meta,
        [*heads, w_attn, prob],
        [shared, shared_r, du0, du_r, du1, dy2, yh, inv, s12, w],
        [((8, D), F32), ((5, 384, SEQ), BF), ((16, 384), F32)],
        GRAD_OUTS + [((SEQ, D), F32), ((SEQ, D), BF)],
        GRAD_SCRATCH
        + [
            pltpu.VMEM((4, 8, ROWS, D), BF),
            pltpu.VMEM((SEQ, D), F32),
            pltpu.VMEM((SEQ, D), BF),
            pltpu.SemaphoreType.DMA((6,)),
        ]
        + AttnBack.SCRATCH,
        14.0,
    )


def attn_back_body(meta, raw, ins, outs, _, da, da_sem, *scratch):
    da_copy = pltpu.make_async_copy(raw[0], da, da_sem.at[0])
    da_copy.start()
    attn = AttnBack(0, raw[1:], scratch)
    attn.start()
    turned, qv = outs
    da_copy.wait()
    attn.run(da, turned.at[0], turned.at[1], turned.at[2], qv)


def attn_back(meta, heads, w_attn, prob, da):
    return kernel_call(
        attn_back_body,
        "attn_back",
        meta,
        [da, *heads, w_attn, prob],
        [],
        [((3, 384, SEQ), BF), ((16, 384), F32)],
        [],
        [pltpu.VMEM((SEQ, D), BF), pltpu.SemaphoreType.DMA((1,))] + AttnBack.SCRATCH,
        7.0,
    )


def attn_grad_body(meta, _, ins, outs, __, acc, x_t):
    xo, xr, zo, zr, turned, sent, sent_r, o_own, shared_r = ins[:9]
    qv0, qv1, sums_one, sums_two, db1 = ins[9:]
    vec = outs[4]
    for rel, qv in ((0, qv0), (1, qv1)):
        h = meta[1] ^ rel
        put_lines(vec, 3 * h, qv[0:1, :])
        put_lines(vec, 6 + 3 * h, qv[8:9, :])
    for line, sums, row in (
        (2, sums_one, 0),
        (3, sums_two, 0),
        (4, sums_one, 1),
        (5, sums_one, 2),
        (6, sums_two, 1),
        (7, sums_two, 2),
    ):
        put_lines(vec, 6 * line, sums[row : row + 1, :])
    for i in range(4):
        put_lines(vec, 48 + 6 * i, db1[i : i + 1, :])
    for i, v in enumerate((xo, xr, zo, zr)):
        x_t[:, i * HALF : (i + 1) * HALF] = v[...].T
    for half, side, k in ((1, 0, 2), (0, 0, 0), (0, 1, 1)):
        for m in range(3):
            rows = pl.ds(m * 256, 256)
            total = dot_t(x_t[rows, :SEQ], turned[k]) + dot_t(x_t[rows, SEQ:], sent_r[k])
            acc[half, rows, side * 384 : (side + 1) * 384] = total.astype(BF)
    for i in range(2):
        total = dot_t(sent[3 + i], o_own[...]) + dot_t(sent_r[3 + i], shared_r[0])
        acc[1, i * 384 : (i + 1) * 384, 384:] = total.astype(BF)
    for half in range(2):
        put_out(meta, acc, outs, half)


def attn_grad(meta, xs, turned, sent, sent_r, o_own, shared_r, small):
    return kernel_call(
        attn_grad_body,
        "attn_grad",
        meta,
        [],
        [*xs, turned, sent, sent_r, o_own, shared_r, *small],
        GRAD_OUTS + [((LINES, 128), F32)],
        [],
        GRAD_SCRATCH + [pltpu.VMEM((D, 2 * SEQ), BF)],
        5.0,
    )


def adamw(weight, moment_one, moment_two, grad, rate, decay):
    new_one = BETA_ONE * moment_one + (1.0 - BETA_ONE) * grad
    new_two = BETA_TWO * moment_two + (1.0 - BETA_TWO) * grad * grad
    fixed_one = new_one / (1.0 - BETA_ONE**STEP)
    fixed_two = new_two / (1.0 - BETA_TWO**STEP)
    update = fixed_one / (jnp.sqrt(fixed_two) + ADAM_EPS) + decay * weight
    return (weight - rate * update, new_one, new_two)


def after(v, *deps):
    return lax.optimization_barrier((v, *deps))[0]


def other_core(v):
    return lax.ppermute(v, "tensor", [(0, 1), (1, 0)])


def shift(v, mask, n):
    return lax.ppermute(v, "dp", [(i, i ^ mask) for i in range(n)])


class Gather:
    def __init__(self, shard, n):
        self.n, self.shard, self.mark = n, shard, shard

    def z_all(self, *deps):
        if self.n == BLOCKS:
            shard = after(self.shard, *deps)
            self.z = [shard] + [shift(shard, z, self.n) for z in Z_MASKS[1:]]
            self.mark = shard

    def z_wait(self, *deps):
        if self.n == BLOCKS:
            self.z = after(tuple(self.z), *deps)
            self.mark = self.z[1:]

    def far_wait(self, *deps):
        if self.n == BLOCKS:
            self.far_side = after(tuple(self.far_side), *deps)
            self.mark = tuple(self.far_side)

    def near_wait(self, *deps):
        if self.n == BLOCKS:
            self.came = after(tuple(self.came), *deps)
            self.mark = tuple(self.came)

    def near(self, *deps):
        if self.n != BLOCKS:
            return
        parts = after(tuple(self.z), *deps)
        self.own = [
            jnp.stack([v[:, half * D : (half + 1) * D] for v in parts]) for half in range(2)
        ]
        self.mark = tuple(self.own)
        self.came = [shift(s, step[0], self.n) for s, step in zip(self.own, (STEP_A, STEP_B))]

    def far(self, *deps):
        if self.n != BLOCKS:
            return
        came = after(tuple(self.came), *deps)
        self.own = [jnp.concatenate([s, c]) for s, c in zip(self.own, came)]
        self.mark = tuple(self.own)
        self.far_side = [shift(o, step[1], self.n) for o, step in zip(self.own, (STEP_A, STEP_B))]

    def core(self, *deps):
        if self.n == BLOCKS:
            self.own_other = [other_core(o) for o in after(tuple(self.own), *deps)]
            self.mark = tuple(self.own_other)

    def pieces(self, *deps):
        if self.n == BLOCKS:
            far = after(tuple(self.far_side), *deps)
            result = []
            for half in range(2):
                far_other = other_core(far[half])
                result += [self.own[half], far[half], self.own_other[half], far_other]
            self.mark = far[1]
            return result
        full = lax.all_gather(self.shard, "dp", axis=0, tiled=True)
        blocks = full.reshape(BLOCKS, ROWS, 2 * D)
        result = []
        for half in range(2):
            cols = slice(half * D, (half + 1) * D)
            own = [blocks[jnp.array(m), :, cols] for m in MASKS[half]]
            result += own + [other_core(v) for v in own]
        return result


def added(*parts):
    total = parts[0].astype(F32)
    for p in parts[1:]:
        total = total + p.astype(F32)
    return total


class Scatter:
    def __init__(self, meta, pieces, n):
        self.meta = meta
        self.n, self.pieces, self.mark = n, pieces, pieces[0]
        if n == BLOCKS:
            self.keep = [pieces[0], pieces[2]]
            self.came = [
                shift(v, step[1], n) for v, step in zip((pieces[1], pieces[3]), (STEP_A, STEP_B))
            ]

    def near(self, *deps):
        if self.n != BLOCKS:
            return
        came = after(tuple(self.came), *deps)
        self.keep, send = near_sums(self.meta, self.keep, came)
        self.came = [shift(s, step[0], self.n) for s, step in zip(send, (STEP_A, STEP_B))]
        self.mark = tuple(send)

    def wait(self, *deps):
        if self.n == BLOCKS:
            self.came = after(tuple(self.came), *deps)
            self.mark = tuple(self.came)

    def z_all(self, *deps):
        if self.n != BLOCKS:
            return
        came = after(tuple(self.came), *deps)
        self.row, *sends = z_sums(self.meta, self.keep, came)
        self.mark = tuple(sends)
        self.came = [shift(s, z, self.n) for s, z in zip(sends, Z_MASKS[1:])]

    def parts(self, *deps):
        if self.n == BLOCKS:
            return [self.row, *after(tuple(self.came), *deps)]
        whole = self.whole()
        zero = jnp.zeros(whole.shape, BF)
        return [whole, zero, zero, zero]

    def whole(self):
        result = []
        for half in range(2):
            order = MASKS[half][0] + MASKS[half][1]
            back = [order.index(i) for i in range(BLOCKS)]
            full = jnp.concatenate(self.pieces[2 * half : 2 * half + 2])[jnp.array(back)]
            full = full.reshape(D, D).astype(F32)
            result.append(lax.psum_scatter(full, "dp", scatter_dimension=0, tiled=True))
        return jnp.concatenate(result, 1)


class Everywhere:
    def __init__(self, v, n):
        self.n, self.v = n, v

    def core(self, *deps):
        if self.n == BLOCKS:
            v = after(self.v, *deps)
            self.v = v + other_core(v)

    def step(self, masks, *deps):
        if self.n == BLOCKS:
            v = after(self.v, *deps)
            came = [shift(v, m, self.n) for m in masks]
            self.v = v + came[0] if len(came) == 1 else (v + came[0]) + (came[1] + came[2])

    def total(self):
        return self.v if self.n == BLOCKS else lax.psum(self.v, ("dp", "tensor"))


XY_MASKS = (1, 2, 3)


def last_steps(small, every):
    if every.n != BLOCKS:
        return small.total(), every.total()
    lines = every.v.shape[0]
    every.v = jnp.concatenate([every.v, small.v])
    every.step(XY_MASKS)
    v = every.v[:lines]
    near, both, far = [
        shift(s, m, every.n) for s, m in zip((v, every.v, v), Z_MASKS[1:])
    ]
    return every.v[lines:] + both[lines:], (v + near) + (both[:lines] + far)


def per_device(
    frames,
    cotangent,
    lengths,
    attn_w,
    attn_m,
    attn_v,
    ffn_w,
    ffn_m,
    ffn_v,
    small_w,
    small_m,
    small_v,
):
    n = lax.axis_size("dp")
    t = lax.axis_index("tensor")
    d = lax.axis_index("dp") if n == BLOCKS else 0
    length = lax.dynamic_index_in_dim(lengths[:, 0], t, 0, keepdims=False)
    meta = jnp.stack([jnp.asarray(d, jnp.int32), jnp.asarray(t, jnp.int32), length])
    s12 = small_w.reshape(12, D)
    half = SEQ // lax.axis_size("tensor")
    count = jnp.sum(jnp.clip(lengths - t * half, 0, half)).astype(F32).reshape(1, 1)

    def pick(v, i):
        return lax.dynamic_index_in_dim(v[:, 0], i, 0, keepdims=False)

    def joined(own, other):
        return jnp.where(t == 0, jnp.stack([own, other]), jnp.stack([other, own]))[:, None]

    attn = Gather(jnp.concatenate([attn_w[i] for i in range(4)], 1).astype(BF), n)
    up = Gather(ffn_w[0].astype(BF), n)
    down = Gather(ffn_w[1].astype(BF), n)
    attn.z_all()
    frames_r = other_core(frames)
    xo, zr = pick(frames, t), pick(frames, 1 - t)
    xr, zo = pick(frames_r, t), pick(frames_r, 1 - t)
    cotangent_r = other_core(cotangent)
    co, cr = pick(cotangent, t), pick(cotangent_r, t)
    attn.near(xr, cr)
    up.z_all(attn.mark)
    attn.far()
    up.near(attn.mark)
    attn.core()
    attn_pieces = attn.pieces(up.mark)
    down.z_all(attn.mark)
    up.far(attn.mark)
    first = attn_first(after(meta, up.mark, down.mark, count), xo, xr, attn_pieces, s12)
    later, o_first, out_w, *heads_first = first
    *heads_first, w_attn, prob_first = heads_first
    down.near(o_first)
    second = attn_second(after(meta, down.mark), xo, xr, s12, later, o_first, out_w)
    yh, inv, hb, shared, *heads_second = second
    *heads_second, prob_second = heads_second
    heads, prob = (heads_first, heads_second), (prob_first, prob_second)
    down.near_wait(inv)
    up.far_wait(inv)
    up.core(down.mark)
    up_pieces = up.pieces()
    down.far()
    down_far = down.mark
    down.core(up_pieces[1], up_pieces[3])
    f0, f1, gp, w_up = ffn_up(after(meta, down_far), hb, up_pieces, s12)
    down.far_wait(gp)
    down_pieces = down.pieces()
    f_r = other_core(after(f1, *down_pieces))
    shared_r = other_core(after(shared, *down_pieces))
    out_o, out_r, dz, dz_t, dy2, sums_two, w_down = ffn_down(
        meta, f0, f1, down_pieces, yh, co, cr, s12
    )
    dz_r = other_core(after(dz_t, f_r, shared_r))
    du0, du1, db1 = ffn_back(after(meta, f_r, shared_r), dz, w_down, gp)
    du_r = other_core(after(du1, dz_r))
    down_sum = Scatter(
        meta,
        down_grad_call(after(meta, db1), dz_t, dz_r, f0, f_r), n
    )
    *up_grad, dy1, da = middle(
        after(meta, down_sum.mark),
        heads[1],
        w_attn,
        prob[1],
        shared,
        shared_r,
        du0,
        du_r,
        du1,
        dy2,
        yh,
        inv,
        s12,
        w_up,
    )
    sums_one, sent, qv1, *up_grad = up_grad
    down_sum.wait(qv1)
    up_sum = Scatter(meta, after(tuple(up_grad), down_sum.mark), n)
    down_sum.near()
    sent_r = other_core(after(sent, down_sum.mark))
    turned0, qv0 = attn_back(after(meta, down_sum.mark), heads[0], w_attn, prob[0], da)
    down_sum.z_all(qv0, sent_r)
    *attn_grads, vec = attn_grad(
        after(meta, down_sum.mark),
        (xo, xr, zo, zr),
        turned0,
        sent,
        sent_r,
        heads[0][3],
        shared_r,
        (qv0, qv1, sums_one, sums_two, db1),
    )
    up_sum.wait(attn_grads[0])
    up_sum.near()
    down_sum.wait(up_sum.mark)
    small = Everywhere(vec, n)
    attn_sum = Scatter(meta, after(tuple(attn_grads), down_sum.mark), n)
    small.core(down_sum.mark)
    small.step((4,))
    up_sum.wait()
    up_sum.z_all(small.v)
    small_state = [v.reshape(LINES, 128) for v in (small_w, small_m, small_v)]
    attn_sum.near(up_sum.mark)
    dx_o, dx_r = frames_back(after(meta, attn_sum.mark), dy1, (turned0, sent), w_attn)
    attn_sum.wait(dx_o)
    up_sum.wait(dx_o)
    attn_sum.z_all(up_sum.mark)
    dx_other = other_core(after(dx_r, attn_sum.mark))
    out_other = other_core(after(out_r, attn_sum.mark))
    frames_grad = joined(dx_o, dx_other)
    output = joined(out_o, out_other)
    grads, square = totals(
        meta, count, attn_sum.parts(frames_grad, output) + up_sum.parts() + down_sum.parts()
    )
    every = Everywhere(square, n)
    every.core()
    small_all, square_all = last_steps(small, every)
    state = (attn_w, attn_m, attn_v, ffn_w, ffn_m, ffn_v)
    norm, small_new, small_m_new, small_v_new, *new_state = adamw_call(
        meta, square_all, small_all, grads, small_state, state
    )
    attn_new, attn_m_new, attn_v_new, ffn_new, ffn_m_new, ffn_v_new = new_state
    grad_norm = norm[0, 0]
    small_new, small_m_new, small_v_new = [
        v.reshape(SMALL) for v in (small_new, small_m_new, small_v_new)
    ]
    return (
        output,
        frames_grad,
        grad_norm,
        attn_new,
        attn_m_new,
        attn_v_new,
        ffn_new,
        ffn_m_new,
        ffn_v_new,
        small_new,
        small_m_new,
        small_v_new,
    )


def solution(mesh):
    rows = P(None, "dp", "tensor", None)
    weights = P(None, "dp", "tensor")
    in_specs = (rows, rows, P(None, "dp")) + (weights,) * 6 + (P(),) * 3
    out_specs = (rows, rows, P()) + (weights,) * 6 + (P(),) * 3
    return jax.shard_map(
        per_device, mesh=mesh, in_specs=in_specs, out_specs=out_specs, check_vma=False
    )
```

```python
import math

import jax
import jax.numpy as jnp
from jax import lax
from jax.experimental import pallas as pl
from jax.experimental.pallas import tpu as pltpu
from jax.sharding import PartitionSpec as P

HD = 64
D = 768
FF = 3072
SEQ = 512
HALF = SEQ // 2
STEP = 10
SMALL = 9216
PAIRS = 6
BLOCKS = 16
ROWS = D // BLOCKS

EPS_NORM = 1e-05
MASK_FILL = -1e30
BETA_ONE = 0.9
BETA_TWO = 0.999
ADAM_EPS = 1e-08
CLIP_NORM = 0.1
RATE = 0.1
SMALL_RATE = 1.5
DECAY = 0.01

BF = jnp.bfloat16
F32 = jnp.float32

STEP_A = (2, 1)
STEP_B = (1, 2)
Z_MASKS = (0, 4, 8, 12)
MASKS = tuple(
    (
        tuple(z for z in Z_MASKS) + tuple(z + near for z in Z_MASKS),
        tuple(z + far for z in Z_MASKS) + tuple(z + near + far for z in Z_MASKS),
    )
    for near, far in (STEP_A, STEP_B)
)


def dot(left, right):
    return jnp.dot(left, right, preferred_element_type=F32)


def dot_t(left, right):
    return lax.dot_general(left, right, (((1,), (1,)), ((), ())), preferred_element_type=F32)


def gelu_pair(u):
    phi = 0.5 * lax.erf(u * math.sqrt(0.5)) + 0.5
    return u * phi, phi + u * jnp.exp(-0.5 * u * u) * (1.0 / math.sqrt(2.0 * math.pi))


HBM = pl.BlockSpec(memory_space=pltpu.HBM)
SMEM = pl.BlockSpec(memory_space=pltpu.SMEM)


VMEM = pl.BlockSpec(memory_space=pltpu.VMEM)


def kernel_call(body, name, meta, raw, ins, outs, raw_outs, scratch, micros):
    n_raw, n_in, n_out, n_raw_out = len(raw), len(ins), len(outs), len(raw_outs)

    def run(meta_ref, *refs):
        cuts = [0, n_raw, n_in, n_out, n_raw_out]
        for i in range(1, 5):
            cuts[i] += cuts[i - 1]
        groups = [refs[cuts[i] : cuts[i + 1]] for i in range(4)]
        body(meta_ref, *groups, *refs[cuts[4] :])

    held = sum(
        math.prod(v.shape) * (2 if v.dtype == BF else 4) for v in scratch if v.dtype in (BF, F32)
    )
    return pl.pallas_call(
        run,
        name=name,
        in_specs=[SMEM] + [HBM] * n_raw + [VMEM] * n_in,
        out_specs=[VMEM] * n_out + [HBM] * n_raw_out,
        out_shape=[jax.ShapeDtypeStruct(s, d) for s, d in outs]
        + [pltpu.HBM(s, d) for s, d in raw_outs],
        scratch_shapes=scratch,
        compiler_params=pltpu.CompilerParams(vmem_limit_bytes=held + SPARE),
        cost_estimate=pl.CostEstimate(
            flops=int(micros * 1.15e9), bytes_accessed=0, transcendentals=0
        ),
    )(meta, *[pltpu.with_memory_space_constraint(v, pltpu.HBM) for v in raw], *ins)


SPARE = 8 * 2**20
W_SHAPE = (4, D, D)


def place(meta, pieces, w):
    d = meta[0]
    for part in range(4):
        rel, half = divmod(part, 2)
        for sel in range(2):
            src = pieces[half * 4 + rel * 2 + sel]
            for j in range(8):
                row = pl.multiple_of((d ^ MASKS[half][sel][j]) * ROWS, 16)
                w[part, pl.ds(row, ROWS), :] = src[j]


def chunk(c):
    return pl.ds(pl.multiple_of(c * CHUNK, CHUNK), CHUNK)


CHUNK = 256
PER_PART = D // CHUNK


def row_sum(v):
    return jnp.sum(v, 0, keepdims=True)


def attend(meta, q_ref, k_ref, v_ref, qt_ref, ot_ref, o_ref, p_buf, p_out, p_sems):
    t, length = meta[1], meta[2]
    row = lax.broadcasted_iota(jnp.int32, (SEQ, 1), 0)
    position = jnp.where(row < HALF, row + t * HALF, row + (1 - t) * HALF - HALF)
    valid = position < length
    lane = lax.broadcasted_iota(jnp.int32, (SEQ, 128), 1)

    def pair(i, carry):
        keys = k_ref[i]
        q_t = q_ref[i].T
        lines = pl.ds(pl.multiple_of(i * 128, 128), 128)
        qt_ref[lines, :] = q_t
        v_t = v_ref[i].T
        halves = []
        for hh in range(2):
            own = (lane < HD) if hh == 0 else (lane >= HD)
            s = dot(jnp.where(own, keys, jnp.zeros_like(keys)), q_t)
            s = jnp.where(valid, s, MASK_FILL)
            e = jnp.exp(s - jnp.max(s, 0, keepdims=True))
            prob = (e * (1.0 / jnp.sum(e, 0, keepdims=True))).astype(BF)
            head = 2 * i + hh
            p_buf[head] = prob
            pltpu.make_async_copy(p_buf.at[head], p_out.at[head], p_sems.at[head]).start()
            halves.append(dot(v_t[hh * HD : (hh + 1) * HD], prob))
        o_t = jnp.concatenate(halves, 0).astype(BF)
        ot_ref[lines, :] = o_t
        o_ref[:, lines] = o_t.T
        return carry

    lax.fori_loop(0, 3, pair, 0, unroll=True)


def attend_wait(p_buf, p_out, p_sems):
    for i in range(6):
        pltpu.make_async_copy(p_buf.at[i], p_out.at[i], p_sems.at[i]).wait()


TURNED = ((384, SEQ), BF)
HEADS = [((3, SEQ, 128), BF), ((3, SEQ, 128), BF), TURNED, TURNED]
ATTEND_SCRATCH = [
    pltpu.VMEM((6, SEQ, SEQ), BF),
    pltpu.SemaphoreType.DMA((6,)),
    pltpu.SemaphoreType.DMA((5,)),
]


def attn_first_body(meta, _, ins, outs, raw_outs, p_buf, p_sems, sems, w, q_ref, *head_refs):
    xo, xr, s12, *pieces = ins
    later, o_ref, out_w = outs
    place(meta, pieces, w)
    copies = [
        pltpu.make_async_copy(a, raw_outs[i], sems.at[i]) for i, a in enumerate([*head_refs, w])
    ]
    copies[4].start()
    t = meta[1]
    for rel in range(2):
        if rel == 0:
            targets = q_ref, head_refs[0], head_refs[1]
        else:
            targets = later.at[0], later.at[1], later.at[2]
        cols = pl.ds(pl.multiple_of((t ^ rel) * 384, 128), 384)
        bq = s12[0:1, cols]
        bv = s12[1:2, cols]
        for r, x in ((0, xo), (1, xr)):
            rows = pl.ds(r * HALF, HALF)
            qk = dot(x[...], w[rel * 2])
            q = (qk[:, :384] + bq).astype(BF) * jnp.asarray(HD**-0.5, BF)
            k = qk[:, 384:].astype(BF)
            v = (dot(x[...], w[rel * 2 + 1, :, :384]) + bv).astype(BF)
            for ref, value in zip(targets, (q, k, v)):
                for i in range(3):
                    ref[i, rows, :] = value[:, i * 128 : (i + 1) * 128]
        out_w[rel] = w[rel * 2 + 1, :, 384:]
    k_ref, v_ref, qt_ref, ot_ref = head_refs
    attend(meta, q_ref, k_ref, v_ref, qt_ref, ot_ref, o_ref, p_buf, raw_outs[5], p_sems)
    for c in copies[:4]:
        c.start()
    for c in copies:
        c.wait()
    attend_wait(p_buf, raw_outs[5], p_sems)


def attn_first(meta, xo, xr, pieces, s12):
    return kernel_call(
        attn_first_body,
        "attn_first",
        meta,
        [],
        [xo, xr, s12, *pieces],
        [((3, 3, SEQ, 128), BF), ((SEQ, 384), BF), ((2, D, 384), BF)],
        HEADS + [(W_SHAPE, BF), ((6, SEQ, SEQ), BF)],
        ATTEND_SCRATCH
        + [pltpu.VMEM(W_SHAPE, BF), pltpu.VMEM((3, SEQ, 128), BF)]
        + [pltpu.VMEM(*h) for h in HEADS],
        9.0,
    )


def attn_second_body(meta, _, ins, outs, raw_outs, p_buf, p_sems, sems, o_ref, qt_ref, ot_ref):
    xo, xr, s12, later, o_first, out_w = ins
    yh, rs, hb, shared = outs
    held = later.at[1], later.at[2], qt_ref, ot_ref
    copies = [pltpu.make_async_copy(a, raw_outs[i], sems.at[i]) for i, a in enumerate(held)]
    for c in copies[:2]:
        c.start()
    attend(
        meta,
        later.at[0],
        later.at[1],
        later.at[2],
        qt_ref,
        ot_ref,
        o_ref,
        p_buf,
        raw_outs[4],
        p_sems,
    )
    for c in copies[2:]:
        c.start()
    bo, g1, c1 = s12[2:3, :], s12[4:5, :], s12[5:6, :]
    for r, x in ((0, xo), (1, xr)):
        rows = pl.ds(r * HALF, HALF)
        a = dot_t(o_first[rows, :], out_w[0]) + dot_t(o_ref[rows, :], out_w[1])
        y = x[...].astype(F32) + a + bo
        centred = y - jnp.mean(y, -1, keepdims=True)
        inv = lax.rsqrt(jnp.mean(centred * centred, -1, keepdims=True) + EPS_NORM)
        hat = centred * inv
        yh[rows, :] = hat
        rs[rows, :] = inv
        hb[rows, :] = (hat * g1 + c1).astype(BF)
    shared[0] = ot_ref[...]
    for i in range(2):
        shared[1 + i] = hb[:, i * 384 : (i + 1) * 384].T
    for c in copies:
        c.wait()
    attend_wait(p_buf, raw_outs[4], p_sems)


def attn_second(meta, xo, xr, s12, later, o_first, out_w):
    return kernel_call(
        attn_second_body,
        "attn_second",
        meta,
        [],
        [xo, xr, s12, later, o_first, out_w],
        [((SEQ, D), F32), ((SEQ, 1), F32), ((SEQ, D), BF), ((3, 384, SEQ), BF)],
        HEADS + [((6, SEQ, SEQ), BF)],
        ATTEND_SCRATCH + [pltpu.VMEM((SEQ, 384), BF), pltpu.VMEM(*TURNED), pltpu.VMEM(*TURNED)],
        8.0,
    )


def ffn_up_body(meta, _, ins, outs, __):
    hb, s12, *pieces = ins
    f0, f1, gp, w = outs
    place(meta, pieces, w)
    for part in range(4):
        rel, half = divmod(part, 2)
        bias_row = pl.ds(8 + 2 * (meta[1] ^ rel) + half, 1)
        f_ref = (f0, f1)[rel]
        for c in range(PER_PART):
            cols = slice(c * CHUNK, (c + 1) * CHUNK)
            u = dot(hb[...], w[part, :, cols]) + s12[bias_row, cols]
            f, slope = gelu_pair(u)
            f_ref[half, :, cols] = f.astype(BF)
            gp[part, :, cols] = slope.astype(BF)


SIDE = ((2, SEQ, D), BF)
SLABS = ((2, 384, SEQ), BF)


def ffn_up(meta, hb, pieces, s12):
    return kernel_call(
        ffn_up_body,
        "ffn_up",
        meta,
        [],
        [hb, s12, *pieces],
        [SIDE, SIDE, ((4, SEQ, D), BF), (W_SHAPE, BF)],
        [],
        [],
        5.0,
    )


def norm_back(grad, hat, inv, gain):
    scaled = grad * gain
    return inv * (
        scaled
        - jnp.mean(scaled, -1, keepdims=True)
        - hat * jnp.mean(scaled * hat, -1, keepdims=True)
    )


def ffn_down_body(meta, _, ins, outs, __):
    f0, f1, yh, co, cr, s12, *pieces = ins
    out_o, out_r, dz, dz_t, dy2, sums, w = outs
    place(meta, pieces, w)
    t, length = meta[1], meta[2]
    b2 = s12[3:4, :]
    g1, c1, g2, c2 = s12[4:5, :], s12[5:6, :], s12[6:7, :], s12[7:8, :]
    fs = (f0, f1)
    for part in range(4):
        rel, half = divmod(part, 2)
        z = dot_t(fs[rel][half], w[part])
        dy2[...] = z if part == 0 else dy2[...] + z
    totals = [jnp.zeros((1, D), F32)] * 3
    for r, cot, out in ((0, co, out_o), (1, cr, out_r)):
        rows = pl.ds(r * HALF, HALF)
        y = yh[rows, :] * g1 + c1 + dy2[rows, :] + b2
        centred = y - jnp.mean(y, -1, keepdims=True)
        inv = lax.rsqrt(jnp.mean(centred * centred, -1, keepdims=True) + EPS_NORM)
        hat = centred * inv
        out[...] = (hat * g2 + c2).astype(BF)
        row = lax.broadcasted_iota(jnp.int32, (HALF, 1), 0)
        valid = row + (t ^ r) * HALF < length
        dout = jnp.where(valid, cot[...].astype(F32), 0.0)
        grad = norm_back(dout, hat, inv, g2)
        dy2[rows, :] = grad
        dz[rows, :] = grad.astype(BF)
        totals = [a + row_sum(b) for a, b in zip(totals, (grad, dout * hat, dout))]
    for i in range(3):
        sums[i : i + 1, :] = totals[i]
    for i in range(2):
        dz_t[i] = dz[:, i * 384 : (i + 1) * 384].T


def ffn_down(meta, f0, f1, pieces, yh, co, cr, s12):
    return kernel_call(
        ffn_down_body,
        "ffn_down",
        meta,
        [],
        [f0, f1, yh, co, cr, s12, *pieces],
        [
            ((HALF, D), BF),
            ((HALF, D), BF),
            ((SEQ, D), BF),
            SLABS,
            ((SEQ, D), F32),
            ((8, D), F32),
            (W_SHAPE, BF),
        ],
        [],
        [],
        5.0,
    )


def ffn_back_body(meta, _, ins, outs, __):
    dz, gp, w = ins
    du0, du1, db1 = outs
    for part in (2, 3, 0, 1):
        rel, half = divmod(part, 2)
        bias_row = pl.ds(2 * (meta[1] ^ rel) + half, 1)
        du_ref = (du0, du1)[rel]
        for c in range(PER_PART):
            cols = slice(c * CHUNK, (c + 1) * CHUNK)
            du = dot(dz[...], w[part, :, cols]) * gp[part, :, cols].astype(F32)
            db1[bias_row, cols] = row_sum(du)
            du_ref[half, :, cols] = du.astype(BF)


def ffn_back(meta, dz, w, gp):
    return kernel_call(
        ffn_back_body,
        "ffn_back",
        meta,
        [],
        [dz, gp, w],
        [SIDE, SIDE, ((4, D), F32)],
        [],
        [],
        3.5,
    )


def hidden_back(ins, outs):
    du0, du1, dy2, yh, inv, small, w = ins
    dy1, da, sums = outs
    dus = (du0, du1)
    for part in range(4):
        rel, half = divmod(part, 2)
        before = dy2 if part == 0 else dy1
        dy1[...] = before[...] + dot_t(dus[rel][half], w[part])
    g1 = small[4:5, :]
    totals = [jnp.zeros((1, D), F32)] * 3
    for r in range(2):
        rows = pl.ds(r * HALF, HALF)
        dh = dy1[rows, :]
        hat = yh[rows, :]
        grad = norm_back(dh, hat, inv[rows, :], g1)
        dy1[rows, :] = grad
        da[rows, :] = grad.astype(BF)
        totals = [a + row_sum(b) for a, b in zip(totals, (grad, dh * hat, dh))]
    for i in range(3):
        sums[i : i + 1, :] = totals[i]


class AttnBack:
    SCRATCH = [
        pltpu.VMEM((D, D), BF),
        pltpu.VMEM((6, SEQ, SEQ), BF),
        pltpu.SemaphoreType.DMA((6,)),
        pltpu.SemaphoreType.DMA((5,)),
        pltpu.VMEM((3, 128, SEQ), BF),
        pltpu.VMEM((3, 128, SEQ), BF),
    ] + [pltpu.VMEM(*h) for h in HEADS]

    def __init__(self, rel, raw, scratch):
        *head_in, w_in, self.p_in = raw
        self.w, self.p_buf, self.p_sems, sems, self.do_t, self.k_t, *self.heads = scratch
        self.copies = [pltpu.make_async_copy(w_in.at[rel * 2 + 1], self.w, sems.at[4])]
        self.copies += [
            pltpu.make_async_copy(a, b, sems.at[i])
            for i, (a, b) in enumerate(zip(head_in, self.heads))
        ]

    def start(self):
        for c in self.copies:
            c.start()
        for i in range(6):
            pltpu.make_async_copy(self.p_in.at[i], self.p_buf.at[i], self.p_sems.at[i]).start()

    def run(self, da, dq, dk, dv, sums):
        w, do_t_ref, k_t_ref = self.w, self.do_t, self.k_t
        k_ref, v_ref, qt_ref, ot_ref = self.heads
        self.copies[0].wait()
        do = dot(da[...], w[:, 384:]).astype(BF)
        for c in self.copies[1:]:
            c.wait()
        for i in range(3):
            do_t_ref[i] = do[:, i * 128 : (i + 1) * 128].T
            k_t_ref[i] = k_ref[i].T
        lane = lax.broadcasted_iota(jnp.int32, (SEQ, 128), 1)

        def pair(i, carry):
            vp = v_ref[i]
            do_t = do_t_ref[i]
            base = pl.multiple_of(i * 128, 128)
            both = do_t.astype(F32) * ot_ref[pl.ds(base, 128), :].astype(F32)
            for hh in range(2):
                own = (lane < HD) if hh == 0 else (lane >= HD)
                inside = slice(hh * HD, (hh + 1) * HD)
                delta = row_sum(both[inside])
                slope = dot(jnp.where(own, vp, jnp.zeros_like(vp)), do_t)
                head = 2 * i + hh
                pltpu.make_async_copy(
                    self.p_in.at[head], self.p_buf.at[head], self.p_sems.at[head]
                ).wait()
                prob = self.p_buf[head]
                ds = (prob.astype(F32) * (slope - delta)).astype(BF)
                lines = pl.ds(base + hh * HD, HD)
                dv[lines, :] = dot_t(do_t[inside], prob).astype(BF)
                dk[lines, :] = dot_t(qt_ref[lines, :], ds).astype(BF)
                dq[lines, :] = (dot(k_t_ref[i, inside, :], ds) * (HD**-0.5)).astype(BF)
            return carry

        lax.fori_loop(0, 3, pair, 0, unroll=True)
        ones = jnp.ones((8, SEQ), BF)
        sums[0:8, :] = dot_t(ones, dq[...])
        sums[8:16, :] = dot_t(ones, dv[...])


LINES = SMALL // 128


def put_lines(vec, first, row):
    for i in range(row.shape[1] // 128):
        vec[pl.ds(first + i, 1), :] = row[:, i * 128 : (i + 1) * 128]


def frames_back_body(meta, raw, ins, outs, _, total, w, dy1, sem):
    grads = ins
    copies = [pltpu.make_async_copy(raw[0].at[i], w.at[i], sem.at[i]) for i in range(4)]
    copies.append(pltpu.make_async_copy(raw[1], dy1, sem.at[4]))
    for c in copies:
        c.start()
    for c in copies:
        c.wait()
    for m in range(3):
        rows = pl.ds(m * 256, 256)
        acc = None
        for rel in range(2):
            for side, left in enumerate(
                (w[rel * 2, rows, :384], w[rel * 2, rows, 384:], w[rel * 2 + 1, rows, :384])
            ):
                term = dot(left, grads[rel][side])
                acc = term if acc is None else acc + term
        total[rows, :] = acc
    for r in range(2):
        rows = pl.ds(r * HALF, HALF)
        outs[r][...] = dy1[rows, :] + total[:, r * HALF : (r + 1) * HALF].T


def frames_back(meta, dy1, turned, w):
    return kernel_call(
        frames_back_body,
        "frames_back",
        meta,
        [w, dy1],
        turned,
        [((HALF, D), F32)] * 2,
        [],
        [
            pltpu.VMEM((D, SEQ), F32),
            pltpu.VMEM(W_SHAPE, BF),
            pltpu.VMEM((SEQ, D), F32),
            pltpu.SemaphoreType.DMA((5,)),
        ],
        3.5,
    )


def near_body(meta, _, ins, outs, __):
    for half in range(2):
        keep, came = ins[half], ins[2 + half]
        for i in range(4):
            outs[2 + half][i] = (keep[4 + i].astype(F32) + came[4 + i].astype(F32)).astype(BF)
            outs[half][i] = (keep[i].astype(F32) + came[i].astype(F32)).astype(BF)


def near_sums(meta, keep, came):
    outs = kernel_call(
        near_body, "near_sums", meta, [], [*keep, *came], [((4, ROWS, D), BF)] * 4, [], [], 0.5
    )
    return outs[:2], outs[2:]


def z_body(meta, _, ins, outs, __):
    for half in range(2):
        keep, came = ins[half], ins[2 + half]
        cols = slice(half * D, (half + 1) * D)
        for i in range(4):
            outs[i][:, cols] = (keep[i].astype(F32) + came[i].astype(F32)).astype(outs[i].dtype)


ROW = (ROWS, 2 * D)


def z_sums(meta, keep, came):
    return kernel_call(
        z_body, "z_sums", meta, [], [*keep, *came], [(ROW, F32)] + [(ROW, BF)] * 3, [], [], 4.0
    )


def totals_body(meta, _, ins, outs, __):
    count = ins[0]
    grads, vec = outs
    square = jnp.zeros((1, 1), F32)
    for k in range(3):
        row, *came = ins[1 + 4 * k : 5 + 4 * k]
        total = row[...]
        for c in came:
            total = total + c[...].astype(F32)
        grads[k] = total
        square = square + jnp.sum(row_sum(total * total), 1, keepdims=True)
    lane = lax.broadcasted_iota(jnp.int32, (8, 128), 1)
    vec[...] = jnp.where(lane == 0, square, jnp.where(lane == 1, count[...], 0.0))


def totals(meta, count, parts):
    return kernel_call(
        totals_body,
        "totals",
        meta,
        [],
        [count, *parts],
        [((3, *parts[0].shape), F32), ((8, 128), F32)],
        [],
        [],
        1.0,
    )


def adamw_body(meta, raw, ins, outs, raw_outs, *scratch):
    square, vec, grads, small_w, small_m, small_v, aw, am, av, fw, fm, fv = ins
    norm_out, small_out = outs[0], outs[1:]
    new_a, new_f, sems = scratch
    frame_count = square[0:1, 1:2]
    small = vec[...]
    squares = square[0:1, 0:1] + jnp.sum(row_sum(small * small), 1, keepdims=True)
    norm = jnp.sqrt(squares) / frame_count
    norm_out[...] = norm
    factor = jnp.minimum(1.0, CLIP_NORM / norm) / frame_count
    copies = []
    for i in range(4):
        cols = slice((i % 2) * 384 + (i // 2) * D, (i % 2) * 384 + (i // 2) * D + 384)
        rate = RATE * 0.5 * SEQ**0.5 if i == 3 else RATE
        for k, v in enumerate(adamw(aw[i], am[i], av[i], grads[0, :, cols] * factor, rate, DECAY)):
            new_a[k, i] = v
    for k in range(3):
        copies.append(pltpu.make_async_copy(new_a.at[k], raw_outs[k], sems.at[k]))
        copies[-1].start()
    for i in range(2):
        for k, v in enumerate(adamw(fw[i], fm[i], fv[i], grads[1 + i] * factor, RATE, DECAY)):
            new_f[k, i] = v
    for k in range(3):
        copies.append(pltpu.make_async_copy(new_f.at[k], raw_outs[3 + k], sems.at[3 + k]))
        copies[-1].start()
    new_small = adamw(small_w[...], small_m[...], small_v[...], small * factor, SMALL_RATE, 0.0)
    for out, v in zip(small_out, new_small):
        out[...] = v
    for c in copies:
        c.wait()


def adamw_call(meta, square, vec, grads, small, state):
    shapes = [v.shape for v in state]
    return kernel_call(
        adamw_body,
        "adamw",
        meta,
        [],
        [square, vec, grads, *small, *state],
        [((1, 1), F32)] + [((LINES, 128), F32)] * 3,
        [(s, F32) for s in shapes],
        [
            pltpu.VMEM((3, *shapes[0]), F32),
            pltpu.VMEM((3, *shapes[3]), F32),
            pltpu.SemaphoreType.DMA((6,)),
        ],
        3.0,
    )


def put_out(meta, acc, outs, half):
    d = meta[0]
    for sel in range(2):
        for j in range(8):
            row = pl.multiple_of((d ^ MASKS[half][sel][j]) * ROWS, 16)
            outs[half * 2 + sel][j] = acc[half, pl.ds(row, ROWS), :]


GRAD_OUTS = [((8, ROWS, D), BF)] * 4
GRAD_SCRATCH = [pltpu.VMEM((2, D, D), BF)]


def ffn_grad(meta, left_o, left_r, right_o, right_r, outs, acc):
    for half in range(2):
        for i in range(2):
            total = dot(left_o[i], right_o[half]) + dot(left_r[i], right_r[half])
            acc[half, i * 384 : (i + 1) * 384, :] = total.astype(BF)
        put_out(meta, acc, outs, half)


def down_grad_body(meta, _, ins, outs, __, acc):
    dz_o, dz_r, f_o, f_r = ins
    ffn_grad(meta, dz_o, dz_r, f_o, f_r, outs, acc)


def down_grad_call(meta, *ins):
    return kernel_call(
        down_grad_body, "down_grad", meta, [], ins, GRAD_OUTS, [], GRAD_SCRATCH, 4.0
    )


def middle_body(meta, raw, ins, outs, raw_outs, acc, grads, dy1, da, out_sems, *scratch):
    attn = AttnBack(1, raw, scratch)
    attn.start()
    shared, shared_r, du0, du_r, *rest = ins
    sums_one, sent, qv = outs
    copies = [
        pltpu.make_async_copy(a, b, out_sems.at[i])
        for i, (a, b) in enumerate(zip([*[grads.at[i] for i in range(4)], dy1, da], raw_outs))
    ]
    ffn_grad(
        meta,
        shared.at[pl.ds(1, 2)],
        shared_r.at[pl.ds(1, 2)],
        du0,
        du_r,
        [grads.at[i] for i in range(4)],
        acc,
    )
    for c in copies[:4]:
        c.start()
    hidden_back([du0, *rest], (dy1, da, sums_one))
    for c in copies[4:]:
        c.start()
    for i in range(2):
        sent[3 + i] = da[:, i * 384 : (i + 1) * 384].T
    attn.run(da, sent.at[0], sent.at[1], sent.at[2], qv)
    for c in copies:
        c.wait()


def middle(meta, heads, w_attn, prob, shared, shared_r, du0, du_r, du1, dy2, yh, inv, s12, w):
    return kernel_call(
        middle_body,
        "up_grad_hidden_back_attn_back",
        meta,
        [*heads, w_attn, prob],
        [shared, shared_r, du0, du_r, du1, dy2, yh, inv, s12, w],
        [((8, D), F32), ((5, 384, SEQ), BF), ((16, 384), F32)],
        GRAD_OUTS + [((SEQ, D), F32), ((SEQ, D), BF)],
        GRAD_SCRATCH
        + [
            pltpu.VMEM((4, 8, ROWS, D), BF),
            pltpu.VMEM((SEQ, D), F32),
            pltpu.VMEM((SEQ, D), BF),
            pltpu.SemaphoreType.DMA((6,)),
        ]
        + AttnBack.SCRATCH,
        14.0,
    )


def attn_back_body(meta, raw, ins, outs, _, da, da_sem, *scratch):
    da_copy = pltpu.make_async_copy(raw[0], da, da_sem.at[0])
    da_copy.start()
    attn = AttnBack(0, raw[1:], scratch)
    attn.start()
    turned, qv = outs
    da_copy.wait()
    attn.run(da, turned.at[0], turned.at[1], turned.at[2], qv)


def attn_back(meta, heads, w_attn, prob, da):
    return kernel_call(
        attn_back_body,
        "attn_back",
        meta,
        [da, *heads, w_attn, prob],
        [],
        [((3, 384, SEQ), BF), ((16, 384), F32)],
        [],
        [pltpu.VMEM((SEQ, D), BF), pltpu.SemaphoreType.DMA((1,))] + AttnBack.SCRATCH,
        7.0,
    )


def attn_grad_body(meta, _, ins, outs, __, acc, x_t):
    xo, xr, zo, zr, turned, sent, sent_r, o_own, shared_r = ins[:9]
    qv0, qv1, sums_one, sums_two, db1 = ins[9:]
    vec = outs[4]
    for rel, qv in ((0, qv0), (1, qv1)):
        h = meta[1] ^ rel
        put_lines(vec, 3 * h, qv[0:1, :])
        put_lines(vec, 6 + 3 * h, qv[8:9, :])
    for line, sums, row in (
        (2, sums_one, 0),
        (3, sums_two, 0),
        (4, sums_one, 1),
        (5, sums_one, 2),
        (6, sums_two, 1),
        (7, sums_two, 2),
    ):
        put_lines(vec, 6 * line, sums[row : row + 1, :])
    for i in range(4):
        put_lines(vec, 48 + 6 * i, db1[i : i + 1, :])
    for i, v in enumerate((xo, xr, zo, zr)):
        x_t[:, i * HALF : (i + 1) * HALF] = v[...].T
    for half, side, k in ((1, 0, 2), (0, 0, 0), (0, 1, 1)):
        for m in range(3):
            rows = pl.ds(m * 256, 256)
            total = dot_t(x_t[rows, :SEQ], turned[k]) + dot_t(x_t[rows, SEQ:], sent_r[k])
            acc[half, rows, side * 384 : (side + 1) * 384] = total.astype(BF)
    for i in range(2):
        total = dot_t(sent[3 + i], o_own[...]) + dot_t(sent_r[3 + i], shared_r[0])
        acc[1, i * 384 : (i + 1) * 384, 384:] = total.astype(BF)
    for half in range(2):
        put_out(meta, acc, outs, half)


def attn_grad(meta, xs, turned, sent, sent_r, o_own, shared_r, small):
    return kernel_call(
        attn_grad_body,
        "attn_grad",
        meta,
        [],
        [*xs, turned, sent, sent_r, o_own, shared_r, *small],
        GRAD_OUTS + [((LINES, 128), F32)],
        [],
        GRAD_SCRATCH + [pltpu.VMEM((D, 2 * SEQ), BF)],
        5.0,
    )


def adamw(weight, moment_one, moment_two, grad, rate, decay):
    new_one = BETA_ONE * moment_one + (1.0 - BETA_ONE) * grad
    new_two = BETA_TWO * moment_two + (1.0 - BETA_TWO) * grad * grad
    fixed_one = new_one / (1.0 - BETA_ONE**STEP)
    fixed_two = new_two / (1.0 - BETA_TWO**STEP)
    update = fixed_one / (jnp.sqrt(fixed_two) + ADAM_EPS) + decay * weight
    return (weight - rate * update, new_one, new_two)


def after(v, *deps):
    return lax.optimization_barrier((v, *deps))[0]


def other_core(v):
    return lax.ppermute(v, "tensor", [(0, 1), (1, 0)])


def shift(v, mask, n):
    return lax.ppermute(v, "dp", [(i, i ^ mask) for i in range(n)])


class Gather:
    def __init__(self, shard, n):
        self.n, self.shard, self.mark = n, shard, shard

    def z_all(self, *deps):
        if self.n == BLOCKS:
            shard = after(self.shard, *deps)
            self.z = [shard] + [shift(shard, z, self.n) for z in Z_MASKS[1:]]
            self.mark = shard

    def z_wait(self, *deps):
        if self.n == BLOCKS:
            self.z = after(tuple(self.z), *deps)
            self.mark = self.z[1:]

    def far_wait(self, *deps):
        if self.n == BLOCKS:
            self.far_side = after(tuple(self.far_side), *deps)
            self.mark = tuple(self.far_side)

    def near_wait(self, *deps):
        if self.n == BLOCKS:
            self.came = after(tuple(self.came), *deps)
            self.mark = tuple(self.came)

    def near(self, *deps):
        if self.n != BLOCKS:
            return
        parts = after(tuple(self.z), *deps)
        self.own = [
            jnp.stack([v[:, half * D : (half + 1) * D] for v in parts]) for half in range(2)
        ]
        self.mark = tuple(self.own)
        self.came = [shift(s, step[0], self.n) for s, step in zip(self.own, (STEP_A, STEP_B))]

    def far(self, *deps):
        if self.n != BLOCKS:
            return
        came = after(tuple(self.came), *deps)
        self.own = [jnp.concatenate([s, c]) for s, c in zip(self.own, came)]
        self.mark = tuple(self.own)
        self.far_side = [shift(o, step[1], self.n) for o, step in zip(self.own, (STEP_A, STEP_B))]

    def core(self, *deps):
        if self.n == BLOCKS:
            self.own_other = [other_core(o) for o in after(tuple(self.own), *deps)]
            self.mark = tuple(self.own_other)

    def pieces(self, *deps):
        if self.n == BLOCKS:
            far = after(tuple(self.far_side), *deps)
            result = []
            for half in range(2):
                far_other = other_core(far[half])
                result += [self.own[half], far[half], self.own_other[half], far_other]
            self.mark = far[1]
            return result
        full = lax.all_gather(self.shard, "dp", axis=0, tiled=True)
        blocks = full.reshape(BLOCKS, ROWS, 2 * D)
        result = []
        for half in range(2):
            cols = slice(half * D, (half + 1) * D)
            own = [blocks[jnp.array(m), :, cols] for m in MASKS[half]]
            result += own + [other_core(v) for v in own]
        return result


def added(*parts):
    total = parts[0].astype(F32)
    for p in parts[1:]:
        total = total + p.astype(F32)
    return total


class Scatter:
    def __init__(self, meta, pieces, n):
        self.meta = meta
        self.n, self.pieces, self.mark = n, pieces, pieces[0]
        if n == BLOCKS:
            self.keep = [pieces[0], pieces[2]]
            self.came = [
                shift(v, step[1], n) for v, step in zip((pieces[1], pieces[3]), (STEP_A, STEP_B))
            ]

    def near(self, *deps):
        if self.n != BLOCKS:
            return
        came = after(tuple(self.came), *deps)
        self.keep, send = near_sums(self.meta, self.keep, came)
        self.came = [shift(s, step[0], self.n) for s, step in zip(send, (STEP_A, STEP_B))]
        self.mark = tuple(send)

    def wait(self, *deps):
        if self.n == BLOCKS:
            self.came = after(tuple(self.came), *deps)
            self.mark = tuple(self.came)

    def z_all(self, *deps):
        if self.n != BLOCKS:
            return
        came = after(tuple(self.came), *deps)
        self.row, *sends = z_sums(self.meta, self.keep, came)
        self.mark = tuple(sends)
        self.came = [shift(s, z, self.n) for s, z in zip(sends, Z_MASKS[1:])]

    def parts(self, *deps):
        if self.n == BLOCKS:
            return [self.row, *after(tuple(self.came), *deps)]
        whole = self.whole()
        zero = jnp.zeros(whole.shape, BF)
        return [whole, zero, zero, zero]

    def whole(self):
        result = []
        for half in range(2):
            order = MASKS[half][0] + MASKS[half][1]
            back = [order.index(i) for i in range(BLOCKS)]
            full = jnp.concatenate(self.pieces[2 * half : 2 * half + 2])[jnp.array(back)]
            full = full.reshape(D, D).astype(F32)
            result.append(lax.psum_scatter(full, "dp", scatter_dimension=0, tiled=True))
        return jnp.concatenate(result, 1)


class Everywhere:
    def __init__(self, v, n):
        self.n, self.v = n, v

    def core(self, *deps):
        if self.n == BLOCKS:
            v = after(self.v, *deps)
            self.v = v + other_core(v)

    def step(self, masks, *deps):
        if self.n == BLOCKS:
            v = after(self.v, *deps)
            came = [shift(v, m, self.n) for m in masks]
            self.v = v + came[0] if len(came) == 1 else (v + came[0]) + (came[1] + came[2])

    def total(self):
        return self.v if self.n == BLOCKS else lax.psum(self.v, ("dp", "tensor"))


XY_MASKS = (1, 2, 3)


def last_steps(small, every):
    if every.n != BLOCKS:
        return small.total(), every.total()
    lines = every.v.shape[0]
    every.v = jnp.concatenate([every.v, small.v])
    every.step(XY_MASKS)
    v = every.v[:lines]
    near, both, far = [
        shift(s, m, every.n) for s, m in zip((v, every.v, v), Z_MASKS[1:])
    ]
    return every.v[lines:] + both[lines:], (v + near) + (both[:lines] + far)


def per_device(
    frames,
    cotangent,
    lengths,
    attn_w,
    attn_m,
    attn_v,
    ffn_w,
    ffn_m,
    ffn_v,
    small_w,
    small_m,
    small_v,
):
    n = lax.axis_size("dp")
    t = lax.axis_index("tensor")
    d = lax.axis_index("dp") if n == BLOCKS else 0
    length = lax.dynamic_index_in_dim(lengths[:, 0], t, 0, keepdims=False)
    meta = jnp.stack([jnp.asarray(d, jnp.int32), jnp.asarray(t, jnp.int32), length])
    s12 = small_w.reshape(12, D)
    half = SEQ // lax.axis_size("tensor")
    count = jnp.sum(jnp.clip(lengths - t * half, 0, half)).astype(F32).reshape(1, 1)

    def pick(v, i):
        return lax.dynamic_index_in_dim(v[:, 0], i, 0, keepdims=False)

    def joined(own, other):
        return jnp.where(t == 0, jnp.stack([own, other]), jnp.stack([other, own]))[:, None]

    attn = Gather(jnp.concatenate([attn_w[i] for i in range(4)], 1).astype(BF), n)
    up = Gather(ffn_w[0].astype(BF), n)
    down = Gather(ffn_w[1].astype(BF), n)
    attn.z_all()
    frames_r = other_core(frames)
    xo, zr = pick(frames, t), pick(frames, 1 - t)
    xr, zo = pick(frames_r, t), pick(frames_r, 1 - t)
    cotangent_r = other_core(cotangent)
    co, cr = pick(cotangent, t), pick(cotangent_r, t)
    attn.near(xr, cr)
    up.z_all(attn.mark)
    attn.far()
    up.near(attn.mark)
    attn.core()
    attn_pieces = attn.pieces(up.mark)
    down.z_all(attn.mark)
    up.far(attn.mark)
    first = attn_first(after(meta, up.mark, down.mark, count), xo, xr, attn_pieces, s12)
    later, o_first, out_w, *heads_first = first
    *heads_first, w_attn, prob_first = heads_first
    down.near(o_first)
    second = attn_second(after(meta, down.mark), xo, xr, s12, later, o_first, out_w)
    yh, inv, hb, shared, *heads_second = second
    *heads_second, prob_second = heads_second
    heads, prob = (heads_first, heads_second), (prob_first, prob_second)
    down.near_wait(inv)
    up.far_wait(inv)
    up.core(down.mark)
    up_pieces = up.pieces()
    down.far()
    down_far = down.mark
    down.core(up_pieces[1], up_pieces[3])
    f0, f1, gp, w_up = ffn_up(after(meta, down_far), hb, up_pieces, s12)
    down.far_wait(gp)
    down_pieces = down.pieces()
    f_r = other_core(after(f1, *down_pieces))
    shared_r = other_core(after(shared, *down_pieces))
    out_o, out_r, dz, dz_t, dy2, sums_two, w_down = ffn_down(
        meta, f0, f1, down_pieces, yh, co, cr, s12
    )
    dz_r = other_core(after(dz_t, f_r, shared_r))
    du0, du1, db1 = ffn_back(after(meta, f_r, shared_r), dz, w_down, gp)
    du_r = other_core(after(du1, dz_r))
    down_sum = Scatter(
        meta,
        down_grad_call(after(meta, db1), dz_t, dz_r, f0, f_r), n
    )
    *up_grad, dy1, da = middle(
        after(meta, down_sum.mark),
        heads[1],
        w_attn,
        prob[1],
        shared,
        shared_r,
        du0,
        du_r,
        du1,
        dy2,
        yh,
        inv,
        s12,
        w_up,
    )
    sums_one, sent, qv1, *up_grad = up_grad
    down_sum.wait(qv1)
    up_sum = Scatter(meta, after(tuple(up_grad), down_sum.mark), n)
    down_sum.near()
    sent_r = other_core(after(sent, down_sum.mark))
    turned0, qv0 = attn_back(after(meta, down_sum.mark), heads[0], w_attn, prob[0], da)
    down_sum.z_all(qv0, sent_r)
    *attn_grads, vec = attn_grad(
        after(meta, down_sum.mark),
        (xo, xr, zo, zr),
        turned0,
        sent,
        sent_r,
        heads[0][3],
        shared_r,
        (qv0, qv1, sums_one, sums_two, db1),
    )
    up_sum.wait(attn_grads[0])
    up_sum.near()
    down_sum.wait(up_sum.mark)
    small = Everywhere(vec, n)
    attn_sum = Scatter(meta, after(tuple(attn_grads), down_sum.mark), n)
    small.core(down_sum.mark)
    small.step((4,))
    up_sum.wait()
    up_sum.z_all(small.v)
    small_state = [v.reshape(LINES, 128) for v in (small_w, small_m, small_v)]
    attn_sum.near(up_sum.mark)
    dx_o, dx_r = frames_back(after(meta, attn_sum.mark), dy1, (turned0, sent), w_attn)
    attn_sum.wait(dx_o)
    up_sum.wait(dx_o)
    attn_sum.z_all(up_sum.mark)
    dx_other = other_core(after(dx_r, attn_sum.mark))
    out_other = other_core(after(out_r, attn_sum.mark))
    frames_grad = joined(dx_o, dx_other)
    output = joined(out_o, out_other)
    grads, square = totals(
        meta, count, attn_sum.parts(frames_grad, output) + up_sum.parts() + down_sum.parts()
    )
    every = Everywhere(square, n)
    every.core()
    small_all, square_all = last_steps(small, every)
    state = (attn_w, attn_m, attn_v, ffn_w, ffn_m, ffn_v)
    norm, small_new, small_m_new, small_v_new, *new_state = adamw_call(
        meta, square_all, small_all, grads, small_state, state
    )
    attn_new, attn_m_new, attn_v_new, ffn_new, ffn_m_new, ffn_v_new = new_state
    grad_norm = norm[0, 0]
    small_new, small_m_new, small_v_new = [
        v.reshape(SMALL) for v in (small_new, small_m_new, small_v_new)
    ]
    return (
        output,
        frames_grad,
        grad_norm,
        attn_new,
        attn_m_new,
        attn_v_new,
        ffn_new,
        ffn_m_new,
        ffn_v_new,
        small_new,
        small_m_new,
        small_v_new,
    )


def solution(mesh):
    rows = P(None, "dp", "tensor", None)
    weights = P(None, "dp", "tensor")
    in_specs = (rows, rows, P(None, "dp")) + (weights,) * 6 + (P(),) * 3
    out_specs = (rows, rows, P()) + (weights,) * 6 + (P(),) * 3
    return jax.shard_map(
        per_device, mesh=mesh, in_specs=in_specs, out_specs=out_specs, check_vma=False
    )
```

```python
import math

import jax
import jax.numpy as jnp
from jax import lax
from jax.experimental import pallas as pl
from jax.experimental.pallas import tpu as pltpu
from jax.sharding import PartitionSpec as P

HD = 64
D = 768
FF = 3072
SEQ = 512
HALF = SEQ // 2
STEP = 10
SMALL = 9216
PAIRS = 6
BLOCKS = 16
ROWS = D // BLOCKS

EPS_NORM = 1e-05
MASK_FILL = -1e30
BETA_ONE = 0.9
BETA_TWO = 0.999
ADAM_EPS = 1e-08
CLIP_NORM = 0.1
RATE = 0.1
SMALL_RATE = 1.5
DECAY = 0.01

BF = jnp.bfloat16
F32 = jnp.float32

STEP_A = (2, 1)
STEP_B = (1, 2)
Z_MASKS = (0, 4, 8, 12)
MASKS = tuple(
    (
        tuple(z for z in Z_MASKS) + tuple(z + near for z in Z_MASKS),
        tuple(z + far for z in Z_MASKS) + tuple(z + near + far for z in Z_MASKS),
    )
    for near, far in (STEP_A, STEP_B)
)


def dot(left, right):
    return jnp.dot(left, right, preferred_element_type=F32)


def dot_t(left, right):
    return lax.dot_general(left, right, (((1,), (1,)), ((), ())), preferred_element_type=F32)


def gelu_pair(u):
    phi = 0.5 * lax.erf(u * math.sqrt(0.5)) + 0.5
    return u * phi, phi + u * jnp.exp(-0.5 * u * u) * (1.0 / math.sqrt(2.0 * math.pi))


HBM = pl.BlockSpec(memory_space=pltpu.HBM)
SMEM = pl.BlockSpec(memory_space=pltpu.SMEM)


VMEM = pl.BlockSpec(memory_space=pltpu.VMEM)


def kernel_call(body, name, meta, raw, ins, outs, raw_outs, scratch, micros):
    n_raw, n_in, n_out, n_raw_out = len(raw), len(ins), len(outs), len(raw_outs)

    def run(meta_ref, *refs):
        cuts = [0, n_raw, n_in, n_out, n_raw_out]
        for i in range(1, 5):
            cuts[i] += cuts[i - 1]
        groups = [refs[cuts[i] : cuts[i + 1]] for i in range(4)]
        body(meta_ref, *groups, *refs[cuts[4] :])

    held = sum(
        math.prod(v.shape) * (2 if v.dtype == BF else 4) for v in scratch if v.dtype in (BF, F32)
    )
    return pl.pallas_call(
        run,
        name=name,
        in_specs=[SMEM] + [HBM] * n_raw + [VMEM] * n_in,
        out_specs=[VMEM] * n_out + [HBM] * n_raw_out,
        out_shape=[jax.ShapeDtypeStruct(s, d) for s, d in outs]
        + [pltpu.HBM(s, d) for s, d in raw_outs],
        scratch_shapes=scratch,
        compiler_params=pltpu.CompilerParams(vmem_limit_bytes=held + SPARE),
        cost_estimate=pl.CostEstimate(
            flops=int(micros * 1.15e9), bytes_accessed=0, transcendentals=0
        ),
    )(meta, *[pltpu.with_memory_space_constraint(v, pltpu.HBM) for v in raw], *ins)


SPARE = 8 * 2**20
W_SHAPE = (4, D, D)


def place(meta, pieces, w):
    d = meta[0]
    for part in range(4):
        rel, half = divmod(part, 2)
        for sel in range(2):
            src = pieces[half * 4 + rel * 2 + sel]
            for j in range(8):
                row = pl.multiple_of((d ^ MASKS[half][sel][j]) * ROWS, 16)
                w[part, pl.ds(row, ROWS), :] = src[j]


def chunk(c):
    return pl.ds(pl.multiple_of(c * CHUNK, CHUNK), CHUNK)


CHUNK = 256
PER_PART = D // CHUNK


def row_sum(v):
    return jnp.sum(v, 0, keepdims=True)


def attend(meta, q_ref, k_ref, v_ref, qt_ref, ot_ref, o_ref, p_buf, p_out, p_sems):
    t, length = meta[1], meta[2]
    row = lax.broadcasted_iota(jnp.int32, (SEQ, 1), 0)
    position = jnp.where(row < HALF, row + t * HALF, row + (1 - t) * HALF - HALF)
    valid = position < length
    lane = lax.broadcasted_iota(jnp.int32, (SEQ, 128), 1)

    def pair(i, carry):
        keys = k_ref[i]
        q_t = q_ref[i].T
        lines = pl.ds(pl.multiple_of(i * 128, 128), 128)
        qt_ref[lines, :] = q_t
        v_t = v_ref[i].T
        halves = []
        for hh in range(2):
            own = (lane < HD) if hh == 0 else (lane >= HD)
            s = dot(jnp.where(own, keys, jnp.zeros_like(keys)), q_t)
            s = jnp.where(valid, s, MASK_FILL)
            e = jnp.exp(s - jnp.max(s, 0, keepdims=True))
            prob = (e * (1.0 / jnp.sum(e, 0, keepdims=True))).astype(BF)
            head = 2 * i + hh
            p_buf[head] = prob
            pltpu.make_async_copy(p_buf.at[head], p_out.at[head], p_sems.at[head]).start()
            halves.append(dot(v_t[hh * HD : (hh + 1) * HD], prob))
        o_t = jnp.concatenate(halves, 0).astype(BF)
        ot_ref[lines, :] = o_t
        o_ref[:, lines] = o_t.T
        return carry

    lax.fori_loop(0, 3, pair, 0)


def attend_wait(p_buf, p_out, p_sems):
    for i in range(6):
        pltpu.make_async_copy(p_buf.at[i], p_out.at[i], p_sems.at[i]).wait()


TURNED = ((384, SEQ), BF)
HEADS = [((3, SEQ, 128), BF), ((3, SEQ, 128), BF), TURNED, TURNED]
ATTEND_SCRATCH = [
    pltpu.VMEM((6, SEQ, SEQ), BF),
    pltpu.SemaphoreType.DMA((6,)),
    pltpu.SemaphoreType.DMA((5,)),
]


def attn_first_body(meta, _, ins, outs, raw_outs, p_buf, p_sems, sems, w, q_ref, *head_refs):
    xo, xr, s12, *pieces = ins
    later, o_ref, out_w = outs
    place(meta, pieces, w)
    copies = [
        pltpu.make_async_copy(a, raw_outs[i], sems.at[i]) for i, a in enumerate([*head_refs, w])
    ]
    copies[4].start()
    t = meta[1]
    for rel in range(2):
        if rel == 0:
            targets = q_ref, head_refs[0], head_refs[1]
        else:
            targets = later.at[0], later.at[1], later.at[2]
        cols = pl.ds(pl.multiple_of((t ^ rel) * 384, 128), 384)
        bq = s12[0:1, cols]
        bv = s12[1:2, cols]
        for r, x in ((0, xo), (1, xr)):
            rows = pl.ds(r * HALF, HALF)
            qk = dot(x[...], w[rel * 2])
            q = (qk[:, :384] + bq).astype(BF) * jnp.asarray(HD**-0.5, BF)
            k = qk[:, 384:].astype(BF)
            v = (dot(x[...], w[rel * 2 + 1, :, :384]) + bv).astype(BF)
            for ref, value in zip(targets, (q, k, v)):
                for i in range(3):
                    ref[i, rows, :] = value[:, i * 128 : (i + 1) * 128]
        out_w[rel] = w[rel * 2 + 1, :, 384:]
    k_ref, v_ref, qt_ref, ot_ref = head_refs
    attend(meta, q_ref, k_ref, v_ref, qt_ref, ot_ref, o_ref, p_buf, raw_outs[5], p_sems)
    for c in copies[:4]:
        c.start()
    for c in copies:
        c.wait()
    attend_wait(p_buf, raw_outs[5], p_sems)


def attn_first(meta, xo, xr, pieces, s12):
    return kernel_call(
        attn_first_body,
        "attn_first",
        meta,
        [],
        [xo, xr, s12, *pieces],
        [((3, 3, SEQ, 128), BF), ((SEQ, 384), BF), ((2, D, 384), BF)],
        HEADS + [(W_SHAPE, BF), ((6, SEQ, SEQ), BF)],
        ATTEND_SCRATCH
        + [pltpu.VMEM(W_SHAPE, BF), pltpu.VMEM((3, SEQ, 128), BF)]
        + [pltpu.VMEM(*h) for h in HEADS],
        9.0,
    )


def attn_second_body(meta, _, ins, outs, raw_outs, p_buf, p_sems, sems, o_ref, qt_ref, ot_ref):
    xo, xr, s12, later, o_first, out_w = ins
    yh, rs, hb, shared = outs
    held = later.at[1], later.at[2], qt_ref, ot_ref
    copies = [pltpu.make_async_copy(a, raw_outs[i], sems.at[i]) for i, a in enumerate(held)]
    for c in copies[:2]:
        c.start()
    attend(
        meta,
        later.at[0],
        later.at[1],
        later.at[2],
        qt_ref,
        ot_ref,
        o_ref,
        p_buf,
        raw_outs[4],
        p_sems,
    )
    for c in copies[2:]:
        c.start()
    bo, g1, c1 = s12[2:3, :], s12[4:5, :], s12[5:6, :]
    for r, x in ((0, xo), (1, xr)):
        rows = pl.ds(r * HALF, HALF)
        a = dot_t(o_first[rows, :], out_w[0]) + dot_t(o_ref[rows, :], out_w[1])
        y = x[...].astype(F32) + a + bo
        centred = y - jnp.mean(y, -1, keepdims=True)
        inv = lax.rsqrt(jnp.mean(centred * centred, -1, keepdims=True) + EPS_NORM)
        hat = centred * inv
        yh[rows, :] = hat
        rs[rows, :] = inv
        hb[rows, :] = (hat * g1 + c1).astype(BF)
    shared[0] = ot_ref[...]
    for i in range(2):
        shared[1 + i] = hb[:, i * 384 : (i + 1) * 384].T
    for c in copies:
        c.wait()
    attend_wait(p_buf, raw_outs[4], p_sems)


def attn_second(meta, xo, xr, s12, later, o_first, out_w):
    return kernel_call(
        attn_second_body,
        "attn_second",
        meta,
        [],
        [xo, xr, s12, later, o_first, out_w],
        [((SEQ, D), F32), ((SEQ, 1), F32), ((SEQ, D), BF), ((3, 384, SEQ), BF)],
        HEADS + [((6, SEQ, SEQ), BF)],
        ATTEND_SCRATCH + [pltpu.VMEM((SEQ, 384), BF), pltpu.VMEM(*TURNED), pltpu.VMEM(*TURNED)],
        8.0,
    )


def ffn_up_body(meta, _, ins, outs, __):
    hb, s12, *pieces = ins
    f0, f1, gp, w = outs
    place(meta, pieces, w)
    for part in range(4):
        rel, half = divmod(part, 2)
        bias_row = pl.ds(8 + 2 * (meta[1] ^ rel) + half, 1)
        f_ref = (f0, f1)[rel]
        for c in range(PER_PART):
            cols = slice(c * CHUNK, (c + 1) * CHUNK)
            u = dot(hb[...], w[part, :, cols]) + s12[bias_row, cols]
            f, slope = gelu_pair(u)
            f_ref[half, :, cols] = f.astype(BF)
            gp[part, :, cols] = slope.astype(BF)


SIDE = ((2, SEQ, D), BF)
SLABS = ((2, 384, SEQ), BF)


def ffn_up(meta, hb, pieces, s12):
    return kernel_call(
        ffn_up_body,
        "ffn_up",
        meta,
        [],
        [hb, s12, *pieces],
        [SIDE, SIDE, ((4, SEQ, D), BF), (W_SHAPE, BF)],
        [],
        [],
        5.0,
    )


def norm_back(grad, hat, inv, gain):
    scaled = grad * gain
    return inv * (
        scaled
        - jnp.mean(scaled, -1, keepdims=True)
        - hat * jnp.mean(scaled * hat, -1, keepdims=True)
    )


def ffn_down_body(meta, _, ins, outs, __):
    f0, f1, yh, co, cr, s12, *pieces = ins
    out_o, out_r, dz, dz_t, dy2, sums, w = outs
    place(meta, pieces, w)
    t, length = meta[1], meta[2]
    b2 = s12[3:4, :]
    g1, c1, g2, c2 = s12[4:5, :], s12[5:6, :], s12[6:7, :], s12[7:8, :]
    fs = (f0, f1)
    for part in range(4):
        rel, half = divmod(part, 2)
        z = dot_t(fs[rel][half], w[part])
        dy2[...] = z if part == 0 else dy2[...] + z
    totals = [jnp.zeros((1, D), F32)] * 3
    for r, cot, out in ((0, co, out_o), (1, cr, out_r)):
        rows = pl.ds(r * HALF, HALF)
        y = yh[rows, :] * g1 + c1 + dy2[rows, :] + b2
        centred = y - jnp.mean(y, -1, keepdims=True)
        inv = lax.rsqrt(jnp.mean(centred * centred, -1, keepdims=True) + EPS_NORM)
        hat = centred * inv
        out[...] = (hat * g2 + c2).astype(BF)
        row = lax.broadcasted_iota(jnp.int32, (HALF, 1), 0)
        valid = row + (t ^ r) * HALF < length
        dout = jnp.where(valid, cot[...].astype(F32), 0.0)
        grad = norm_back(dout, hat, inv, g2)
        dy2[rows, :] = grad
        dz[rows, :] = grad.astype(BF)
        totals = [a + row_sum(b) for a, b in zip(totals, (grad, dout * hat, dout))]
    for i in range(3):
        sums[i : i + 1, :] = totals[i]
    for i in range(2):
        dz_t[i] = dz[:, i * 384 : (i + 1) * 384].T


def ffn_down(meta, f0, f1, pieces, yh, co, cr, s12):
    return kernel_call(
        ffn_down_body,
        "ffn_down",
        meta,
        [],
        [f0, f1, yh, co, cr, s12, *pieces],
        [
            ((HALF, D), BF),
            ((HALF, D), BF),
            ((SEQ, D), BF),
            SLABS,
            ((SEQ, D), F32),
            ((8, D), F32),
            (W_SHAPE, BF),
        ],
        [],
        [],
        5.0,
    )


def ffn_back_body(meta, _, ins, outs, __):
    dz, gp, w = ins
    du0, du1, db1 = outs
    for part in (2, 3, 0, 1):
        rel, half = divmod(part, 2)
        bias_row = pl.ds(2 * (meta[1] ^ rel) + half, 1)
        du_ref = (du0, du1)[rel]
        for c in range(PER_PART):
            cols = slice(c * CHUNK, (c + 1) * CHUNK)
            du = dot(dz[...], w[part, :, cols]) * gp[part, :, cols].astype(F32)
            db1[bias_row, cols] = row_sum(du)
            du_ref[half, :, cols] = du.astype(BF)


def ffn_back(meta, dz, w, gp):
    return kernel_call(
        ffn_back_body,
        "ffn_back",
        meta,
        [],
        [dz, gp, w],
        [SIDE, SIDE, ((4, D), F32)],
        [],
        [],
        3.5,
    )


def hidden_back(ins, outs):
    du0, du1, dy2, yh, inv, small, w = ins
    dy1, da, sums = outs
    dus = (du0, du1)
    dy1[...] = dy2[...]
    for rel in range(2):

        def step(half, carry, rel=rel):
            dy1[...] += dot_t(dus[rel][half], w[2 * rel + half])
            return carry

        lax.fori_loop(0, 2, step, 0)
    g1 = small[4:5, :]
    totals = [jnp.zeros((1, D), F32)] * 3
    for r in range(2):
        rows = pl.ds(r * HALF, HALF)
        dh = dy1[rows, :]
        hat = yh[rows, :]
        grad = norm_back(dh, hat, inv[rows, :], g1)
        dy1[rows, :] = grad
        da[rows, :] = grad.astype(BF)
        totals = [a + row_sum(b) for a, b in zip(totals, (grad, dh * hat, dh))]
    for i in range(3):
        sums[i : i + 1, :] = totals[i]


class AttnBack:
    SCRATCH = [
        pltpu.VMEM((D, D), BF),
        pltpu.VMEM((6, SEQ, SEQ), BF),
        pltpu.SemaphoreType.DMA((6,)),
        pltpu.SemaphoreType.DMA((5,)),
        pltpu.VMEM((3, 128, SEQ), BF),
        pltpu.VMEM((3, 128, SEQ), BF),
    ] + [pltpu.VMEM(*h) for h in HEADS]

    def __init__(self, rel, raw, scratch):
        *head_in, w_in, self.p_in = raw
        self.w, self.p_buf, self.p_sems, sems, self.do_t, self.k_t, *self.heads = scratch
        self.copies = [pltpu.make_async_copy(w_in.at[rel * 2 + 1], self.w, sems.at[4])]
        self.copies += [
            pltpu.make_async_copy(a, b, sems.at[i])
            for i, (a, b) in enumerate(zip(head_in, self.heads))
        ]

    def start(self):
        for c in self.copies:
            c.start()
        for i in range(6):
            pltpu.make_async_copy(self.p_in.at[i], self.p_buf.at[i], self.p_sems.at[i]).start()

    def run(self, da, dq, dk, dv, sums):
        w, do_t_ref, k_t_ref = self.w, self.do_t, self.k_t
        k_ref, v_ref, qt_ref, ot_ref = self.heads
        self.copies[0].wait()
        do = dot(da[...], w[:, 384:]).astype(BF)
        for c in self.copies[1:]:
            c.wait()
        for i in range(3):
            do_t_ref[i] = do[:, i * 128 : (i + 1) * 128].T
            k_t_ref[i] = k_ref[i].T
        lane = lax.broadcasted_iota(jnp.int32, (SEQ, 128), 1)

        def pair(i, carry):
            vp = v_ref[i]
            do_t = do_t_ref[i]
            base = pl.multiple_of(i * 128, 128)
            both = do_t.astype(F32) * ot_ref[pl.ds(base, 128), :].astype(F32)
            for hh in range(2):
                own = (lane < HD) if hh == 0 else (lane >= HD)
                inside = slice(hh * HD, (hh + 1) * HD)
                delta = row_sum(both[inside])
                slope = dot(jnp.where(own, vp, jnp.zeros_like(vp)), do_t)
                head = 2 * i + hh
                pltpu.make_async_copy(
                    self.p_in.at[head], self.p_buf.at[head], self.p_sems.at[head]
                ).wait()
                prob = self.p_buf[head]
                ds = (prob.astype(F32) * (slope - delta)).astype(BF)
                lines = pl.ds(base + hh * HD, HD)
                dv[lines, :] = dot_t(do_t[inside], prob).astype(BF)
                dk[lines, :] = dot_t(qt_ref[lines, :], ds).astype(BF)
                dq[lines, :] = (dot(k_t_ref[i, inside, :], ds) * (HD**-0.5)).astype(BF)
            return carry

        lax.fori_loop(0, 3, pair, 0)
        ones = jnp.ones((8, SEQ), BF)
        sums[0:8, :] = dot_t(ones, dq[...])
        sums[8:16, :] = dot_t(ones, dv[...])


LINES = SMALL // 128


def put_lines(vec, first, row):
    for i in range(row.shape[1] // 128):
        vec[pl.ds(first + i, 1), :] = row[:, i * 128 : (i + 1) * 128]


def frames_back_body(meta, raw, ins, outs, _, total, w, dy1, sem):
    grads = ins
    copies = [pltpu.make_async_copy(raw[0].at[i], w.at[i], sem.at[i]) for i in range(4)]
    copies.append(pltpu.make_async_copy(raw[1], dy1, sem.at[4]))
    for c in copies:
        c.start()
    for c in copies:
        c.wait()
    for m in range(3):
        rows = pl.ds(m * 256, 256)
        acc = None
        for rel in range(2):
            for side, left in enumerate(
                (w[rel * 2, rows, :384], w[rel * 2, rows, 384:], w[rel * 2 + 1, rows, :384])
            ):
                term = dot(left, grads[rel][side])
                acc = term if acc is None else acc + term
        total[rows, :] = acc
    for r in range(2):
        rows = pl.ds(r * HALF, HALF)
        outs[r][...] = dy1[rows, :] + total[:, r * HALF : (r + 1) * HALF].T


def frames_back(meta, dy1, turned, w):
    return kernel_call(
        frames_back_body,
        "frames_back",
        meta,
        [w, dy1],
        turned,
        [((HALF, D), F32)] * 2,
        [],
        [
            pltpu.VMEM((D, SEQ), F32),
            pltpu.VMEM(W_SHAPE, BF),
            pltpu.VMEM((SEQ, D), F32),
            pltpu.SemaphoreType.DMA((5,)),
        ],
        3.5,
    )


def near_body(meta, _, ins, outs, __):
    for half in range(2):
        keep, came = ins[half], ins[2 + half]
        for i in range(4):
            outs[2 + half][i] = (keep[4 + i].astype(F32) + came[4 + i].astype(F32)).astype(BF)
            outs[half][i] = (keep[i].astype(F32) + came[i].astype(F32)).astype(BF)


def near_sums(meta, keep, came):
    outs = kernel_call(
        near_body, "near_sums", meta, [], [*keep, *came], [((4, ROWS, D), BF)] * 4, [], [], 0.5
    )
    return outs[:2], outs[2:]


def z_body(meta, _, ins, outs, __):
    for half in range(2):
        keep, came = ins[half], ins[2 + half]
        cols = slice(half * D, (half + 1) * D)
        for i in range(4):
            outs[i][:, cols] = (keep[i].astype(F32) + came[i].astype(F32)).astype(outs[i].dtype)


ROW = (ROWS, 2 * D)


def z_sums(meta, keep, came):
    return kernel_call(
        z_body, "z_sums", meta, [], [*keep, *came], [(ROW, F32)] + [(ROW, BF)] * 3, [], [], 4.0
    )


def totals_body(meta, _, ins, outs, __):
    count = ins[0]
    grads, vec = outs
    square = jnp.zeros((1, 1), F32)
    for k in range(3):
        row, *came = ins[1 + 4 * k : 5 + 4 * k]
        total = row[...]
        for c in came:
            total = total + c[...].astype(F32)
        grads[k] = total
        square = square + jnp.sum(row_sum(total * total), 1, keepdims=True)
    lane = lax.broadcasted_iota(jnp.int32, (8, 128), 1)
    vec[...] = jnp.where(lane == 0, square, jnp.where(lane == 1, count[...], 0.0))


def totals(meta, count, parts):
    return kernel_call(
        totals_body,
        "totals",
        meta,
        [],
        [count, *parts],
        [((3, *parts[0].shape), F32), ((8, 128), F32)],
        [],
        [],
        1.0,
    )


def adamw_body(meta, raw, ins, outs, raw_outs, *scratch):
    square, vec, grads, small_w, small_m, small_v, aw, am, av, fw, fm, fv = ins
    norm_out, small_out = outs[0], outs[1:]
    new_a, new_f, sems = scratch
    frame_count = square[0:1, 1:2]
    small = vec[...]
    squares = square[0:1, 0:1] + jnp.sum(row_sum(small * small), 1, keepdims=True)
    norm = jnp.sqrt(squares) / frame_count
    norm_out[...] = norm
    factor = jnp.minimum(1.0, CLIP_NORM / norm) / frame_count
    copies = []
    for i in range(4):
        cols = slice((i % 2) * 384 + (i // 2) * D, (i % 2) * 384 + (i // 2) * D + 384)
        rate = RATE * 0.5 * SEQ**0.5 if i == 3 else RATE
        for k, v in enumerate(adamw(aw[i], am[i], av[i], grads[0, :, cols] * factor, rate, DECAY)):
            new_a[k, i] = v
    for k in range(3):
        copies.append(pltpu.make_async_copy(new_a.at[k], raw_outs[k], sems.at[k]))
        copies[-1].start()
    for i in range(2):
        for k, v in enumerate(adamw(fw[i], fm[i], fv[i], grads[1 + i] * factor, RATE, DECAY)):
            new_f[k, i] = v
    for k in range(3):
        copies.append(pltpu.make_async_copy(new_f.at[k], raw_outs[3 + k], sems.at[3 + k]))
        copies[-1].start()
    new_small = adamw(small_w[...], small_m[...], small_v[...], small * factor, SMALL_RATE, 0.0)
    for out, v in zip(small_out, new_small):
        out[...] = v
    for c in copies:
        c.wait()


def adamw_call(meta, square, vec, grads, small, state):
    shapes = [v.shape for v in state]
    return kernel_call(
        adamw_body,
        "adamw",
        meta,
        [],
        [square, vec, grads, *small, *state],
        [((1, 1), F32)] + [((LINES, 128), F32)] * 3,
        [(s, F32) for s in shapes],
        [
            pltpu.VMEM((3, *shapes[0]), F32),
            pltpu.VMEM((3, *shapes[3]), F32),
            pltpu.SemaphoreType.DMA((6,)),
        ],
        3.0,
    )


def put_out(meta, acc, outs, half):
    d = meta[0]
    for sel in range(2):
        for j in range(8):
            row = pl.multiple_of((d ^ MASKS[half][sel][j]) * ROWS, 16)
            outs[half * 2 + sel][j] = acc[half, pl.ds(row, ROWS), :]


GRAD_OUTS = [((8, ROWS, D), BF)] * 4
GRAD_SCRATCH = [pltpu.VMEM((2, D, D), BF)]


def ffn_grad(meta, left_o, left_r, right_o, right_r, outs, acc):
    for half in range(2):
        for i in range(2):
            total = dot(left_o[i], right_o[half]) + dot(left_r[i], right_r[half])
            acc[half, i * 384 : (i + 1) * 384, :] = total.astype(BF)
        put_out(meta, acc, outs, half)


def down_grad_body(meta, _, ins, outs, __, acc):
    dz_o, dz_r, f_o, f_r = ins
    ffn_grad(meta, dz_o, dz_r, f_o, f_r, outs, acc)


def down_grad_call(meta, *ins):
    return kernel_call(
        down_grad_body, "down_grad", meta, [], ins, GRAD_OUTS, [], GRAD_SCRATCH, 4.0
    )


def middle_body(meta, raw, ins, outs, raw_outs, acc, grads, dy1, da, out_sems, *scratch):
    attn = AttnBack(1, raw, scratch)
    attn.start()
    shared, shared_r, du0, du_r, *rest = ins
    sums_one, sent, qv = outs
    copies = [
        pltpu.make_async_copy(a, b, out_sems.at[i])
        for i, (a, b) in enumerate(zip([*[grads.at[i] for i in range(4)], dy1, da], raw_outs))
    ]
    ffn_grad(
        meta,
        shared.at[pl.ds(1, 2)],
        shared_r.at[pl.ds(1, 2)],
        du0,
        du_r,
        [grads.at[i] for i in range(4)],
        acc,
    )
    for c in copies[:4]:
        c.start()
    hidden_back([du0, *rest], (dy1, da, sums_one))
    for c in copies[4:]:
        c.start()
    for i in range(2):
        sent[3 + i] = da[:, i * 384 : (i + 1) * 384].T
    attn.run(da, sent.at[0], sent.at[1], sent.at[2], qv)
    for c in copies:
        c.wait()


def middle(meta, heads, w_attn, prob, shared, shared_r, du0, du_r, du1, dy2, yh, inv, s12, w):
    return kernel_call(
        middle_body,
        "up_grad_hidden_back_attn_back",
        meta,
        [*heads, w_attn, prob],
        [shared, shared_r, du0, du_r, du1, dy2, yh, inv, s12, w],
        [((8, D), F32), ((5, 384, SEQ), BF), ((16, 384), F32)],
        GRAD_OUTS + [((SEQ, D), F32), ((SEQ, D), BF)],
        GRAD_SCRATCH
        + [
            pltpu.VMEM((4, 8, ROWS, D), BF),
            pltpu.VMEM((SEQ, D), F32),
            pltpu.VMEM((SEQ, D), BF),
            pltpu.SemaphoreType.DMA((6,)),
        ]
        + AttnBack.SCRATCH,
        14.0,
    )


def attn_back_body(meta, raw, ins, outs, _, da, da_sem, *scratch):
    da_copy = pltpu.make_async_copy(raw[0], da, da_sem.at[0])
    da_copy.start()
    attn = AttnBack(0, raw[1:], scratch)
    attn.start()
    turned, qv = outs
    da_copy.wait()
    attn.run(da, turned.at[0], turned.at[1], turned.at[2], qv)


def attn_back(meta, heads, w_attn, prob, da):
    return kernel_call(
        attn_back_body,
        "attn_back",
        meta,
        [da, *heads, w_attn, prob],
        [],
        [((3, 384, SEQ), BF), ((16, 384), F32)],
        [],
        [pltpu.VMEM((SEQ, D), BF), pltpu.SemaphoreType.DMA((1,))] + AttnBack.SCRATCH,
        7.0,
    )


def attn_grad_body(meta, _, ins, outs, __, acc, x_t):
    xo, xr, zo, zr, turned, sent, sent_r, o_own, shared_r = ins[:9]
    qv0, qv1, sums_one, sums_two, db1 = ins[9:]
    vec = outs[4]
    for rel, qv in ((0, qv0), (1, qv1)):
        h = meta[1] ^ rel
        put_lines(vec, 3 * h, qv[0:1, :])
        put_lines(vec, 6 + 3 * h, qv[8:9, :])
    for line, sums, row in (
        (2, sums_one, 0),
        (3, sums_two, 0),
        (4, sums_one, 1),
        (5, sums_one, 2),
        (6, sums_two, 1),
        (7, sums_two, 2),
    ):
        put_lines(vec, 6 * line, sums[row : row + 1, :])
    for i in range(4):
        put_lines(vec, 48 + 6 * i, db1[i : i + 1, :])
    for i, v in enumerate((xo, xr, zo, zr)):
        x_t[:, i * HALF : (i + 1) * HALF] = v[...].T
    for half, side, k in ((1, 0, 2), (0, 0, 0), (0, 1, 1)):
        for m in range(3):
            rows = pl.ds(m * 256, 256)
            total = dot_t(x_t[rows, :SEQ], turned[k]) + dot_t(x_t[rows, SEQ:], sent_r[k])
            acc[half, rows, side * 384 : (side + 1) * 384] = total.astype(BF)
    for i in range(2):
        total = dot_t(sent[3 + i], o_own[...]) + dot_t(sent_r[3 + i], shared_r[0])
        acc[1, i * 384 : (i + 1) * 384, 384:] = total.astype(BF)
    for half in range(2):
        put_out(meta, acc, outs, half)


def attn_grad(meta, xs, turned, sent, sent_r, o_own, shared_r, small):
    return kernel_call(
        attn_grad_body,
        "attn_grad",
        meta,
        [],
        [*xs, turned, sent, sent_r, o_own, shared_r, *small],
        GRAD_OUTS + [((LINES, 128), F32)],
        [],
        GRAD_SCRATCH + [pltpu.VMEM((D, 2 * SEQ), BF)],
        5.0,
    )


def adamw(weight, moment_one, moment_two, grad, rate, decay):
    new_one = BETA_ONE * moment_one + (1.0 - BETA_ONE) * grad
    new_two = BETA_TWO * moment_two + (1.0 - BETA_TWO) * grad * grad
    fixed_one = new_one / (1.0 - BETA_ONE**STEP)
    fixed_two = new_two / (1.0 - BETA_TWO**STEP)
    update = fixed_one / (jnp.sqrt(fixed_two) + ADAM_EPS) + decay * weight
    return (weight - rate * update, new_one, new_two)


def after(v, *deps):
    return lax.optimization_barrier((v, *deps))[0]


def other_core(v):
    return lax.ppermute(v, "tensor", [(0, 1), (1, 0)])


def shift(v, mask, n):
    return lax.ppermute(v, "dp", [(i, i ^ mask) for i in range(n)])


class Gather:
    def __init__(self, shard, n):
        self.n, self.shard, self.mark = n, shard, shard

    def z_all(self, *deps):
        if self.n == BLOCKS:
            shard = after(self.shard, *deps)
            self.z = [shard] + [shift(shard, z, self.n) for z in Z_MASKS[1:]]
            self.mark = shard

    def z_wait(self, *deps):
        if self.n == BLOCKS:
            self.z = after(tuple(self.z), *deps)
            self.mark = self.z[1:]

    def far_wait(self, *deps):
        if self.n == BLOCKS:
            self.far_side = after(tuple(self.far_side), *deps)
            self.mark = tuple(self.far_side)

    def near_wait(self, *deps):
        if self.n == BLOCKS:
            self.came = after(tuple(self.came), *deps)
            self.mark = tuple(self.came)

    def near(self, *deps):
        if self.n != BLOCKS:
            return
        parts = after(tuple(self.z), *deps)
        self.own = [
            jnp.stack([v[:, half * D : (half + 1) * D] for v in parts]) for half in range(2)
        ]
        self.mark = tuple(self.own)
        self.came = [shift(s, step[0], self.n) for s, step in zip(self.own, (STEP_A, STEP_B))]

    def far(self, *deps):
        if self.n != BLOCKS:
            return
        came = after(tuple(self.came), *deps)
        self.own = [jnp.concatenate([s, c]) for s, c in zip(self.own, came)]
        self.mark = tuple(self.own)
        self.far_side = [shift(o, step[1], self.n) for o, step in zip(self.own, (STEP_A, STEP_B))]

    def core(self, *deps):
        if self.n == BLOCKS:
            self.own_other = [other_core(o) for o in after(tuple(self.own), *deps)]
            self.mark = tuple(self.own_other)

    def pieces(self, *deps):
        if self.n == BLOCKS:
            far = after(tuple(self.far_side), *deps)
            result = []
            for half in range(2):
                far_other = other_core(far[half])
                result += [self.own[half], far[half], self.own_other[half], far_other]
            self.mark = far[1]
            return result
        full = lax.all_gather(self.shard, "dp", axis=0, tiled=True)
        blocks = full.reshape(BLOCKS, ROWS, 2 * D)
        result = []
        for half in range(2):
            cols = slice(half * D, (half + 1) * D)
            own = [blocks[jnp.array(m), :, cols] for m in MASKS[half]]
            result += own + [other_core(v) for v in own]
        return result


def added(*parts):
    total = parts[0].astype(F32)
    for p in parts[1:]:
        total = total + p.astype(F32)
    return total


class Scatter:
    def __init__(self, meta, pieces, n):
        self.meta = meta
        self.n, self.pieces, self.mark = n, pieces, pieces[0]
        if n == BLOCKS:
            self.keep = [pieces[0], pieces[2]]
            self.came = [
                shift(v, step[1], n) for v, step in zip((pieces[1], pieces[3]), (STEP_A, STEP_B))
            ]

    def near(self, *deps):
        if self.n != BLOCKS:
            return
        came = after(tuple(self.came), *deps)
        self.keep, send = near_sums(self.meta, self.keep, came)
        self.came = [shift(s, step[0], self.n) for s, step in zip(send, (STEP_A, STEP_B))]
        self.mark = tuple(send)

    def wait(self, *deps):
        if self.n == BLOCKS:
            self.came = after(tuple(self.came), *deps)
            self.mark = tuple(self.came)

    def z_all(self, *deps):
        if self.n != BLOCKS:
            return
        came = after(tuple(self.came), *deps)
        self.row, *sends = z_sums(self.meta, self.keep, came)
        self.mark = tuple(sends)
        self.came = [shift(s, z, self.n) for s, z in zip(sends, Z_MASKS[1:])]

    def parts(self, *deps):
        if self.n == BLOCKS:
            return [self.row, *after(tuple(self.came), *deps)]
        whole = self.whole()
        zero = jnp.zeros(whole.shape, BF)
        return [whole, zero, zero, zero]

    def whole(self):
        result = []
        for half in range(2):
            order = MASKS[half][0] + MASKS[half][1]
            back = [order.index(i) for i in range(BLOCKS)]
            full = jnp.concatenate(self.pieces[2 * half : 2 * half + 2])[jnp.array(back)]
            full = full.reshape(D, D).astype(F32)
            result.append(lax.psum_scatter(full, "dp", scatter_dimension=0, tiled=True))
        return jnp.concatenate(result, 1)


class Everywhere:
    def __init__(self, v, n):
        self.n, self.v = n, v

    def core(self, *deps):
        if self.n == BLOCKS:
            v = after(self.v, *deps)
            self.v = v + other_core(v)

    def step(self, masks, *deps):
        if self.n == BLOCKS:
            v = after(self.v, *deps)
            came = [shift(v, m, self.n) for m in masks]
            self.v = v + came[0] if len(came) == 1 else (v + came[0]) + (came[1] + came[2])

    def total(self):
        return self.v if self.n == BLOCKS else lax.psum(self.v, ("dp", "tensor"))


XY_MASKS = (1, 2, 3)


def last_steps(small, every):
    if every.n != BLOCKS:
        return small.total(), every.total()
    lines = every.v.shape[0]
    every.v = jnp.concatenate([every.v, small.v])
    every.step(XY_MASKS)
    v = every.v[:lines]
    near, both, far = [
        shift(s, m, every.n) for s, m in zip((v, every.v, v), Z_MASKS[1:])
    ]
    return every.v[lines:] + both[lines:], (v + near) + (both[:lines] + far)


def per_device(
    frames,
    cotangent,
    lengths,
    attn_w,
    attn_m,
    attn_v,
    ffn_w,
    ffn_m,
    ffn_v,
    small_w,
    small_m,
    small_v,
):
    n = lax.axis_size("dp")
    t = lax.axis_index("tensor")
    d = lax.axis_index("dp") if n == BLOCKS else 0
    length = lax.dynamic_index_in_dim(lengths[:, 0], t, 0, keepdims=False)
    meta = jnp.stack([jnp.asarray(d, jnp.int32), jnp.asarray(t, jnp.int32), length])
    s12 = small_w.reshape(12, D)
    half = SEQ // lax.axis_size("tensor")
    count = jnp.sum(jnp.clip(lengths - t * half, 0, half)).astype(F32).reshape(1, 1)

    def pick(v, i):
        return lax.dynamic_index_in_dim(v[:, 0], i, 0, keepdims=False)

    def joined(own, other):
        return jnp.where(t == 0, jnp.stack([own, other]), jnp.stack([other, own]))[:, None]

    attn = Gather(jnp.concatenate([attn_w[i] for i in range(4)], 1).astype(BF), n)
    up = Gather(ffn_w[0].astype(BF), n)
    down = Gather(ffn_w[1].astype(BF), n)
    attn.z_all()
    frames_r = other_core(frames)
    xo, zr = pick(frames, t), pick(frames, 1 - t)
    xr, zo = pick(frames_r, t), pick(frames_r, 1 - t)
    cotangent_r = other_core(cotangent)
    co, cr = pick(cotangent, t), pick(cotangent_r, t)
    attn.near(xr, cr)
    up.z_all(attn.mark)
    attn.far()
    up.near(attn.mark)
    attn.core()
    attn_pieces = attn.pieces(up.mark)
    down.z_all(attn.mark)
    up.far(attn.mark)
    first = attn_first(after(meta, up.mark, down.mark, count), xo, xr, attn_pieces, s12)
    later, o_first, out_w, *heads_first = first
    *heads_first, w_attn, prob_first = heads_first
    down.near(o_first)
    second = attn_second(after(meta, down.mark), xo, xr, s12, later, o_first, out_w)
    yh, inv, hb, shared, *heads_second = second
    *heads_second, prob_second = heads_second
    heads, prob = (heads_first, heads_second), (prob_first, prob_second)
    down.near_wait(inv)
    up.far_wait(inv)
    up.core(down.mark)
    up_pieces = up.pieces()
    down.far()
    down_far = down.mark
    down.core(up_pieces[1], up_pieces[3])
    f0, f1, gp, w_up = ffn_up(after(meta, down_far), hb, up_pieces, s12)
    down.far_wait(gp)
    down_pieces = down.pieces()
    f_r = other_core(after(f1, *down_pieces))
    shared_r = other_core(after(shared, *down_pieces))
    out_o, out_r, dz, dz_t, dy2, sums_two, w_down = ffn_down(
        meta, f0, f1, down_pieces, yh, co, cr, s12
    )
    dz_r = other_core(after(dz_t, f_r, shared_r))
    du0, du1, db1 = ffn_back(after(meta, f_r, shared_r), dz, w_down, gp)
    du_r = other_core(after(du1, dz_r))
    down_sum = Scatter(
        meta,
        down_grad_call(after(meta, db1), dz_t, dz_r, f0, f_r), n
    )
    *up_grad, dy1, da = middle(
        after(meta, down_sum.mark),
        heads[1],
        w_attn,
        prob[1],
        shared,
        shared_r,
        du0,
        du_r,
        du1,
        dy2,
        yh,
        inv,
        s12,
        w_up,
    )
    sums_one, sent, qv1, *up_grad = up_grad
    down_sum.wait(qv1)
    up_sum = Scatter(meta, after(tuple(up_grad), down_sum.mark), n)
    down_sum.near()
    sent_r = other_core(after(sent, down_sum.mark))
    turned0, qv0 = attn_back(after(meta, down_sum.mark), heads[0], w_attn, prob[0], da)
    down_sum.z_all(qv0, sent_r)
    *attn_grads, vec = attn_grad(
        after(meta, down_sum.mark),
        (xo, xr, zo, zr),
        turned0,
        sent,
        sent_r,
        heads[0][3],
        shared_r,
        (qv0, qv1, sums_one, sums_two, db1),
    )
    up_sum.wait(attn_grads[0])
    up_sum.near()
    down_sum.wait(up_sum.mark)
    small = Everywhere(vec, n)
    attn_sum = Scatter(meta, after(tuple(attn_grads), down_sum.mark), n)
    small.core(down_sum.mark)
    small.step((4,))
    up_sum.wait()
    up_sum.z_all(small.v)
    small_state = [v.reshape(LINES, 128) for v in (small_w, small_m, small_v)]
    attn_sum.near(up_sum.mark)
    dx_o, dx_r = frames_back(after(meta, attn_sum.mark), dy1, (turned0, sent), w_attn)
    attn_sum.wait(dx_o)
    up_sum.wait(dx_o)
    attn_sum.z_all(up_sum.mark)
    dx_other = other_core(after(dx_r, attn_sum.mark))
    out_other = other_core(after(out_r, attn_sum.mark))
    frames_grad = joined(dx_o, dx_other)
    output = joined(out_o, out_other)
    grads, square = totals(
        meta, count, attn_sum.parts(frames_grad, output) + up_sum.parts() + down_sum.parts()
    )
    every = Everywhere(square, n)
    every.core()
    small_all, square_all = last_steps(small, every)
    state = (attn_w, attn_m, attn_v, ffn_w, ffn_m, ffn_v)
    norm, small_new, small_m_new, small_v_new, *new_state = adamw_call(
        meta, square_all, small_all, grads, small_state, state
    )
    attn_new, attn_m_new, attn_v_new, ffn_new, ffn_m_new, ffn_v_new = new_state
    grad_norm = norm[0, 0]
    small_new, small_m_new, small_v_new = [
        v.reshape(SMALL) for v in (small_new, small_m_new, small_v_new)
    ]
    return (
        output,
        frames_grad,
        grad_norm,
        attn_new,
        attn_m_new,
        attn_v_new,
        ffn_new,
        ffn_m_new,
        ffn_v_new,
        small_new,
        small_m_new,
        small_v_new,
    )


def solution(mesh):
    rows = P(None, "dp", "tensor", None)
    weights = P(None, "dp", "tensor")
    in_specs = (rows, rows, P(None, "dp")) + (weights,) * 6 + (P(),) * 3
    out_specs = (rows, rows, P()) + (weights,) * 6 + (P(),) * 3
    return jax.shard_map(
        per_device, mesh=mesh, in_specs=in_specs, out_specs=out_specs, check_vma=False
    )
```

```python
import math

import jax
import jax.numpy as jnp
from jax import lax
from jax.experimental import pallas as pl
from jax.experimental.pallas import tpu as pltpu
from jax.sharding import PartitionSpec as P

HD = 64
D = 768
FF = 3072
SEQ = 512
HALF = SEQ // 2
STEP = 10
SMALL = 9216
PAIRS = 6
BLOCKS = 16
ROWS = D // BLOCKS

EPS_NORM = 1e-05
MASK_FILL = -1e30
BETA_ONE = 0.9
BETA_TWO = 0.999
ADAM_EPS = 1e-08
CLIP_NORM = 0.1
RATE = 0.1
SMALL_RATE = 1.5
DECAY = 0.01

BF = jnp.bfloat16
F32 = jnp.float32

STEP_A = (2, 1)
STEP_B = (1, 2)
Z_MASKS = (0, 4, 8, 12)
MASKS = tuple(
    (
        tuple(z for z in Z_MASKS) + tuple(z + near for z in Z_MASKS),
        tuple(z + far for z in Z_MASKS) + tuple(z + near + far for z in Z_MASKS),
    )
    for near, far in (STEP_A, STEP_B)
)


def dot(left, right):
    return jnp.dot(left, right, preferred_element_type=F32)


def dot_t(left, right):
    return lax.dot_general(left, right, (((1,), (1,)), ((), ())), preferred_element_type=F32)


def gelu_pair(u):
    phi = 0.5 * lax.erf(u * math.sqrt(0.5)) + 0.5
    return u * phi, phi + u * jnp.exp(-0.5 * u * u) * (1.0 / math.sqrt(2.0 * math.pi))


HBM = pl.BlockSpec(memory_space=pltpu.HBM)
SMEM = pl.BlockSpec(memory_space=pltpu.SMEM)


VMEM = pl.BlockSpec(memory_space=pltpu.VMEM)


def kernel_call(body, name, meta, raw, ins, outs, raw_outs, scratch, micros):
    n_raw, n_in, n_out, n_raw_out = len(raw), len(ins), len(outs), len(raw_outs)

    def run(meta_ref, *refs):
        cuts = [0, n_raw, n_in, n_out, n_raw_out]
        for i in range(1, 5):
            cuts[i] += cuts[i - 1]
        groups = [refs[cuts[i] : cuts[i + 1]] for i in range(4)]
        body(meta_ref, *groups, *refs[cuts[4] :])

    held = sum(
        math.prod(v.shape) * (2 if v.dtype == BF else 4) for v in scratch if v.dtype in (BF, F32)
    )
    return pl.pallas_call(
        run,
        name=name,
        in_specs=[SMEM] + [HBM] * n_raw + [VMEM] * n_in,
        out_specs=[VMEM] * n_out + [HBM] * n_raw_out,
        out_shape=[jax.ShapeDtypeStruct(s, d) for s, d in outs]
        + [pltpu.HBM(s, d) for s, d in raw_outs],
        scratch_shapes=scratch,
        compiler_params=pltpu.CompilerParams(vmem_limit_bytes=held + SPARE),
        cost_estimate=pl.CostEstimate(
            flops=int(micros * 1.15e9), bytes_accessed=0, transcendentals=0
        ),
    )(meta, *[pltpu.with_memory_space_constraint(v, pltpu.HBM) for v in raw], *ins)


SPARE = 8 * 2**20
W_SHAPE = (4, D, D)


def place(meta, pieces, w):
    d = meta[0]
    for part in range(4):
        rel, half = divmod(part, 2)
        for sel in range(2):
            src = pieces[half * 4 + rel * 2 + sel]
            for j in range(8):
                row = pl.multiple_of((d ^ MASKS[half][sel][j]) * ROWS, 16)
                w[part, pl.ds(row, ROWS), :] = src[j]


def chunk(c):
    return pl.ds(pl.multiple_of(c * CHUNK, CHUNK), CHUNK)


CHUNK = 256
PER_PART = D // CHUNK


def row_sum(v):
    return jnp.sum(v, 0, keepdims=True)


def attend(meta, q_ref, k_ref, v_ref, qt_ref, ot_ref, o_ref, p_buf, p_out, p_sems):
    t, length = meta[1], meta[2]
    row = lax.broadcasted_iota(jnp.int32, (SEQ, 1), 0)
    position = jnp.where(row < HALF, row + t * HALF, row + (1 - t) * HALF - HALF)
    valid = position < length
    lane = lax.broadcasted_iota(jnp.int32, (SEQ, 128), 1)

    def pair(i, carry):
        keys = k_ref[i]
        q_t = q_ref[i].T
        lines = pl.ds(pl.multiple_of(i * 128, 128), 128)
        qt_ref[lines, :] = q_t
        v_t = v_ref[i].T
        halves = []
        for hh in range(2):
            own = (lane < HD) if hh == 0 else (lane >= HD)
            s = dot(jnp.where(own, keys, jnp.zeros_like(keys)), q_t)
            s = jnp.where(valid, s, MASK_FILL)
            e = jnp.exp(s - jnp.max(s, 0, keepdims=True))
            prob = (e * (1.0 / jnp.sum(e, 0, keepdims=True))).astype(BF)
            head = 2 * i + hh
            p_buf[head] = prob
            pltpu.make_async_copy(p_buf.at[head], p_out.at[head], p_sems.at[head]).start()
            halves.append(dot(v_t[hh * HD : (hh + 1) * HD], prob))
        o_t = jnp.concatenate(halves, 0).astype(BF)
        ot_ref[lines, :] = o_t
        o_ref[:, lines] = o_t.T
        return carry

    lax.fori_loop(0, 3, pair, 0)


def attend_wait(p_buf, p_out, p_sems):
    for i in range(6):
        pltpu.make_async_copy(p_buf.at[i], p_out.at[i], p_sems.at[i]).wait()


TURNED = ((384, SEQ), BF)
HEADS = [((3, SEQ, 128), BF), ((3, SEQ, 128), BF), TURNED, TURNED]
ATTEND_SCRATCH = [
    pltpu.VMEM((6, SEQ, SEQ), BF),
    pltpu.SemaphoreType.DMA((6,)),
    pltpu.SemaphoreType.DMA((5,)),
]


def attn_first_body(meta, _, ins, outs, raw_outs, p_buf, p_sems, sems, w, q_ref, *head_refs):
    xo, xr, s12, *pieces = ins
    later, o_ref, out_w = outs
    place(meta, pieces, w)
    copies = [
        pltpu.make_async_copy(a, raw_outs[i], sems.at[i]) for i, a in enumerate([*head_refs, w])
    ]
    copies[4].start()
    t = meta[1]
    for rel in range(2):
        if rel == 0:
            targets = q_ref, head_refs[0], head_refs[1]
        else:
            targets = later.at[0], later.at[1], later.at[2]
        cols = pl.ds(pl.multiple_of((t ^ rel) * 384, 128), 384)
        bq = s12[0:1, cols]
        bv = s12[1:2, cols]
        for r, x in ((0, xo), (1, xr)):
            rows = pl.ds(r * HALF, HALF)
            qk = dot(x[...], w[rel * 2])
            q = (qk[:, :384] + bq).astype(BF) * jnp.asarray(HD**-0.5, BF)
            k = qk[:, 384:].astype(BF)
            v = (dot(x[...], w[rel * 2 + 1, :, :384]) + bv).astype(BF)
            for ref, value in zip(targets, (q, k, v)):
                for i in range(3):
                    ref[i, rows, :] = value[:, i * 128 : (i + 1) * 128]
        out_w[rel] = w[rel * 2 + 1, :, 384:]
    k_ref, v_ref, qt_ref, ot_ref = head_refs
    attend(meta, q_ref, k_ref, v_ref, qt_ref, ot_ref, o_ref, p_buf, raw_outs[5], p_sems)
    for c in copies[:4]:
        c.start()
    for c in copies:
        c.wait()
    attend_wait(p_buf, raw_outs[5], p_sems)


def attn_first(meta, xo, xr, pieces, s12):
    return kernel_call(
        attn_first_body,
        "attn_first",
        meta,
        [],
        [xo, xr, s12, *pieces],
        [((3, 3, SEQ, 128), BF), ((SEQ, 384), BF), ((2, D, 384), BF)],
        HEADS + [(W_SHAPE, BF), ((6, SEQ, SEQ), BF)],
        ATTEND_SCRATCH
        + [pltpu.VMEM(W_SHAPE, BF), pltpu.VMEM((3, SEQ, 128), BF)]
        + [pltpu.VMEM(*h) for h in HEADS],
        9.0,
    )


def attn_second_body(meta, _, ins, outs, raw_outs, p_buf, p_sems, sems, o_ref, qt_ref, ot_ref):
    xo, xr, s12, later, o_first, out_w = ins
    yh, rs, hb, shared = outs
    held = later.at[1], later.at[2], qt_ref, ot_ref
    copies = [pltpu.make_async_copy(a, raw_outs[i], sems.at[i]) for i, a in enumerate(held)]
    for c in copies[:2]:
        c.start()
    attend(
        meta,
        later.at[0],
        later.at[1],
        later.at[2],
        qt_ref,
        ot_ref,
        o_ref,
        p_buf,
        raw_outs[4],
        p_sems,
    )
    for c in copies[2:]:
        c.start()
    bo, g1, c1 = s12[2:3, :], s12[4:5, :], s12[5:6, :]
    for r, x in ((0, xo), (1, xr)):
        rows = pl.ds(r * HALF, HALF)
        a = dot_t(o_first[rows, :], out_w[0]) + dot_t(o_ref[rows, :], out_w[1])
        y = x[...].astype(F32) + a + bo
        centred = y - jnp.mean(y, -1, keepdims=True)
        inv = lax.rsqrt(jnp.mean(centred * centred, -1, keepdims=True) + EPS_NORM)
        hat = centred * inv
        yh[rows, :] = hat
        rs[rows, :] = inv
        hb[rows, :] = (hat * g1 + c1).astype(BF)
    shared[0] = ot_ref[...]
    for i in range(2):
        shared[1 + i] = hb[:, i * 384 : (i + 1) * 384].T
    for c in copies:
        c.wait()
    attend_wait(p_buf, raw_outs[4], p_sems)


def attn_second(meta, xo, xr, s12, later, o_first, out_w):
    return kernel_call(
        attn_second_body,
        "attn_second",
        meta,
        [],
        [xo, xr, s12, later, o_first, out_w],
        [((SEQ, D), F32), ((SEQ, 1), F32), ((SEQ, D), BF), ((3, 384, SEQ), BF)],
        HEADS + [((6, SEQ, SEQ), BF)],
        ATTEND_SCRATCH + [pltpu.VMEM((SEQ, 384), BF), pltpu.VMEM(*TURNED), pltpu.VMEM(*TURNED)],
        8.0,
    )


def ffn_up_body(meta, _, ins, outs, __):
    hb, s12, *pieces = ins
    f0, f1, gp, w = outs
    place(meta, pieces, w)
    for part in range(4):
        rel, half = divmod(part, 2)
        bias_row = pl.ds(8 + 2 * (meta[1] ^ rel) + half, 1)
        f_ref = (f0, f1)[rel]
        for c in range(PER_PART):
            cols = slice(c * CHUNK, (c + 1) * CHUNK)
            u = dot(hb[...], w[part, :, cols]) + s12[bias_row, cols]
            f, slope = gelu_pair(u)
            f_ref[half, :, cols] = f.astype(BF)
            gp[part, :, cols] = slope.astype(BF)


SIDE = ((2, SEQ, D), BF)
SLABS = ((2, 384, SEQ), BF)


def ffn_up(meta, hb, pieces, s12):
    return kernel_call(
        ffn_up_body,
        "ffn_up",
        meta,
        [],
        [hb, s12, *pieces],
        [SIDE, SIDE, ((4, SEQ, D), BF), (W_SHAPE, BF)],
        [],
        [],
        5.0,
    )


def norm_back(grad, hat, inv, gain):
    scaled = grad * gain
    return inv * (
        scaled
        - jnp.mean(scaled, -1, keepdims=True)
        - hat * jnp.mean(scaled * hat, -1, keepdims=True)
    )


def ffn_down_body(meta, _, ins, outs, __):
    f0, f1, yh, co, cr, s12, *pieces = ins
    out_o, out_r, dz, dz_t, dy2, sums, w = outs
    place(meta, pieces, w)
    t, length = meta[1], meta[2]
    b2 = s12[3:4, :]
    g1, c1, g2, c2 = s12[4:5, :], s12[5:6, :], s12[6:7, :], s12[7:8, :]
    fs = (f0, f1)
    for part in range(4):
        rel, half = divmod(part, 2)
        z = dot_t(fs[rel][half], w[part])
        dy2[...] = z if part == 0 else dy2[...] + z
    totals = [jnp.zeros((1, D), F32)] * 3
    for r, cot, out in ((0, co, out_o), (1, cr, out_r)):
        rows = pl.ds(r * HALF, HALF)
        y = yh[rows, :] * g1 + c1 + dy2[rows, :] + b2
        centred = y - jnp.mean(y, -1, keepdims=True)
        inv = lax.rsqrt(jnp.mean(centred * centred, -1, keepdims=True) + EPS_NORM)
        hat = centred * inv
        out[...] = (hat * g2 + c2).astype(BF)
        row = lax.broadcasted_iota(jnp.int32, (HALF, 1), 0)
        valid = row + (t ^ r) * HALF < length
        dout = jnp.where(valid, cot[...].astype(F32), 0.0)
        grad = norm_back(dout, hat, inv, g2)
        dy2[rows, :] = grad
        dz[rows, :] = grad.astype(BF)
        totals = [a + row_sum(b) for a, b in zip(totals, (grad, dout * hat, dout))]
    for i in range(3):
        sums[i : i + 1, :] = totals[i]
    for i in range(2):
        dz_t[i] = dz[:, i * 384 : (i + 1) * 384].T


def ffn_down(meta, f0, f1, pieces, yh, co, cr, s12):
    return kernel_call(
        ffn_down_body,
        "ffn_down",
        meta,
        [],
        [f0, f1, yh, co, cr, s12, *pieces],
        [
            ((HALF, D), BF),
            ((HALF, D), BF),
            ((SEQ, D), BF),
            SLABS,
            ((SEQ, D), F32),
            ((8, D), F32),
            (W_SHAPE, BF),
        ],
        [],
        [],
        5.0,
    )


def ffn_back_body(meta, _, ins, outs, __):
    dz, gp, w = ins
    du0, du1, db1 = outs
    for part in (2, 3, 0, 1):
        rel, half = divmod(part, 2)
        bias_row = pl.ds(2 * (meta[1] ^ rel) + half, 1)
        du_ref = (du0, du1)[rel]
        for c in range(PER_PART):
            cols = slice(c * CHUNK, (c + 1) * CHUNK)
            du = dot(dz[...], w[part, :, cols]) * gp[part, :, cols].astype(F32)
            db1[bias_row, cols] = row_sum(du)
            du_ref[half, :, cols] = du.astype(BF)


def ffn_back(meta, dz, w, gp):
    return kernel_call(
        ffn_back_body,
        "ffn_back",
        meta,
        [],
        [dz, gp, w],
        [SIDE, SIDE, ((4, D), F32)],
        [],
        [],
        3.5,
    )


def hidden_back(ins, outs):
    du0, du1, dy2, yh, inv, small, w = ins
    dy1, da, sums = outs
    dus = (du0, du1)
    dy1[...] = dy2[...]
    for rel in range(2):

        def step(half, carry, rel=rel):
            dy1[...] += dot_t(dus[rel][half], w[2 * rel + half])
            return carry

        lax.fori_loop(0, 2, step, 0)
    g1 = small[4:5, :]
    totals = [jnp.zeros((1, D), F32)] * 3
    for r in range(2):
        rows = pl.ds(r * HALF, HALF)
        dh = dy1[rows, :]
        hat = yh[rows, :]
        grad = norm_back(dh, hat, inv[rows, :], g1)
        dy1[rows, :] = grad
        da[rows, :] = grad.astype(BF)
        totals = [a + row_sum(b) for a, b in zip(totals, (grad, dh * hat, dh))]
    for i in range(3):
        sums[i : i + 1, :] = totals[i]


class AttnBack:
    SCRATCH = [
        pltpu.VMEM((D, D), BF),
        pltpu.VMEM((6, SEQ, SEQ), BF),
        pltpu.SemaphoreType.DMA((6,)),
        pltpu.SemaphoreType.DMA((5,)),
        pltpu.VMEM((3, 128, SEQ), BF),
        pltpu.VMEM((3, 128, SEQ), BF),
    ] + [pltpu.VMEM(*h) for h in HEADS]

    def __init__(self, rel, raw, scratch):
        *head_in, w_in, self.p_in = raw
        self.w, self.p_buf, self.p_sems, sems, self.do_t, self.k_t, *self.heads = scratch
        self.copies = [pltpu.make_async_copy(w_in.at[rel * 2 + 1], self.w, sems.at[4])]
        self.copies += [
            pltpu.make_async_copy(a, b, sems.at[i])
            for i, (a, b) in enumerate(zip(head_in, self.heads))
        ]

    def start(self):
        for c in self.copies:
            c.start()
        for i in range(6):
            pltpu.make_async_copy(self.p_in.at[i], self.p_buf.at[i], self.p_sems.at[i]).start()

    def run(self, da, dq, dk, dv, sums):
        w, do_t_ref, k_t_ref = self.w, self.do_t, self.k_t
        k_ref, v_ref, qt_ref, ot_ref = self.heads
        self.copies[0].wait()
        do = dot(da[...], w[:, 384:]).astype(BF)
        for c in self.copies[1:]:
            c.wait()
        for i in range(3):
            do_t_ref[i] = do[:, i * 128 : (i + 1) * 128].T
            k_t_ref[i] = k_ref[i].T
        lane = lax.broadcasted_iota(jnp.int32, (SEQ, 128), 1)

        def pair(i, carry):
            vp = v_ref[i]
            do_t = do_t_ref[i]
            base = pl.multiple_of(i * 128, 128)
            both = do_t.astype(F32) * ot_ref[pl.ds(base, 128), :].astype(F32)
            for hh in range(2):
                own = (lane < HD) if hh == 0 else (lane >= HD)
                inside = slice(hh * HD, (hh + 1) * HD)
                delta = row_sum(both[inside])
                slope = dot(jnp.where(own, vp, jnp.zeros_like(vp)), do_t)
                head = 2 * i + hh
                pltpu.make_async_copy(
                    self.p_in.at[head], self.p_buf.at[head], self.p_sems.at[head]
                ).wait()
                prob = self.p_buf[head]
                ds = (prob.astype(F32) * (slope - delta)).astype(BF)
                lines = pl.ds(base + hh * HD, HD)
                dv[lines, :] = dot_t(do_t[inside], prob).astype(BF)
                dk[lines, :] = dot_t(qt_ref[lines, :], ds).astype(BF)
                dq[lines, :] = (dot(k_t_ref[i, inside, :], ds) * (HD**-0.5)).astype(BF)
            return carry

        lax.fori_loop(0, 3, pair, 0)
        ones = jnp.ones((8, SEQ), BF)
        sums[0:8, :] = dot_t(ones, dq[...])
        sums[8:16, :] = dot_t(ones, dv[...])


LINES = SMALL // 128


def put_lines(vec, first, row):
    for i in range(row.shape[1] // 128):
        vec[pl.ds(first + i, 1), :] = row[:, i * 128 : (i + 1) * 128]


def frames_back_body(meta, raw, ins, outs, _, total, w, dy1, sem):
    grads = ins
    copies = [pltpu.make_async_copy(raw[0].at[i], w.at[i], sem.at[i]) for i in range(4)]
    copies.append(pltpu.make_async_copy(raw[1], dy1, sem.at[4]))
    for c in copies:
        c.start()
    for c in copies:
        c.wait()
    for m in range(3):
        rows = pl.ds(m * 256, 256)
        acc = None
        for rel in range(2):
            for side, left in enumerate(
                (w[rel * 2, rows, :384], w[rel * 2, rows, 384:], w[rel * 2 + 1, rows, :384])
            ):
                term = dot(left, grads[rel][side])
                acc = term if acc is None else acc + term
        total[rows, :] = acc
    for r in range(2):
        rows = pl.ds(r * HALF, HALF)
        outs[r][...] = dy1[rows, :] + total[:, r * HALF : (r + 1) * HALF].T


def frames_back(meta, dy1, turned, w):
    return kernel_call(
        frames_back_body,
        "frames_back",
        meta,
        [w, dy1],
        turned,
        [((HALF, D), F32)] * 2,
        [],
        [
            pltpu.VMEM((D, SEQ), F32),
            pltpu.VMEM(W_SHAPE, BF),
            pltpu.VMEM((SEQ, D), F32),
            pltpu.SemaphoreType.DMA((5,)),
        ],
        3.5,
    )


def near_body(meta, _, ins, outs, __):
    for half in range(2):
        keep, came = ins[half], ins[2 + half]
        for i in range(4):
            outs[2 + half][i] = (keep[4 + i].astype(F32) + came[4 + i].astype(F32)).astype(BF)
            outs[half][i] = (keep[i].astype(F32) + came[i].astype(F32)).astype(BF)


def near_sums(meta, keep, came):
    outs = kernel_call(
        near_body, "near_sums", meta, [], [*keep, *came], [((4, ROWS, D), BF)] * 4, [], [], 0.5
    )
    return outs[:2], outs[2:]


def z_body(meta, _, ins, outs, __):
    for half in range(2):
        keep, came = ins[half], ins[2 + half]
        cols = slice(half * D, (half + 1) * D)
        for i in range(4):
            outs[i][:, cols] = (keep[i].astype(F32) + came[i].astype(F32)).astype(outs[i].dtype)


ROW = (ROWS, 2 * D)


def z_sums(meta, keep, came):
    return kernel_call(
        z_body, "z_sums", meta, [], [*keep, *came], [(ROW, F32)] + [(ROW, BF)] * 3, [], [], 4.0
    )


def totals_body(meta, _, ins, outs, __):
    count = ins[0]
    grads, vec = outs
    square = jnp.zeros((1, 1), F32)
    for k in range(3):
        row, *came = ins[1 + 4 * k : 5 + 4 * k]
        total = row[...]
        for c in came:
            total = total + c[...].astype(F32)
        grads[k] = total
        square = square + jnp.sum(row_sum(total * total), 1, keepdims=True)
    lane = lax.broadcasted_iota(jnp.int32, (8, 128), 1)
    vec[...] = jnp.where(lane == 0, square, jnp.where(lane == 1, count[...], 0.0))


def totals(meta, count, parts):
    return kernel_call(
        totals_body,
        "totals",
        meta,
        [],
        [count, *parts],
        [((3, *parts[0].shape), F32), ((8, 128), F32)],
        [],
        [],
        1.0,
    )


def adamw_body(meta, raw, ins, outs, raw_outs, *scratch):
    square, vec, grads, small_w, small_m, small_v, aw, am, av, fw, fm, fv = ins
    norm_out, small_out = outs[0], outs[1:]
    new_a, new_f, sems = scratch
    frame_count = square[0:1, 1:2]
    small = vec[...]
    squares = square[0:1, 0:1] + jnp.sum(row_sum(small * small), 1, keepdims=True)
    norm = jnp.sqrt(squares) / frame_count
    norm_out[...] = norm
    factor = jnp.minimum(1.0, CLIP_NORM / norm) / frame_count
    copies = []
    for i in range(4):
        cols = slice((i % 2) * 384 + (i // 2) * D, (i % 2) * 384 + (i // 2) * D + 384)
        rate = RATE * 0.5 * SEQ**0.5 if i == 3 else RATE
        for k, v in enumerate(adamw(aw[i], am[i], av[i], grads[0, :, cols] * factor, rate, DECAY)):
            new_a[k, i] = v
    for k in range(3):
        copies.append(pltpu.make_async_copy(new_a.at[k], raw_outs[k], sems.at[k]))
        copies[-1].start()
    for i in range(2):
        for k, v in enumerate(adamw(fw[i], fm[i], fv[i], grads[1 + i] * factor, RATE, DECAY)):
            new_f[k, i] = v
    for k in range(3):
        copies.append(pltpu.make_async_copy(new_f.at[k], raw_outs[3 + k], sems.at[3 + k]))
        copies[-1].start()
    new_small = adamw(small_w[...], small_m[...], small_v[...], small * factor, SMALL_RATE, 0.0)
    for out, v in zip(small_out, new_small):
        out[...] = v
    for c in copies:
        c.wait()


def adamw_call(meta, square, vec, grads, small, state):
    shapes = [v.shape for v in state]
    return kernel_call(
        adamw_body,
        "adamw",
        meta,
        [],
        [square, vec, grads, *small, *state],
        [((1, 1), F32)] + [((LINES, 128), F32)] * 3,
        [(s, F32) for s in shapes],
        [
            pltpu.VMEM((3, *shapes[0]), F32),
            pltpu.VMEM((3, *shapes[3]), F32),
            pltpu.SemaphoreType.DMA((6,)),
        ],
        3.0,
    )


def put_out(meta, acc, outs, half):
    d = meta[0]
    for sel in range(2):
        for j in range(8):
            row = pl.multiple_of((d ^ MASKS[half][sel][j]) * ROWS, 16)
            outs[half * 2 + sel][j] = acc[half, pl.ds(row, ROWS), :]


GRAD_OUTS = [((8, ROWS, D), BF)] * 4
GRAD_SCRATCH = [pltpu.VMEM((2, D, D), BF)]


def ffn_grad(meta, left_o, left_r, right_o, right_r, outs, acc):
    for half in range(2):

        def step(i, carry, half=half):
            total = dot(left_o[i], right_o[half]) + dot(left_r[i], right_r[half])
            acc[half, pl.ds(pl.multiple_of(i * 384, 16), 384), :] = total.astype(BF)
            return carry

        lax.fori_loop(0, 2, step, 0)
        put_out(meta, acc, outs, half)


def down_grad_body(meta, _, ins, outs, __, acc):
    dz_o, dz_r, f_o, f_r = ins
    ffn_grad(meta, dz_o, dz_r, f_o, f_r, outs, acc)


def down_grad_call(meta, *ins):
    return kernel_call(
        down_grad_body, "down_grad", meta, [], ins, GRAD_OUTS, [], GRAD_SCRATCH, 4.0
    )


def middle_body(meta, raw, ins, outs, raw_outs, acc, grads, dy1, da, out_sems, *scratch):
    attn = AttnBack(1, raw, scratch)
    attn.start()
    shared, shared_r, du0, du_r, *rest = ins
    sums_one, sent, qv = outs
    copies = [
        pltpu.make_async_copy(a, b, out_sems.at[i])
        for i, (a, b) in enumerate(zip([*[grads.at[i] for i in range(4)], dy1, da], raw_outs))
    ]
    ffn_grad(
        meta,
        shared.at[pl.ds(1, 2)],
        shared_r.at[pl.ds(1, 2)],
        du0,
        du_r,
        [grads.at[i] for i in range(4)],
        acc,
    )
    for c in copies[:4]:
        c.start()
    hidden_back([du0, *rest], (dy1, da, sums_one))
    for c in copies[4:]:
        c.start()
    for i in range(2):
        sent[3 + i] = da[:, i * 384 : (i + 1) * 384].T
    attn.run(da, sent.at[0], sent.at[1], sent.at[2], qv)
    for c in copies:
        c.wait()


def middle(meta, heads, w_attn, prob, shared, shared_r, du0, du_r, du1, dy2, yh, inv, s12, w):
    return kernel_call(
        middle_body,
        "up_grad_hidden_back_attn_back",
        meta,
        [*heads, w_attn, prob],
        [shared, shared_r, du0, du_r, du1, dy2, yh, inv, s12, w],
        [((8, D), F32), ((5, 384, SEQ), BF), ((16, 384), F32)],
        GRAD_OUTS + [((SEQ, D), F32), ((SEQ, D), BF)],
        GRAD_SCRATCH
        + [
            pltpu.VMEM((4, 8, ROWS, D), BF),
            pltpu.VMEM((SEQ, D), F32),
            pltpu.VMEM((SEQ, D), BF),
            pltpu.SemaphoreType.DMA((6,)),
        ]
        + AttnBack.SCRATCH,
        14.0,
    )


def attn_back_body(meta, raw, ins, outs, _, da, da_sem, *scratch):
    da_copy = pltpu.make_async_copy(raw[0], da, da_sem.at[0])
    da_copy.start()
    attn = AttnBack(0, raw[1:], scratch)
    attn.start()
    turned, qv = outs
    da_copy.wait()
    attn.run(da, turned.at[0], turned.at[1], turned.at[2], qv)


def attn_back(meta, heads, w_attn, prob, da):
    return kernel_call(
        attn_back_body,
        "attn_back",
        meta,
        [da, *heads, w_attn, prob],
        [],
        [((3, 384, SEQ), BF), ((16, 384), F32)],
        [],
        [pltpu.VMEM((SEQ, D), BF), pltpu.SemaphoreType.DMA((1,))] + AttnBack.SCRATCH,
        7.0,
    )


def attn_grad_body(meta, _, ins, outs, __, acc, x_t):
    xo, xr, zo, zr, turned, sent, sent_r, o_own, shared_r = ins[:9]
    qv0, qv1, sums_one, sums_two, db1 = ins[9:]
    vec = outs[4]
    for rel, qv in ((0, qv0), (1, qv1)):
        h = meta[1] ^ rel
        put_lines(vec, 3 * h, qv[0:1, :])
        put_lines(vec, 6 + 3 * h, qv[8:9, :])
    for line, sums, row in (
        (2, sums_one, 0),
        (3, sums_two, 0),
        (4, sums_one, 1),
        (5, sums_one, 2),
        (6, sums_two, 1),
        (7, sums_two, 2),
    ):
        put_lines(vec, 6 * line, sums[row : row + 1, :])
    for i in range(4):
        put_lines(vec, 48 + 6 * i, db1[i : i + 1, :])
    for i, v in enumerate((xo, xr, zo, zr)):
        x_t[:, i * HALF : (i + 1) * HALF] = v[...].T
    for half, side, k in ((1, 0, 2), (0, 0, 0), (0, 1, 1)):
        for m in range(3):
            rows = pl.ds(m * 256, 256)
            total = dot_t(x_t[rows, :SEQ], turned[k]) + dot_t(x_t[rows, SEQ:], sent_r[k])
            acc[half, rows, side * 384 : (side + 1) * 384] = total.astype(BF)
    for i in range(2):
        total = dot_t(sent[3 + i], o_own[...]) + dot_t(sent_r[3 + i], shared_r[0])
        acc[1, i * 384 : (i + 1) * 384, 384:] = total.astype(BF)
    for half in range(2):
        put_out(meta, acc, outs, half)


def attn_grad(meta, xs, turned, sent, sent_r, o_own, shared_r, small):
    return kernel_call(
        attn_grad_body,
        "attn_grad",
        meta,
        [],
        [*xs, turned, sent, sent_r, o_own, shared_r, *small],
        GRAD_OUTS + [((LINES, 128), F32)],
        [],
        GRAD_SCRATCH + [pltpu.VMEM((D, 2 * SEQ), BF)],
        5.0,
    )


def adamw(weight, moment_one, moment_two, grad, rate, decay):
    new_one = BETA_ONE * moment_one + (1.0 - BETA_ONE) * grad
    new_two = BETA_TWO * moment_two + (1.0 - BETA_TWO) * grad * grad
    fixed_one = new_one / (1.0 - BETA_ONE**STEP)
    fixed_two = new_two / (1.0 - BETA_TWO**STEP)
    update = fixed_one / (jnp.sqrt(fixed_two) + ADAM_EPS) + decay * weight
    return (weight - rate * update, new_one, new_two)


def after(v, *deps):
    return lax.optimization_barrier((v, *deps))[0]


def other_core(v):
    return lax.ppermute(v, "tensor", [(0, 1), (1, 0)])


def shift(v, mask, n):
    return lax.ppermute(v, "dp", [(i, i ^ mask) for i in range(n)])


class Gather:
    def __init__(self, shard, n):
        self.n, self.shard, self.mark = n, shard, shard

    def z_all(self, *deps):
        if self.n == BLOCKS:
            shard = after(self.shard, *deps)
            self.z = [shard] + [shift(shard, z, self.n) for z in Z_MASKS[1:]]
            self.mark = shard

    def z_wait(self, *deps):
        if self.n == BLOCKS:
            self.z = after(tuple(self.z), *deps)
            self.mark = self.z[1:]

    def far_wait(self, *deps):
        if self.n == BLOCKS:
            self.far_side = after(tuple(self.far_side), *deps)
            self.mark = tuple(self.far_side)

    def near_wait(self, *deps):
        if self.n == BLOCKS:
            self.came = after(tuple(self.came), *deps)
            self.mark = tuple(self.came)

    def near(self, *deps):
        if self.n != BLOCKS:
            return
        parts = after(tuple(self.z), *deps)
        self.own = [
            jnp.stack([v[:, half * D : (half + 1) * D] for v in parts]) for half in range(2)
        ]
        self.mark = tuple(self.own)
        self.came = [shift(s, step[0], self.n) for s, step in zip(self.own, (STEP_A, STEP_B))]

    def far(self, *deps):
        if self.n != BLOCKS:
            return
        came = after(tuple(self.came), *deps)
        self.own = [jnp.concatenate([s, c]) for s, c in zip(self.own, came)]
        self.mark = tuple(self.own)
        self.far_side = [shift(o, step[1], self.n) for o, step in zip(self.own, (STEP_A, STEP_B))]

    def core(self, *deps):
        if self.n == BLOCKS:
            self.own_other = [other_core(o) for o in after(tuple(self.own), *deps)]
            self.mark = tuple(self.own_other)

    def pieces(self, *deps):
        if self.n == BLOCKS:
            far = after(tuple(self.far_side), *deps)
            result = []
            for half in range(2):
                far_other = other_core(far[half])
                result += [self.own[half], far[half], self.own_other[half], far_other]
            self.mark = far[1]
            return result
        full = lax.all_gather(self.shard, "dp", axis=0, tiled=True)
        blocks = full.reshape(BLOCKS, ROWS, 2 * D)
        result = []
        for half in range(2):
            cols = slice(half * D, (half + 1) * D)
            own = [blocks[jnp.array(m), :, cols] for m in MASKS[half]]
            result += own + [other_core(v) for v in own]
        return result


def added(*parts):
    total = parts[0].astype(F32)
    for p in parts[1:]:
        total = total + p.astype(F32)
    return total


class Scatter:
    def __init__(self, meta, pieces, n):
        self.meta = meta
        self.n, self.pieces, self.mark = n, pieces, pieces[0]
        if n == BLOCKS:
            self.keep = [pieces[0], pieces[2]]
            self.came = [
                shift(v, step[1], n) for v, step in zip((pieces[1], pieces[3]), (STEP_A, STEP_B))
            ]

    def near(self, *deps):
        if self.n != BLOCKS:
            return
        came = after(tuple(self.came), *deps)
        self.keep, send = near_sums(self.meta, self.keep, came)
        self.came = [shift(s, step[0], self.n) for s, step in zip(send, (STEP_A, STEP_B))]
        self.mark = tuple(send)

    def wait(self, *deps):
        if self.n == BLOCKS:
            self.came = after(tuple(self.came), *deps)
            self.mark = tuple(self.came)

    def z_all(self, *deps):
        if self.n != BLOCKS:
            return
        came = after(tuple(self.came), *deps)
        self.row, *sends = z_sums(self.meta, self.keep, came)
        self.mark = tuple(sends)
        self.came = [shift(s, z, self.n) for s, z in zip(sends, Z_MASKS[1:])]

    def parts(self, *deps):
        if self.n == BLOCKS:
            return [self.row, *after(tuple(self.came), *deps)]
        whole = self.whole()
        zero = jnp.zeros(whole.shape, BF)
        return [whole, zero, zero, zero]

    def whole(self):
        result = []
        for half in range(2):
            order = MASKS[half][0] + MASKS[half][1]
            back = [order.index(i) for i in range(BLOCKS)]
            full = jnp.concatenate(self.pieces[2 * half : 2 * half + 2])[jnp.array(back)]
            full = full.reshape(D, D).astype(F32)
            result.append(lax.psum_scatter(full, "dp", scatter_dimension=0, tiled=True))
        return jnp.concatenate(result, 1)


class Everywhere:
    def __init__(self, v, n):
        self.n, self.v = n, v

    def core(self, *deps):
        if self.n == BLOCKS:
            v = after(self.v, *deps)
            self.v = v + other_core(v)

    def step(self, masks, *deps):
        if self.n == BLOCKS:
            v = after(self.v, *deps)
            came = [shift(v, m, self.n) for m in masks]
            self.v = v + came[0] if len(came) == 1 else (v + came[0]) + (came[1] + came[2])

    def total(self):
        return self.v if self.n == BLOCKS else lax.psum(self.v, ("dp", "tensor"))


XY_MASKS = (1, 2, 3)


def last_steps(small, every):
    if every.n != BLOCKS:
        return small.total(), every.total()
    lines = every.v.shape[0]
    every.v = jnp.concatenate([every.v, small.v])
    every.step(XY_MASKS)
    v = every.v[:lines]
    near, both, far = [
        shift(s, m, every.n) for s, m in zip((v, every.v, v), Z_MASKS[1:])
    ]
    return every.v[lines:] + both[lines:], (v + near) + (both[:lines] + far)


def per_device(
    frames,
    cotangent,
    lengths,
    attn_w,
    attn_m,
    attn_v,
    ffn_w,
    ffn_m,
    ffn_v,
    small_w,
    small_m,
    small_v,
):
    n = lax.axis_size("dp")
    t = lax.axis_index("tensor")
    d = lax.axis_index("dp") if n == BLOCKS else 0
    length = lax.dynamic_index_in_dim(lengths[:, 0], t, 0, keepdims=False)
    meta = jnp.stack([jnp.asarray(d, jnp.int32), jnp.asarray(t, jnp.int32), length])
    s12 = small_w.reshape(12, D)
    half = SEQ // lax.axis_size("tensor")
    count = jnp.sum(jnp.clip(lengths - t * half, 0, half)).astype(F32).reshape(1, 1)

    def pick(v, i):
        return lax.dynamic_index_in_dim(v[:, 0], i, 0, keepdims=False)

    def joined(own, other):
        return jnp.where(t == 0, jnp.stack([own, other]), jnp.stack([other, own]))[:, None]

    attn = Gather(jnp.concatenate([attn_w[i] for i in range(4)], 1).astype(BF), n)
    up = Gather(ffn_w[0].astype(BF), n)
    down = Gather(ffn_w[1].astype(BF), n)
    attn.z_all()
    frames_r = other_core(frames)
    xo, zr = pick(frames, t), pick(frames, 1 - t)
    xr, zo = pick(frames_r, t), pick(frames_r, 1 - t)
    cotangent_r = other_core(cotangent)
    co, cr = pick(cotangent, t), pick(cotangent_r, t)
    attn.near(xr, cr)
    up.z_all(attn.mark)
    attn.far()
    up.near(attn.mark)
    attn.core()
    attn_pieces = attn.pieces(up.mark)
    down.z_all(attn.mark)
    up.far(attn.mark)
    first = attn_first(after(meta, up.mark, down.mark, count), xo, xr, attn_pieces, s12)
    later, o_first, out_w, *heads_first = first
    *heads_first, w_attn, prob_first = heads_first
    down.near(o_first)
    second = attn_second(after(meta, down.mark), xo, xr, s12, later, o_first, out_w)
    yh, inv, hb, shared, *heads_second = second
    *heads_second, prob_second = heads_second
    heads, prob = (heads_first, heads_second), (prob_first, prob_second)
    down.near_wait(inv)
    up.far_wait(inv)
    up.core(down.mark)
    up_pieces = up.pieces()
    down.far()
    down_far = down.mark
    down.core(up_pieces[1], up_pieces[3])
    f0, f1, gp, w_up = ffn_up(after(meta, down_far), hb, up_pieces, s12)
    down.far_wait(gp)
    down_pieces = down.pieces()
    f_r = other_core(after(f1, *down_pieces))
    shared_r = other_core(after(shared, *down_pieces))
    out_o, out_r, dz, dz_t, dy2, sums_two, w_down = ffn_down(
        meta, f0, f1, down_pieces, yh, co, cr, s12
    )
    dz_r = other_core(after(dz_t, f_r, shared_r))
    du0, du1, db1 = ffn_back(after(meta, f_r, shared_r), dz, w_down, gp)
    du_r = other_core(after(du1, dz_r))
    down_sum = Scatter(
        meta,
        down_grad_call(after(meta, db1), dz_t, dz_r, f0, f_r), n
    )
    *up_grad, dy1, da = middle(
        after(meta, down_sum.mark),
        heads[1],
        w_attn,
        prob[1],
        shared,
        shared_r,
        du0,
        du_r,
        du1,
        dy2,
        yh,
        inv,
        s12,
        w_up,
    )
    sums_one, sent, qv1, *up_grad = up_grad
    down_sum.wait(qv1)
    up_sum = Scatter(meta, after(tuple(up_grad), down_sum.mark), n)
    down_sum.near()
    sent_r = other_core(after(sent, down_sum.mark))
    turned0, qv0 = attn_back(after(meta, down_sum.mark), heads[0], w_attn, prob[0], da)
    down_sum.z_all(qv0, sent_r)
    *attn_grads, vec = attn_grad(
        after(meta, down_sum.mark),
        (xo, xr, zo, zr),
        turned0,
        sent,
        sent_r,
        heads[0][3],
        shared_r,
        (qv0, qv1, sums_one, sums_two, db1),
    )
    up_sum.wait(attn_grads[0])
    up_sum.near()
    down_sum.wait(up_sum.mark)
    small = Everywhere(vec, n)
    attn_sum = Scatter(meta, after(tuple(attn_grads), down_sum.mark), n)
    small.core(down_sum.mark)
    small.step((4,))
    up_sum.wait()
    up_sum.z_all(small.v)
    small_state = [v.reshape(LINES, 128) for v in (small_w, small_m, small_v)]
    attn_sum.near(up_sum.mark)
    dx_o, dx_r = frames_back(after(meta, attn_sum.mark), dy1, (turned0, sent), w_attn)
    attn_sum.wait(dx_o)
    up_sum.wait(dx_o)
    attn_sum.z_all(up_sum.mark)
    dx_other = other_core(after(dx_r, attn_sum.mark))
    out_other = other_core(after(out_r, attn_sum.mark))
    frames_grad = joined(dx_o, dx_other)
    output = joined(out_o, out_other)
    grads, square = totals(
        meta, count, attn_sum.parts(frames_grad, output) + up_sum.parts() + down_sum.parts()
    )
    every = Everywhere(square, n)
    every.core()
    small_all, square_all = last_steps(small, every)
    state = (attn_w, attn_m, attn_v, ffn_w, ffn_m, ffn_v)
    norm, small_new, small_m_new, small_v_new, *new_state = adamw_call(
        meta, square_all, small_all, grads, small_state, state
    )
    attn_new, attn_m_new, attn_v_new, ffn_new, ffn_m_new, ffn_v_new = new_state
    grad_norm = norm[0, 0]
    small_new, small_m_new, small_v_new = [
        v.reshape(SMALL) for v in (small_new, small_m_new, small_v_new)
    ]
    return (
        output,
        frames_grad,
        grad_norm,
        attn_new,
        attn_m_new,
        attn_v_new,
        ffn_new,
        ffn_m_new,
        ffn_v_new,
        small_new,
        small_m_new,
        small_v_new,
    )


def solution(mesh):
    rows = P(None, "dp", "tensor", None)
    weights = P(None, "dp", "tensor")
    in_specs = (rows, rows, P(None, "dp")) + (weights,) * 6 + (P(),) * 3
    out_specs = (rows, rows, P()) + (weights,) * 6 + (P(),) * 3
    return jax.shard_map(
        per_device, mesh=mesh, in_specs=in_specs, out_specs=out_specs, check_vma=False
    )
```
